32 devices in a mesh: grp: 2 (over y), scan: 4 (over z), chan: 4 (over x, core).
Axes of the slice: x: 2, y: 2, z: 4, core: 2. Of those that a mesh axis runs over, the one named last changes fastest.
Arguments:
- frames: bfloat16 [3072, 24576], P(('grp', 'scan'), 'chan'), parts along dimension 0, may hold values from -6 to 6
- counts: int32 [2048], P(('grp', 'scan')), parts along dimension 0, may hold values from 1 to 2, as said below
- point_ray: int32 [2048], P(('grp', 'scan')), parts along dimension 0, may hold values from 0 to 1023, as said below
- channel_pair_weights: bfloat16 [192, 128, 256], P('chan'), may hold values from 0 to 0.049804688
- tile_bin: int32 [192], P('chan'), may hold values from 0 to 14, as said below
- image: float32 [32768, 2048], P(('grp', 'scan'), 'chan'), parts along dimension 0, may hold values from -3 to 8
Outputs:
- corrected: float32 [32768, 2048], P(('grp', 'scan'), 'chan'), parts along dimension 0
The draws below stay inside these ranges and needn't reach their ends.
There are 2 independent parts, one for each index of `grp`. The reference program is written for one: setup_inputs(seed, part) draws one part's arguments, and reference() takes and returns one part's arrays. A program takes and returns all parts, laid end to end along the dimension named above; an argument that names none is the same for every part. Nothing has to cross between parts.
Inputs may be any that keep to these rules, and one draw needn't show every extreme that they name: `counts`: each scan point has one or two frames; the frames of the 256 points of one scan index fill at most 384 slots, and one scan index fills all 384. `point_ray`: A permutation of the rays. Of the points of one scan index, at most 2 * 256 / 4 measure rays of one aligned block of 256 rays, and every block receives that many from some scan index. `tile_bin`: nondecreasing along the pixel blocks, from 0 at the first to 2048/128 - 2 at the last.
All inputs are finite; a program needn't handle non-finite values.
Results may differ from the reference program's by a relative error of at most 0.0045.
Values may be sent and summed in bfloat16 or wider, within the bound.
No kernel may reach another device: no remote copies, remote signals or barrier semaphores. Data moves between devices by JAX's collectives and lax.ppermute only.
A program may use at most 128 MiB of HBM per device.

```python
import math
import jax
import jax.numpy as jnp
from jax import lax

NBIN = 2048
TB = 128
TP = 128
PT_DEV = 256
NIMG = 128
PIX = 24576
FR_DEV = 384
FRAMES = 1536
POINTS = 1024
RAYS = 1024
NANG = 8
CELLS = 16384
PBLK = 192
N_SCAN = 4


def draw_counts(key, part):
    key = jax.random.fold_in(key, 11)
    first, second, third = jax.random.split(key, 3)
    half = PT_DEV // 2
    extra = jax.random.randint(first, (N_SCAN,), 0, half + 1)
    full_dev = jax.random.randint(second, (), 0, N_SCAN)
    extra = jnp.where(jnp.arange(N_SCAN) == full_dev, half, extra)
    ranks = jax.vmap(lambda k: jax.random.permutation(k, PT_DEV))(jax.random.split(third, N_SCAN))
    result = 1 + (ranks < extra[:, None]).astype(jnp.int32)
    return result.reshape(-1).astype(jnp.int32)


def draw_point_ray(key, part):
    key = jax.random.fold_in(key, 23)
    keys = jax.random.split(key, 4)
    base = PT_DEV // N_SCAN
    shifts = jax.random.randint(keys[0], (N_SCAN // 2,), 0, base + 1).at[0].set(base)
    profile = jnp.concatenate([base + shifts, base - shifts])
    profile = profile[jax.random.permutation(keys[1], N_SCAN)]
    source = jnp.arange(N_SCAN)
    load = profile[(source[:, None] - source[None, :]) % N_SCAN]
    ends = jnp.cumsum(load, axis=1)
    before_src = ends - load
    before_dst = jnp.cumsum(load, axis=0) - load
    slots = jnp.arange(PT_DEV)
    dest = jnp.sum((ends[:, None, :] <= slots[None, :, None]).astype(jnp.int32), axis=2)
    within = slots[None, :] - jnp.take_along_axis(before_src, dest, 1)
    place = jnp.take_along_axis(before_dst, dest, 1) + within
    ray_perm = jax.vmap(lambda k: jax.random.permutation(k, PT_DEV))(jax.random.split(keys[2], N_SCAN))
    rays = dest * PT_DEV + ray_perm[dest, place]
    point_perm = jax.vmap(lambda k: jax.random.permutation(k, PT_DEV))(jax.random.split(keys[3], N_SCAN))
    result = jnp.take_along_axis(rays, point_perm, 1)
    return result.reshape(-1).astype(jnp.int32)


def draw_tile_bin(key, part):
    key = jax.random.fold_in(key, 37)
    top = NBIN // TB - 2
    raw = jnp.sort(jax.random.randint(key, (PIX // TP,), 0, top + 1))
    raw = raw.at[0].set(0).at[-1].set(top)
    return raw.astype(jnp.int32)


def smooth_field(key, strength_lo, strength_hi):
    split_random_keys = jax.random.split(key, 3)
    strength = jnp.exp(jax.random.uniform(split_random_keys[0], (NBIN,), jnp.float32, math.log(strength_lo), math.log(strength_hi)))
    wavenum = jax.random.randint(split_random_keys[1], (2,), 1, 4).astype(jnp.float32)
    phases = jax.random.uniform(split_random_keys[2], (2, NBIN), jnp.float32, -math.pi, math.pi)
    cell_ids = jnp.arange(CELLS, dtype=jnp.int32)
    half = (NIMG - 1) / 2.0
    row_pos = ((cell_ids // NIMG).astype(jnp.float32) - half) / NIMG
    col_pos = ((cell_ids % NIMG).astype(jnp.float32) - half) / NIMG
    waves = 1.0 + 0.25 * jnp.cos(math.pi * wavenum[0] * row_pos[:, None] + phases[0][None, :])
    waves = waves + 0.25 * jnp.cos(math.pi * wavenum[1] * col_pos[:, None] + phases[1][None, :])
    return strength[None, :] * waves


def draw_image(key, part):
    key = jax.random.fold_in(key, 53)
    smooth_key, rough_key = jax.random.split(key, 2)
    smooth_component = smooth_field(smooth_key, 1.0, 3.0)
    rough_part = jnp.clip(jax.random.normal(rough_key, (CELLS, NBIN), jnp.float32), -3.0, 3.0)
    return (smooth_component + rough_part).astype(jnp.float32)


def block_scale(rng, shape, pieces, least, largest):
    loudness = 1.0
    for position, parts in pieces:
        draws = jax.random.uniform(jax.random.fold_in(jax.random.fold_in(rng, 6), position), (parts,), jnp.float32, least / len(pieces), largest / len(pieces))
        loudness = loudness * jnp.repeat(jnp.exp(draws), shape[position] // parts).reshape((-1,) + (1,) * (len(shape) - 1 - position))
    return loudness


def scatter_about(stream_key, dims, width, most, cuts=(), kind=jnp.bfloat16):
    entries = jax.random.normal(stream_key, dims, jnp.float32) * width
    if len(cuts) > 0:
        entries = block_scale(stream_key, dims, cuts, -0.22, 0.18) * entries
    return jnp.clip(entries, min=-most, max=most).astype(kind)


def setup_inputs(seed: int = 0, part: int = 0) -> dict:
    key_of = jax.random.split(jax.random.key(seed), 7)
    own_keys = jax.random.split(jax.random.fold_in(key_of[6], part), 7)
    frames = scatter_about(own_keys[0], (FRAMES, PIX), 1.0, 6.0, ((0, 4), (1, 4)))
    counts = draw_counts(jax.random.fold_in(jax.random.fold_in(key_of[6], part), 71), part)
    point_ray = draw_point_ray(jax.random.fold_in(jax.random.fold_in(key_of[6], part), 71), part)
    channel_pair_weights = jnp.clip(0.049804688 * jax.random.uniform(key_of[3], (PBLK, TP, 2 * TB), jnp.float32) ** block_scale(key_of[3], (PBLK, TP, 2 * TB), ((0, 4),), -0.2, 0.2), 0.0, 0.049804688).astype(jnp.bfloat16)
    tile_bin = draw_tile_bin(jax.random.fold_in(key_of[6], 71), part)
    image = draw_image(jax.random.fold_in(jax.random.fold_in(key_of[6], part), 71), part)
    return dict(frames=frames, counts=counts, point_ray=point_ray, channel_pair_weights=channel_pair_weights, tile_bin=tile_bin, image=image)


def hat_weights(ray_numbers, cell_ids, img_side, angles):
    half = (img_side - 1) / 2.0
    theta = (ray_numbers // img_side).astype(jnp.float32) * (math.pi / angles)
    offset = (ray_numbers % img_side).astype(jnp.float32) - half
    upos = (cell_ids // img_side).astype(jnp.float32) - half
    vpos = (cell_ids % img_side).astype(jnp.float32) - half
    along = jnp.cos(theta)[:, None] * upos[None, :] + jnp.sin(theta)[:, None] * vpos[None, :]
    return (jnp.maximum(0.0, 1.0 - jnp.abs(along - offset[:, None])) / img_side).astype(jnp.bfloat16)


def reference(frames, counts, point_ray, channel_pair_weights, tile_bin, image):
    nbb = NBIN // TB
    blocks_ids = jnp.arange(nbb, dtype=jnp.int32)
    lower_hot = (tile_bin[:, None] == blocks_ids[None, :]).astype(jnp.float32)
    upper_hot = ((tile_bin[:, None] + 1) == blocks_ids[None, :]).astype(jnp.float32)
    tiles_across_channels = channel_pair_weights.astype(jnp.float32)

    def integrate(args):
        rows, cnt = args
        ends = jnp.cumsum(cnt)
        slots = jnp.arange(FR_DEV, dtype=jnp.int32)
        owner = jnp.sum((ends[None, :] <= slots[:, None]).astype(jnp.int32), axis=1)
        member = (owner[None, :] == jnp.arange(PT_DEV, dtype=jnp.int32)[:, None]).astype(jnp.bfloat16)
        sums = jnp.dot(member, rows, preferred_element_type=jnp.float32)
        means = (sums / cnt[:, None].astype(jnp.float32)).astype(jnp.bfloat16)
        pixel_grouped_weights = means.astype(jnp.float32).reshape(PT_DEV, PBLK, TP)
        partial_channel_value = jnp.einsum('orj,rjm->rom', pixel_grouped_weights, tiles_across_channels, precision=lax.Precision.HIGHEST)
        placed = jnp.einsum('pk,pfb->kbf', lower_hot, partial_channel_value[:, :, :TB], precision=lax.Precision.HIGHEST)
        placed = placed + jnp.einsum('pk,pfb->kbf', upper_hot, partial_channel_value[:, :, TB:], precision=lax.Precision.HIGHEST)
        return placed.reshape(NBIN, PT_DEV).astype(jnp.bfloat16)

    patterns = lax.map(integrate, (frames.reshape(N_SCAN, FR_DEV, PIX), counts.reshape(N_SCAN, PT_DEV)))
    pattern_rows = jnp.transpose(patterns, (0, 2, 1)).reshape(POINTS, NBIN)
    sinogram = jnp.zeros((RAYS, NBIN), jnp.bfloat16).at[point_ray].set(pattern_rows)
    weights = hat_weights(jnp.arange(RAYS, dtype=jnp.int32), jnp.arange(CELLS, dtype=jnp.int32), NIMG, NANG)
    image_low = image.astype(jnp.bfloat16)
    projected = jnp.dot(weights, image_low, preferred_element_type=jnp.float32)
    row_total = jnp.sum(weights.astype(jnp.float32), axis=1)
    col_total = jnp.sum(weights.astype(jnp.float32), axis=0)
    residual = ((sinogram.astype(jnp.float32) - projected) / row_total[:, None]).astype(jnp.bfloat16)
    back = lax.dot_general(weights, residual, (((0,), (0,)), ((), ())), preferred_element_type=jnp.float32)
    return image + back / col_total[:, None]
```

```python
import functools
import math

import jax
import jax.numpy as jnp
import numpy as np
from jax import lax
from jax.experimental import pallas as pl
from jax.experimental.pallas import tpu as pltpu
from jax.sharding import PartitionSpec as P

NIMG = 128
HALF = (NIMG - 1) / 2.0
LANES = 128
VMEM_BYTES = 50 * 1024 * 1024
F32 = jnp.float32
BF16 = jnp.bfloat16


def angle_tables(angles):
    theta = np.arange(angles, dtype=np.float32) * np.float32(math.pi / angles)
    return [float(c) for c in np.cos(theta)], [float(s) for s in np.sin(theta)]


def ray_geometry(rays, angles):
    cos_tab, sin_tab = angle_tables(angles)
    which = rays // NIMG
    offset = (rays - which * NIMG).astype(F32) - HALF
    cosine = jnp.zeros(rays.shape, F32)
    sine = jnp.zeros(rays.shape, F32)
    for a in range(angles):
        here = which == a
        cosine = jnp.where(here, cos_tab[a], cosine)
        sine = jnp.where(here, sin_tab[a], sine)
    return cosine, sine, offset


def hat(distance):
    return jnp.maximum(1.0 - jnp.abs(distance), 0.0).astype(BF16)


def integrate_kernel(
    nx, per_chunk, tile_bin, place, counts, frames, weights, send, keep_own, keep_rest, member, acc
):
    step = pl.program_id(0)
    points, slots = member.shape
    blocks = weights.shape[0]
    tile_bins = acc.shape[2]

    @pl.when(step == 0)
    def _():
        acc[...] = jnp.zeros_like(acc)
        count_row = counts[...].astype(F32)
        row = lax.broadcasted_iota(jnp.int32, (points, points), 0)
        col = lax.broadcasted_iota(jnp.int32, (points, points), 1)
        ends = jnp.sum(jnp.where(col <= row, count_row, 0.0), axis=1, keepdims=True)
        count = jnp.sum(jnp.where(col == row, count_row, 0.0), axis=1, keepdims=True)
        slot = lax.broadcasted_iota(jnp.int32, (points, slots), 1).astype(F32)
        inside = jnp.logical_and(slot >= ends - count, slot < ends)
        member[...] = jnp.where(inside, 1.0 / count, 0.0).astype(BF16)

    means = jnp.dot(member[...], frames[...], preferred_element_type=F32).astype(BF16)
    for b in range(blocks):
        value = jnp.dot(
            means[:, b * LANES : (b + 1) * LANES], weights[b], preferred_element_type=F32
        )
        k = tile_bin[step * blocks + b]
        acc[k] += value[:, :tile_bins]
        acc[k + 1] += value[:, tile_bins:]

    @pl.when(step == pl.num_programs(0) - 1)
    def _():
        for e in range(nx):
            other, mine = place[2 * e], place[2 * e + 1]
            for j in range(per_chunk):
                lanes = slice(j * tile_bins, (j + 1) * tile_bins)
                send[e, :, lanes] = acc[other * per_chunk + j].astype(BF16)
                if e == 0:
                    keep_own[:, lanes] = acc[mine * per_chunk + j]
                else:
                    keep_rest[e - 1, :, lanes] = acc[mine * per_chunk + j]


def integrate(frames, counts, weights, tile_bin, place, nx, chans):
    slots, pixels = frames.shape
    points = counts.shape[0]
    nblocks, tile_pix, pair = weights.shape
    tile_bins = pair // 2
    blocks = 8 if nblocks % 8 == 0 else 1
    channel_blocks = 2 * nx * chans // tile_bins
    whole = lambda shape: pl.BlockSpec(shape, lambda i, *_: (0,) * len(shape))
    return pl.pallas_call(
        functools.partial(integrate_kernel, nx, chans // tile_bins),
        grid_spec=pltpu.PrefetchScalarGridSpec(
            num_scalar_prefetch=2,
            grid=(nblocks // blocks,),
            in_specs=[
                whole((1, points)),
                pl.BlockSpec((slots, blocks * tile_pix), lambda i, *_: (0, i)),
                pl.BlockSpec((blocks, tile_pix, pair), lambda i, *_: (i, 0, 0)),
            ],
            out_specs=[
                whole((nx, points, chans)),
                whole((points, chans)),
                whole((nx - 1, points, chans)),
            ],
            scratch_shapes=[
                pltpu.VMEM((points, slots), BF16),
                pltpu.VMEM((channel_blocks, points, tile_bins), F32),
            ],
        ),
        out_shape=[
            jax.ShapeDtypeStruct((nx, points, chans), BF16),
            jax.ShapeDtypeStruct((points, chans), F32),
            jax.ShapeDtypeStruct((nx - 1, points, chans), F32),
        ],
        compiler_params=pltpu.CompilerParams(vmem_limit_bytes=VMEM_BYTES),
        cost_estimate=pl.CostEstimate(
            flops=2 * points * pixels * (slots + pair),
            bytes_accessed=2 * (slots * pixels + pixels * pair),
            transcendentals=0,
        ),
        name="integrate",
    )(tile_bin, place, counts.reshape(1, points), frames, weights)


def project_kernel(angles, parts, first_row, rays, image, *refs):
    outs, (cosine, base, tile, total) = refs[:parts], refs[parts:]
    step = pl.program_id(0)
    rows = tile.shape[1] // LANES
    points = total.shape[0] // parts

    @pl.when(step == 0)
    def _():
        total[...] = jnp.zeros_like(total)
        cos_c, sin_c, off_c = ray_geometry(rays[...], angles)
        vpos = lax.broadcasted_iota(jnp.int32, (LANES, LANES), 1).astype(F32) - HALF
        for k in range(rays.shape[0]):
            here = slice(k * LANES, (k + 1) * LANES)
            column = lambda x: jnp.transpose(jnp.broadcast_to(x[k : k + 1, :], (LANES, LANES)))
            cosine[here, :] = column(cos_c)
            base[here, :] = column(sin_c) * vpos - column(off_c)

    for i in range(rows):
        upos = (first_row[0] + step * rows + i).astype(F32) - HALF
        tile[:, i * LANES : (i + 1) * LANES] = hat(base[...] + cosine[...] * upos)
    total[...] += jnp.dot(tile[...], image[...].astype(BF16), preferred_element_type=F32)

    @pl.when(step == pl.num_programs(0) - 1)
    def _():
        for d in range(parts):
            outs[d][...] = total[d * points : (d + 1) * points, :].astype(outs[d].dtype)


def project(rays, image, first_row, angles, parts):
    cells, chans = image.shape
    all_points = rays.shape[0] * LANES
    points = all_points // parts
    rows = min(8, cells // LANES)
    out = pl.BlockSpec((points, chans), lambda i, *_: (0, 0))
    return pl.pallas_call(
        functools.partial(project_kernel, angles, parts),
        grid_spec=pltpu.PrefetchScalarGridSpec(
            num_scalar_prefetch=1,
            grid=(cells // (rows * LANES),),
            in_specs=[
                pl.BlockSpec(rays.shape, lambda i, *_: (0, 0)),
                pl.BlockSpec((rows * LANES, chans), lambda i, *_: (i, 0)),
            ],
            out_specs=[out] * parts,
            scratch_shapes=[
                pltpu.VMEM((all_points, LANES), F32),
                pltpu.VMEM((all_points, LANES), F32),
                pltpu.VMEM((all_points, rows * LANES), BF16),
                pltpu.VMEM((all_points, chans), F32),
            ],
        ),
        out_shape=[
            jax.ShapeDtypeStruct((points, chans), F32 if d == 0 else BF16) for d in range(parts)
        ],
        compiler_params=pltpu.CompilerParams(vmem_limit_bytes=VMEM_BYTES),
        cost_estimate=pl.CostEstimate(
            flops=2 * all_points * cells * chans, bytes_accessed=4 * cells * chans, transcendentals=0
        ),
        name="project",
    )(first_row, rays, image)


def totals_kernel(angles, first_row, rays, row_total, col_recip):
    cos_tab, sin_tab = angle_tables(angles)
    cos_r, sin_r, off_r = ray_geometry(rays[...], angles)
    lane = lax.broadcasted_iota(jnp.int32, (LANES, LANES), 1).astype(F32) - HALF
    vpos = lax.broadcasted_iota(jnp.int32, (LANES, LANES), 0).astype(F32) - HALF
    for k in range(rays.shape[0]):
        base = sin_r[k : k + 1, :] * vpos - off_r[k : k + 1, :]
        slope = cos_r[k : k + 1, :]

        def add_row(i, sums):
            upos = i.astype(F32) - HALF
            return sums + hat(base + slope * upos).astype(F32)

        sums = lax.fori_loop(0, NIMG, add_row, jnp.zeros((LANES, LANES), F32), unroll=4)
        total = jnp.sum(sums, axis=0, keepdims=True)
        row_total[k * LANES : (k + 1) * LANES, :] = jnp.transpose(
            jnp.broadcast_to(total, (LANES, LANES))
        )

    def column_row(i, carry):
        upos = (first_row[0] + i).astype(F32) - HALF
        sums = jnp.zeros((LANES, LANES), F32)
        for a in range(angles):
            sums += hat((sin_tab[a] * vpos - lane) + cos_tab[a] * upos).astype(F32)
        total = jnp.sum(sums, axis=1, keepdims=True)
        start = pl.multiple_of(i * LANES, LANES)
        col_recip[pl.ds(start, LANES), :] = jnp.broadcast_to(1.0 / total, (LANES, LANES))
        return carry

    lax.fori_loop(0, col_recip.shape[0] // LANES, column_row, 0)


def totals(rays, first_row, cells, angles):
    points = rays.shape[0] * LANES
    vmem = pl.BlockSpec(memory_space=pltpu.VMEM)
    return pl.pallas_call(
        functools.partial(totals_kernel, angles),
        in_specs=[pl.BlockSpec(memory_space=pltpu.SMEM), vmem],
        out_specs=[vmem, vmem],
        out_shape=[
            jax.ShapeDtypeStruct((points, LANES), F32),
            jax.ShapeDtypeStruct((cells, LANES), F32),
        ],
        compiler_params=pltpu.CompilerParams(vmem_limit_bytes=VMEM_BYTES),
        cost_estimate=pl.CostEstimate(
            flops=8 * points * NIMG * NIMG * 8, bytes_accessed=4 * cells * LANES, transcendentals=0
        ),
        name="totals",
    )(first_row, rays)


def back_kernel(angles, parts, first_row, rays, *refs):
    residuals, (image, recip, out, base, cosine, joined, tile) = refs[:parts], refs[parts:]
    step = pl.program_id(0)
    points, chans = residuals[0].shape
    rows = tile.shape[0] // LANES

    @pl.when(step == 0)
    def _():
        cos_c, sin_c, off_c = ray_geometry(rays[...], angles)
        cosine[...] = cos_c
        vpos = lax.broadcasted_iota(jnp.int32, (LANES, LANES), 0).astype(F32) - HALF
        for k in range(rays.shape[0]):
            base[:, k * LANES : (k + 1) * LANES] = sin_c[k : k + 1, :] * vpos - off_c[k : k + 1, :]
        for d in range(parts):
            joined[d * points : (d + 1) * points, :] = residuals[d][...]

    for i in range(rows):
        upos = (first_row[0] + step * rows + i).astype(F32) - HALF
        for k in range(rays.shape[0]):
            lanes = slice(k * LANES, (k + 1) * LANES)
            shift = cosine[k : k + 1, :] * upos
            tile[i * LANES : (i + 1) * LANES, lanes] = hat(base[:, lanes] + shift)
    back = jnp.dot(tile[...], joined[...], preferred_element_type=F32)
    for j in range(chans // LANES):
        lanes = slice(j * LANES, (j + 1) * LANES)
        out[:, lanes] = image[:, lanes] + back[:, lanes] * recip[...]


def back_project(rays, residuals, image, recip, first_row, angles):
    cells, chans = image.shape
    parts = len(residuals)
    points = residuals[0].shape[0]
    all_points = parts * points
    rows = min(4, cells // LANES)
    fixed = lambda shape: pl.BlockSpec(shape, lambda i, *_: (0, 0))
    sliding = lambda width: pl.BlockSpec((rows * LANES, width), lambda i, *_: (i, 0))
    return pl.pallas_call(
        functools.partial(back_kernel, angles, parts),
        grid_spec=pltpu.PrefetchScalarGridSpec(
            num_scalar_prefetch=1,
            grid=(cells // (rows * LANES),),
            in_specs=[fixed(rays.shape)]
            + [fixed((points, chans))] * parts
            + [sliding(chans), sliding(LANES)],
            out_specs=sliding(chans),
            scratch_shapes=[
                pltpu.VMEM((LANES, all_points), F32),
                pltpu.VMEM(rays.shape, F32),
                pltpu.VMEM((all_points, chans), BF16),
                pltpu.VMEM((rows * LANES, all_points), BF16),
            ],
        ),
        out_shape=jax.ShapeDtypeStruct((cells, chans), F32),
        compiler_params=pltpu.CompilerParams(vmem_limit_bytes=VMEM_BYTES),
        cost_estimate=pl.CostEstimate(
            flops=2 * all_points * cells * chans, bytes_accessed=8 * cells * chans, transcendentals=0
        ),
        name="back_project",
    )(first_row, rays, *residuals, image, recip)


def rotate(x, axis, shift, n):
    return lax.ppermute(x, axis, [(i, (i + shift) % n) for i in range(n)])


def body(frames, counts, point_ray, channel_pair_weights, tile_bin, image):
    n_scan = lax.axis_size("scan")
    n_chan = lax.axis_size("chan")
    nx = n_chan // 2
    points = counts.shape[0]
    cells, chans = image.shape
    angles = points * n_scan // NIMG
    chan_me = lax.axis_index("chan")
    x_me, core_me = chan_me // 2, chan_me % 2
    first_row = (lax.axis_index("scan") * (cells // NIMG)).astype(jnp.int32).reshape(1)

    own_rays = point_ray.reshape(points // LANES, LANES)
    rays = [own_rays] + [rotate(own_rays, "scan", -d, n_scan) for d in range(1, n_scan)]
    all_rays = jnp.concatenate(rays, axis=0)

    shares = project(all_rays, image, first_row, angles, n_scan)
    arrived = [rotate(shares[d], "scan", d, n_scan) for d in range(1, n_scan)]

    place = []
    for e in range(nx):
        xi = (x_me + e) % nx
        place += [2 * xi + 1 - core_me, 2 * xi + core_me]
    place = jnp.stack(place).astype(jnp.int32)
    send, keep_own, keep_rest = integrate(
        frames, counts, channel_pair_weights, tile_bin, place, nx, chans
    )
    partner = [(i, i ^ 1) for i in range(n_chan)]
    got = lax.ppermute(send, "chan", partner)
    pattern = keep_own + got[0].astype(F32)
    for e in range(1, nx):
        joined = (keep_rest[e - 1] + got[e].astype(F32)).astype(BF16)
        pattern = pattern + rotate(joined, "chan", 2 * e, n_chan).astype(F32)

    row_total, col_recip = totals(own_rays, first_row, cells, angles)
    projected = shares[0]
    for part in arrived:
        projected = projected + part.astype(F32)
    residual = ((pattern * float(NIMG) - projected) / row_total[:, :1]).astype(BF16)
    residuals = [residual] + [rotate(residual, "scan", -d, n_scan) for d in range(1, n_scan)]
    return back_project(all_rays, residuals, image, col_recip, first_row, angles)


def solution(mesh):
    in_specs = (
        P(("grp", "scan"), "chan"),
        P(("grp", "scan")),
        P(("grp", "scan")),
        P("chan", None, None),
        P("chan"),
        P(("grp", "scan"), "chan"),
    )
    out_specs = P(("grp", "scan"), "chan")
    return jax.shard_map(body, mesh=mesh, in_specs=in_specs, out_specs=out_specs, check_vma=False)
```

```python
import functools
import math

import jax
import jax.numpy as jnp
import numpy as np
from jax import lax
from jax.experimental import pallas as pl
from jax.experimental.pallas import tpu as pltpu
from jax.sharding import PartitionSpec as P

NIMG = 128
HALF = (NIMG - 1) / 2.0
LANES = 128
MIB = 1024 * 1024
F32 = jnp.float32
BF16 = jnp.bfloat16


def angle_tables(angles):
    theta = np.arange(angles, dtype=np.float32) * np.float32(math.pi / angles)
    return [float(c) for c in np.cos(theta)], [float(s) for s in np.sin(theta)]


def ray_geometry(rays, angles):
    cos_tab, sin_tab = angle_tables(angles)
    which = rays // NIMG
    offset = (rays - which * NIMG).astype(F32) - HALF
    cosine = jnp.zeros(rays.shape, F32)
    sine = jnp.zeros(rays.shape, F32)
    for a in range(angles):
        here = which == a
        cosine = jnp.where(here, cos_tab[a], cosine)
        sine = jnp.where(here, sin_tab[a], sine)
    return cosine, sine, offset


def hat(distance):
    return jnp.maximum((1.0 - jnp.abs(distance)).astype(BF16), jnp.zeros((), BF16))


def integrate_kernel(
    nx, per_chunk, tile_bin, place, after, counts, frames, weights, send, keep_own, keep_rest, member, acc
):
    step = pl.program_id(0)
    points, slots = member.shape
    blocks = weights.shape[0]
    tile_bins = acc.shape[2]

    @pl.when(step == 0)
    def _():
        acc[...] = jnp.zeros_like(acc)
        count_row = counts[...].astype(F32)
        row = lax.broadcasted_iota(jnp.int32, (points, points), 0)
        col = lax.broadcasted_iota(jnp.int32, (points, points), 1)
        ends = jnp.sum(jnp.where(col <= row, count_row, 0.0), axis=1, keepdims=True)
        count = jnp.sum(jnp.where(col == row, count_row, 0.0), axis=1, keepdims=True)
        slot = lax.broadcasted_iota(jnp.int32, (points, slots), 1).astype(F32)
        inside = jnp.logical_and(slot >= ends - count, slot < ends)
        member[...] = jnp.where(inside, 1.0 / count, 0.0).astype(BF16)

    means = jnp.dot(member[...], frames[...], preferred_element_type=F32).astype(BF16)
    for b in range(blocks):
        value = jnp.dot(
            means[:, b * LANES : (b + 1) * LANES], weights[b], preferred_element_type=F32
        )
        k = tile_bin[step * blocks + b]
        acc[k] += value[:, :tile_bins]
        acc[k + 1] += value[:, tile_bins:]

    @pl.when(step == pl.num_programs(0) - 1)
    def _():
        for e in range(nx):
            other, mine = place[2 * e], place[2 * e + 1]
            for j in range(per_chunk):
                lanes = slice(j * tile_bins, (j + 1) * tile_bins)
                send[e, :, lanes] = acc[other * per_chunk + j].astype(BF16)
                if e == 0:
                    keep_own[:, lanes] = acc[mine * per_chunk + j]
                else:
                    keep_rest[e - 1, :, lanes] = acc[mine * per_chunk + j]


def integrate(frames, counts, weights, tile_bin, place, after, nx, chans):
    slots, pixels = frames.shape
    points = counts.shape[0]
    nblocks, tile_pix, pair = weights.shape
    tile_bins = pair // 2
    blocks = 16 if nblocks % 16 == 0 else 1
    channel_blocks = 2 * nx * chans // tile_bins
    whole = lambda shape: pl.BlockSpec(shape, lambda i, *_: (0,) * len(shape))
    return pl.pallas_call(
        functools.partial(integrate_kernel, nx, chans // tile_bins),
        grid_spec=pltpu.PrefetchScalarGridSpec(
            num_scalar_prefetch=2,
            grid=(nblocks // blocks,),
            in_specs=[
                pl.BlockSpec(memory_space=pl.ANY),
                whole((1, points)),
                pl.BlockSpec((slots, blocks * tile_pix), lambda i, *_: (0, i)),
                pl.BlockSpec((blocks, tile_pix, pair), lambda i, *_: (i, 0, 0)),
            ],
            out_specs=[
                whole((nx, points, chans)),
                whole((points, chans)),
                whole((nx - 1, points, chans)),
            ],
            scratch_shapes=[
                pltpu.VMEM((points, slots), BF16),
                pltpu.VMEM((channel_blocks, points, tile_bins), F32),
            ],
        ),
        out_shape=[
            jax.ShapeDtypeStruct((nx, points, chans), BF16),
            jax.ShapeDtypeStruct((points, chans), F32),
            jax.ShapeDtypeStruct((nx - 1, points, chans), F32),
        ],
        compiler_params=pltpu.CompilerParams(vmem_limit_bytes=24 * MIB),
        cost_estimate=pl.CostEstimate(
            flops=2 * points * pixels * (slots + pair),
            bytes_accessed=2 * (slots * pixels + pixels * pair),
            transcendentals=0,
        ),
        name="integrate",
    )(tile_bin, place, after, counts.reshape(1, points), frames, weights)


def project_kernel(angles, parts, first_row, rays, image, *refs):
    outs, (cosine, base, tile_a, tile_b, total) = refs[:parts], refs[parts:]
    step = pl.program_id(0)
    rows = tile_a.shape[1] // LANES
    half = rows * LANES
    points = total.shape[0] // parts

    def fill(tile, first):
        for i in range(rows):
            upos = (first + i).astype(F32) - HALF
            tile[:, i * LANES : (i + 1) * LANES] = hat(base[...] + cosine[...] * upos)

    @pl.when(step == 0)
    def _():
        total[...] = jnp.zeros_like(total)
        cos_c, sin_c, off_c = ray_geometry(rays[...], angles)
        vpos = lax.broadcasted_iota(jnp.int32, (LANES, LANES), 1).astype(F32) - HALF
        for k in range(rays.shape[0]):
            here = slice(k * LANES, (k + 1) * LANES)
            column = lambda x: jnp.transpose(jnp.broadcast_to(x[k : k + 1, :], (LANES, LANES)))
            cosine[here, :] = column(cos_c)
            base[here, :] = column(sin_c) * vpos - column(off_c)
        fill(tile_a, first_row[0])

    now = first_row[0] + step * (2 * rows)
    fill(tile_b, now + rows)
    total[...] += jnp.dot(tile_a[...], image[:half, :].astype(BF16), preferred_element_type=F32)
    fill(tile_a, now + 2 * rows)
    total[...] += jnp.dot(tile_b[...], image[half:, :].astype(BF16), preferred_element_type=F32)

    @pl.when(step == pl.num_programs(0) - 1)
    def _():
        for d in range(parts):
            outs[d][...] = total[d * points : (d + 1) * points, :].astype(outs[d].dtype)


def project(rays, image, first_row, angles, parts):
    cells, chans = image.shape
    all_points = rays.shape[0] * LANES
    points = all_points // parts
    rows = min(4, cells // LANES // 2)
    out = pl.BlockSpec((points, chans), lambda i, *_: (0, 0))
    return pl.pallas_call(
        functools.partial(project_kernel, angles, parts),
        grid_spec=pltpu.PrefetchScalarGridSpec(
            num_scalar_prefetch=1,
            grid=(cells // (2 * rows * LANES),),
            in_specs=[
                pl.BlockSpec(rays.shape, lambda i, *_: (0, 0)),
                pl.BlockSpec((2 * rows * LANES, chans), lambda i, *_: (i, 0)),
            ],
            out_specs=[out] * parts,
            scratch_shapes=[
                pltpu.VMEM((all_points, LANES), F32),
                pltpu.VMEM((all_points, LANES), F32),
                pltpu.VMEM((all_points, rows * LANES), BF16),
                pltpu.VMEM((all_points, rows * LANES), BF16),
                pltpu.VMEM((all_points, chans), F32),
            ],
        ),
        out_shape=[
            jax.ShapeDtypeStruct((points, chans), F32 if d == 0 else BF16) for d in range(parts)
        ],
        compiler_params=pltpu.CompilerParams(vmem_limit_bytes=32 * MIB),
        cost_estimate=pl.CostEstimate(
            flops=2 * all_points * cells * chans, bytes_accessed=4 * cells * chans, transcendentals=0
        ),
        name="project",
    )(first_row, rays, image)


def row_total_kernel(angles, after, rays, row_total):
    cos_r, sin_r, off_r = ray_geometry(rays[...], angles)
    vpos = lax.broadcasted_iota(jnp.int32, (LANES, LANES), 0).astype(F32) - HALF
    for k in range(rays.shape[0]):
        base = sin_r[k : k + 1, :] * vpos - off_r[k : k + 1, :]
        slope = cos_r[k : k + 1, :]

        def add_row(i, sums):
            upos = i.astype(F32) - HALF
            return sums + hat(base + slope * upos).astype(F32)

        sums = lax.fori_loop(0, NIMG, add_row, jnp.zeros((LANES, LANES), F32), unroll=4)
        total = jnp.sum(sums, axis=0, keepdims=True)
        row_total[k * LANES : (k + 1) * LANES, :] = jnp.transpose(
            jnp.broadcast_to(total, (LANES, LANES))
        )


def row_totals(rays, angles, after):
    points = rays.shape[0] * LANES
    vmem = pl.BlockSpec(memory_space=pltpu.VMEM)
    return pl.pallas_call(
        functools.partial(row_total_kernel, angles),
        in_specs=[pl.BlockSpec(memory_space=pl.ANY), vmem],
        out_specs=vmem,
        out_shape=jax.ShapeDtypeStruct((points, LANES), F32),
        compiler_params=pltpu.CompilerParams(vmem_limit_bytes=8 * MIB),
        cost_estimate=pl.CostEstimate(
            flops=8 * points * NIMG * NIMG, bytes_accessed=4 * points * LANES, transcendentals=0
        ),
        name="row_totals",
    )(after, rays)


def prepare_kernel(angles, first_row, rays, residual, image, tile, recip, partial, base, cosine):
    step = pl.program_id(0)
    chunks = rays.shape[0]
    points, chans = residual.shape
    rows = tile.shape[0] // LANES

    @pl.when(step == 0)
    def _():
        cos_c, sin_c, off_c = ray_geometry(rays[...], angles)
        cosine[...] = cos_c
        vpos = lax.broadcasted_iota(jnp.int32, (LANES, LANES), 0).astype(F32) - HALF
        for k in range(chunks):
            base[:, k * LANES : (k + 1) * LANES] = sin_c[k : k + 1, :] * vpos - off_c[k : k + 1, :]

    for i in range(rows):
        here = slice(i * LANES, (i + 1) * LANES)
        upos = (first_row[0] + step * rows + i).astype(F32) - HALF
        sums = jnp.zeros((LANES, LANES), F32)
        for k in range(chunks):
            lanes = slice(k * LANES, (k + 1) * LANES)
            value = hat(base[:, lanes] + cosine[k : k + 1, :] * upos)
            tile[here, lanes] = value
            sums += value.astype(F32)
        total = jnp.sum(sums, axis=1, keepdims=True)
        recip[here, :] = jnp.broadcast_to(1.0 / total, (LANES, LANES))
    back = jnp.dot(tile[:, :points], residual[...], preferred_element_type=F32)
    for j in range(chans // LANES):
        lanes = slice(j * LANES, (j + 1) * LANES)
        partial[:, lanes] = image[:, lanes] + back[:, lanes] * recip[...]


def prepare(rays, residual, image, first_row, angles):
    cells, chans = image.shape
    all_points = rays.shape[0] * LANES
    rows = min(4, cells // LANES)
    fixed = lambda shape: pl.BlockSpec(shape, lambda i, *_: (0, 0))
    sliding = lambda width: pl.BlockSpec((rows * LANES, width), lambda i, *_: (i, 0))
    return pl.pallas_call(
        functools.partial(prepare_kernel, angles),
        grid_spec=pltpu.PrefetchScalarGridSpec(
            num_scalar_prefetch=1,
            grid=(cells // (rows * LANES),),
            in_specs=[fixed(rays.shape), fixed(residual.shape), sliding(chans)],
            out_specs=[sliding(all_points), sliding(LANES), sliding(chans)],
            scratch_shapes=[pltpu.VMEM((LANES, all_points), F32), pltpu.VMEM(rays.shape, F32)],
        ),
        out_shape=[
            jax.ShapeDtypeStruct((cells, all_points), BF16),
            jax.ShapeDtypeStruct((cells, LANES), F32),
            jax.ShapeDtypeStruct((cells, chans), F32),
        ],
        compiler_params=pltpu.CompilerParams(vmem_limit_bytes=16 * MIB),
        cost_estimate=pl.CostEstimate(
            flops=2 * all_points * cells * chans, bytes_accessed=8 * cells * chans, transcendentals=0
        ),
        name="prepare",
    )(first_row, rays, residual, image)


def back_kernel(parts, *refs):
    residuals, (tile, recip, partial, out, joined) = refs[:parts], refs[parts:]
    step = pl.program_id(0)
    points, chans = residuals[0].shape
    rows = out.shape[0]

    @pl.when(step == 0)
    def _():
        for d in range(parts):
            joined[d * points : (d + 1) * points, :] = residuals[d][...]

    here = pl.ds(pl.multiple_of(step * rows, rows), rows)
    back = jnp.dot(tile[here, points:], joined[...], preferred_element_type=F32)
    scale = recip[here, :]
    for j in range(chans // LANES):
        lanes = slice(j * LANES, (j + 1) * LANES)
        out[:, lanes] = partial[here, lanes] + back[:, lanes] * scale


def back_project(residuals, tile, recip, partial):
    cells, chans = partial.shape
    parts = len(residuals)
    points = residuals[0].shape[0]
    rows = min(1024, cells)
    vmem = pl.BlockSpec(memory_space=pltpu.VMEM)
    return pl.pallas_call(
        functools.partial(back_kernel, parts),
        grid=(cells // rows,),
        in_specs=[vmem] * (parts + 3),
        out_specs=pl.BlockSpec((rows, chans), lambda i: (i, 0)),
        scratch_shapes=[pltpu.VMEM((parts * points, chans), BF16)],
        out_shape=jax.ShapeDtypeStruct((cells, chans), F32),
        compiler_params=pltpu.CompilerParams(vmem_limit_bytes=32 * MIB),
        cost_estimate=pl.CostEstimate(
            flops=2 * parts * points * cells * chans,
            bytes_accessed=4 * cells * chans,
            transcendentals=0,
        ),
        name="back_project",
    )(*residuals, tile, recip, partial)


def rotate(x, axis, shift, n):
    return lax.ppermute(x, axis, [(i, (i + shift) % n) for i in range(n)])


def body(frames, counts, point_ray, channel_pair_weights, tile_bin, image):
    n_scan = lax.axis_size("scan")
    n_chan = lax.axis_size("chan")
    nx = n_chan // 2
    points = counts.shape[0]
    cells, chans = image.shape
    angles = points * n_scan // NIMG
    chan_me = lax.axis_index("chan")
    x_me, core_me = chan_me // 2, chan_me % 2
    first_row = (lax.axis_index("scan") * (cells // NIMG)).astype(jnp.int32).reshape(1)

    own_rays = point_ray.reshape(points // LANES, LANES)
    rays = [own_rays] + [rotate(own_rays, "scan", -d, n_scan) for d in range(1, n_scan)]
    all_rays = jnp.concatenate(rays, axis=0)

    shares = project(all_rays, image, first_row, angles, n_scan)
    arrived = [rotate(shares[d], "scan", d, n_scan) for d in range(1, n_scan)]

    place = []
    for e in range(nx):
        xi = (x_me + e) % nx
        place += [2 * xi + 1 - core_me, 2 * xi + core_me]
    place = jnp.stack(place).astype(jnp.int32)
    send, keep_own, keep_rest = integrate(
        frames, counts, channel_pair_weights, tile_bin, place, shares[0], nx, chans
    )
    partner = [(i, i ^ 1) for i in range(n_chan)]
    got = lax.ppermute(send, "chan", partner)
    pattern = keep_own + got[0].astype(F32)
    for e in range(1, nx):
        joined = (keep_rest[e - 1] + got[e].astype(F32)).astype(BF16)
        pattern = pattern + rotate(joined, "chan", 2 * e, n_chan).astype(F32)

    row_total = row_totals(own_rays, angles, keep_own)
    projected = shares[0]
    for part in arrived:
        projected = projected + part.astype(F32)
    residual = ((pattern * float(NIMG) - projected) / row_total[:, :1]).astype(BF16)
    others = [rotate(residual, "scan", -d, n_scan) for d in range(1, n_scan)]
    tile, col_recip, partial = prepare(all_rays, residual, image, first_row, angles)
    return back_project(others, tile, col_recip, partial)


def solution(mesh):
    in_specs = (
        P(("grp", "scan"), "chan"),
        P(("grp", "scan")),
        P(("grp", "scan")),
        P("chan", None, None),
        P("chan"),
        P(("grp", "scan"), "chan"),
    )
    out_specs = P(("grp", "scan"), "chan")
    return jax.shard_map(body, mesh=mesh, in_specs=in_specs, out_specs=out_specs, check_vma=False)
```

```python
import functools
import math

import jax
import jax.numpy as jnp
import numpy as np
from jax import lax
from jax.experimental import pallas as pl
from jax.experimental.pallas import tpu as pltpu
from jax.sharding import PartitionSpec as P

NIMG = 128
HALF = (NIMG - 1) / 2.0
LANES = 128
MIB = 1024 * 1024
F32 = jnp.float32
BF16 = jnp.bfloat16
SMALL = pl.CostEstimate(flops=1, bytes_accessed=1, transcendentals=0)
LARGE = pl.CostEstimate(flops=10**11, bytes_accessed=10**8, transcendentals=0)


def angle_tables(angles):
    theta = np.arange(angles, dtype=np.float32) * np.float32(math.pi / angles)
    return [float(c) for c in np.cos(theta)], [float(s) for s in np.sin(theta)]


def ray_geometry(rays, angles):
    cos_tab, sin_tab = angle_tables(angles)
    which = rays // NIMG
    offset = (rays - which * NIMG).astype(F32) - HALF
    cosine = jnp.zeros(rays.shape, F32)
    sine = jnp.zeros(rays.shape, F32)
    for a in range(angles):
        here = which == a
        cosine = jnp.where(here, cos_tab[a], cosine)
        sine = jnp.where(here, sin_tab[a], sine)
    return cosine, sine, offset


def hat(distance):
    return jnp.maximum((1.0 - jnp.abs(distance)).astype(BF16), jnp.zeros((), BF16))


def integrate_kernel(
    nx, per_chunk, tile_bin, place, after, counts, frames, weights, send, keep_own, keep_rest, member, acc
):
    step = pl.program_id(0)
    points, slots = member.shape
    blocks = weights.shape[0]
    tile_bins = acc.shape[2]

    @pl.when(step == 0)
    def _():
        acc[...] = jnp.zeros_like(acc)
        count_row = counts[...].astype(F32)
        row = lax.broadcasted_iota(jnp.int32, (points, points), 0)
        col = lax.broadcasted_iota(jnp.int32, (points, points), 1)
        ends = jnp.sum(jnp.where(col <= row, count_row, 0.0), axis=1, keepdims=True)
        count = jnp.sum(jnp.where(col == row, count_row, 0.0), axis=1, keepdims=True)
        slot = lax.broadcasted_iota(jnp.int32, (points, slots), 1).astype(F32)
        inside = jnp.logical_and(slot >= ends - count, slot < ends)
        member[...] = jnp.where(inside, 1.0 / count, 0.0).astype(BF16)

    means = jnp.dot(member[...], frames[...], preferred_element_type=F32).astype(BF16)
    for b in range(blocks):
        value = jnp.dot(
            means[:, b * LANES : (b + 1) * LANES], weights[b], preferred_element_type=F32
        )
        k = tile_bin[step * blocks + b]
        acc[k] += value[:, :tile_bins]
        acc[k + 1] += value[:, tile_bins:]

    @pl.when(step == pl.num_programs(0) - 1)
    def _():
        for e in range(nx):
            other, mine = place[2 * e], place[2 * e + 1]
            for j in range(per_chunk):
                lanes = slice(j * tile_bins, (j + 1) * tile_bins)
                send[e, :, lanes] = acc[other * per_chunk + j].astype(BF16)
                if e == 0:
                    keep_own[:, lanes] = acc[mine * per_chunk + j]
                else:
                    keep_rest[e - 1, :, lanes] = acc[mine * per_chunk + j]


def integrate(frames, counts, weights, tile_bin, place, after, nx, chans):
    slots, pixels = frames.shape
    points = counts.shape[0]
    nblocks, tile_pix, pair = weights.shape
    tile_bins = pair // 2
    blocks = 16 if nblocks % 16 == 0 else 1
    channel_blocks = 2 * nx * chans // tile_bins
    whole = lambda shape: pl.BlockSpec(shape, lambda i, *_: (0,) * len(shape))
    return pl.pallas_call(
        functools.partial(integrate_kernel, nx, chans // tile_bins),
        grid_spec=pltpu.PrefetchScalarGridSpec(
            num_scalar_prefetch=2,
            grid=(nblocks // blocks,),
            in_specs=[
                pl.BlockSpec(memory_space=pl.ANY),
                whole((1, points)),
                pl.BlockSpec((slots, blocks * tile_pix), lambda i, *_: (0, i)),
                pl.BlockSpec((blocks, tile_pix, pair), lambda i, *_: (i, 0, 0)),
            ],
            out_specs=[
                whole((nx, points, chans)),
                whole((points, chans)),
                whole((nx - 1, points, chans)),
            ],
            scratch_shapes=[
                pltpu.VMEM((points, slots), BF16),
                pltpu.VMEM((channel_blocks, points, tile_bins), F32),
            ],
        ),
        out_shape=[
            jax.ShapeDtypeStruct((nx, points, chans), BF16),
            jax.ShapeDtypeStruct((points, chans), F32),
            jax.ShapeDtypeStruct((nx - 1, points, chans), F32),
        ],
        compiler_params=pltpu.CompilerParams(vmem_limit_bytes=24 * MIB),
        cost_estimate=SMALL,
        name="integrate",
    )(tile_bin, place, after, counts.reshape(1, points), frames, weights)


def lower_kernel(image, low):
    low[...] = image[...].astype(BF16)


def lower(image):
    cells, chans = image.shape
    rows = min(1024, cells)
    block = pl.BlockSpec((rows, chans), lambda i: (i, 0))
    return pl.pallas_call(
        lower_kernel,
        grid=(cells // rows,),
        in_specs=[block],
        out_specs=block,
        out_shape=jax.ShapeDtypeStruct((cells, chans), BF16),
        compiler_params=pltpu.CompilerParams(vmem_limit_bytes=16 * MIB),
        cost_estimate=SMALL,
        name="lower",
    )(image)


def row_groups(rows):
    sizes = [min(4, rows)]
    while sum(sizes) < rows:
        sizes.append(min(8, rows - sum(sizes)))
    return sizes


def project_kernel(angles, first_row, rays, image, *refs):
    outs, (cosine, base, tile_a, tile_b, total) = refs[:-5], refs[-5:]
    parts = len(outs)
    points = total.shape[0] // parts
    tiles = (tile_a, tile_b)
    sizes = row_groups(image.shape[0] // LANES)

    def fill(group):
        first = first_row[0] + sum(sizes[:group])
        for i in range(sizes[group]):
            upos = (first + i).astype(F32) - HALF
            tiles[group % 2][:, i * LANES : (i + 1) * LANES] = hat(base[...] + cosine[...] * upos)

    cos_c, sin_c, off_c = ray_geometry(rays[...], angles)
    vpos = lax.broadcasted_iota(jnp.int32, (LANES, LANES), 1).astype(F32) - HALF
    for k in range(rays.shape[0]):
        here = slice(k * LANES, (k + 1) * LANES)
        column = lambda x: jnp.transpose(jnp.broadcast_to(x[k : k + 1, :], (LANES, LANES)))
        cosine[here, :] = column(cos_c)
        base[here, :] = column(sin_c) * vpos - column(off_c)
    fill(0)
    for group, size in enumerate(sizes):
        if group + 1 < len(sizes):
            fill(group + 1)
        start = sum(sizes[:group]) * LANES
        width = size * LANES
        product = jnp.dot(
            tiles[group % 2][:, :width], image[start : start + width, :], preferred_element_type=F32
        )
        if group == 0:
            total[...] = product
        elif group + 1 < len(sizes):
            total[...] += product
        else:
            product += total[...]
            for d in range(parts):
                here = slice(d * points, (d + 1) * points)
                outs[d][...] = product[here, :].astype(outs[d].dtype)


def project(rays, image, first_row, angles, kinds):
    cells, chans = image.shape
    all_points = rays.shape[0] * LANES
    points = all_points // len(kinds)
    widest = max(row_groups(cells // LANES)) * LANES
    vmem = pl.BlockSpec(memory_space=pltpu.VMEM)
    return pl.pallas_call(
        functools.partial(project_kernel, angles),
        in_specs=[pl.BlockSpec(memory_space=pltpu.SMEM), vmem, vmem],
        out_specs=[vmem] * len(kinds),
        scratch_shapes=[
            pltpu.VMEM((all_points, LANES), F32),
            pltpu.VMEM((all_points, LANES), F32),
            pltpu.VMEM((all_points, widest), BF16),
            pltpu.VMEM((all_points, widest), BF16),
            pltpu.VMEM((all_points, chans), F32),
        ],
        out_shape=[jax.ShapeDtypeStruct((points, chans), kind) for kind in kinds],
        compiler_params=pltpu.CompilerParams(vmem_limit_bytes=40 * MIB),
        cost_estimate=SMALL,
        name="project",
    )(first_row, rays, image)


def row_total_kernel(angles, after, rays, row_total):
    cos_r, sin_r, off_r = ray_geometry(rays[...], angles)
    vpos = lax.broadcasted_iota(jnp.int32, (LANES, LANES), 0).astype(F32) - HALF
    for k in range(rays.shape[0]):
        base = sin_r[k : k + 1, :] * vpos - off_r[k : k + 1, :]
        slope = cos_r[k : k + 1, :]

        def add_row(i, sums):
            upos = i.astype(F32) - HALF
            return sums + hat(base + slope * upos).astype(F32)

        sums = lax.fori_loop(0, NIMG, add_row, jnp.zeros((LANES, LANES), F32), unroll=4)
        total = jnp.sum(sums, axis=0, keepdims=True)
        row_total[k * LANES : (k + 1) * LANES, :] = jnp.transpose(
            jnp.broadcast_to(total, (LANES, LANES))
        )


def row_totals(rays, angles, after):
    points = rays.shape[0] * LANES
    vmem = pl.BlockSpec(memory_space=pltpu.VMEM)
    return pl.pallas_call(
        functools.partial(row_total_kernel, angles),
        in_specs=[pl.BlockSpec(memory_space=pl.ANY), vmem],
        out_specs=vmem,
        out_shape=jax.ShapeDtypeStruct((points, LANES), F32),
        compiler_params=pltpu.CompilerParams(vmem_limit_bytes=8 * MIB),
        cost_estimate=LARGE,
        name="row_totals",
    )(after, rays)


def join_kernel(row_total, own, *refs):
    arrived, (scaled, recip) = refs[:-2], refs[-2:]
    total = own[...]
    for part in arrived:
        total += part[...].astype(F32)
    recip[...] = 1.0 / row_total[...]
    for j in range(own.shape[1] // LANES):
        lanes = slice(j * LANES, (j + 1) * LANES)
        scaled[:, lanes] = total[:, lanes] * recip[...]


def join(row_total, own, arrived):
    vmem = pl.BlockSpec(memory_space=pltpu.VMEM)
    return pl.pallas_call(
        join_kernel,
        in_specs=[vmem] * (2 + len(arrived)),
        out_specs=[vmem, vmem],
        out_shape=[
            jax.ShapeDtypeStruct(own.shape, F32),
            jax.ShapeDtypeStruct(row_total.shape, F32),
        ],
        compiler_params=pltpu.CompilerParams(vmem_limit_bytes=8 * MIB),
        cost_estimate=LARGE,
        name="join",
    )(row_total, own, *arrived)


def prepare_kernel(angles, first_row, rays, residual, image, tile, recip, partial, base, cosine):
    step = pl.program_id(0)
    chunks = rays.shape[0]
    points, chans = residual.shape
    rows = tile.shape[0] // LANES

    @pl.when(step == 0)
    def _():
        cos_c, sin_c, off_c = ray_geometry(rays[...], angles)
        cosine[...] = cos_c
        vpos = lax.broadcasted_iota(jnp.int32, (LANES, LANES), 0).astype(F32) - HALF
        for k in range(chunks):
            base[:, k * LANES : (k + 1) * LANES] = sin_c[k : k + 1, :] * vpos - off_c[k : k + 1, :]

    for i in range(rows):
        here = slice(i * LANES, (i + 1) * LANES)
        upos = (first_row[0] + step * rows + i).astype(F32) - HALF
        sums = jnp.zeros((LANES, LANES), F32)
        for k in range(chunks):
            lanes = slice(k * LANES, (k + 1) * LANES)
            value = hat(base[:, lanes] + cosine[k : k + 1, :] * upos)
            tile[here, lanes] = value
            sums += value.astype(F32)
        total = jnp.sum(sums, axis=1, keepdims=True)
        recip[here, :] = jnp.broadcast_to(1.0 / total, (LANES, LANES))
    back = jnp.dot(tile[:, :points], residual[...], preferred_element_type=F32)
    for j in range(chans // LANES):
        lanes = slice(j * LANES, (j + 1) * LANES)
        partial[:, lanes] = image[:, lanes] + back[:, lanes] * recip[...]


def prepare(rays, residual, image, first_row, angles):
    cells, chans = image.shape
    all_points = rays.shape[0] * LANES
    rows = min(4, cells // LANES)
    fixed = lambda shape: pl.BlockSpec(shape, lambda i, *_: (0, 0))
    sliding = lambda width: pl.BlockSpec((rows * LANES, width), lambda i, *_: (i, 0))
    return pl.pallas_call(
        functools.partial(prepare_kernel, angles),
        grid_spec=pltpu.PrefetchScalarGridSpec(
            num_scalar_prefetch=1,
            grid=(cells // (rows * LANES),),
            in_specs=[fixed(rays.shape), fixed(residual.shape), sliding(chans)],
            out_specs=[sliding(all_points), sliding(LANES), sliding(chans)],
            scratch_shapes=[pltpu.VMEM((LANES, all_points), F32), pltpu.VMEM(rays.shape, F32)],
        ),
        out_shape=[
            jax.ShapeDtypeStruct((cells, all_points), BF16),
            jax.ShapeDtypeStruct((cells, LANES), F32),
            jax.ShapeDtypeStruct((cells, chans), F32),
        ],
        compiler_params=pltpu.CompilerParams(vmem_limit_bytes=16 * MIB),
        cost_estimate=SMALL,
        name="prepare",
    )(first_row, rays, residual, image)


def back_kernel(parts, *refs):
    residuals, (tile, recip, partial, out, joined) = refs[:parts], refs[parts:]
    step = pl.program_id(0)
    points, chans = residuals[0].shape
    rows = out.shape[0]

    @pl.when(step == 0)
    def _():
        for d in range(parts):
            joined[d * points : (d + 1) * points, :] = residuals[d][...]

    here = pl.ds(pl.multiple_of(step * rows, rows), rows)
    back = jnp.dot(tile[here, points:], joined[...], preferred_element_type=F32)
    scale = recip[here, :]
    for j in range(chans // LANES):
        lanes = slice(j * LANES, (j + 1) * LANES)
        out[:, lanes] = partial[here, lanes] + back[:, lanes] * scale


def back_project(residuals, tile, recip, partial):
    cells, chans = partial.shape
    parts = len(residuals)
    points = residuals[0].shape[0]
    rows = min(1024, cells)
    vmem = pl.BlockSpec(memory_space=pltpu.VMEM)
    return pl.pallas_call(
        functools.partial(back_kernel, parts),
        grid=(cells // rows,),
        in_specs=[vmem] * (parts + 3),
        out_specs=pl.BlockSpec((rows, chans), lambda i: (i, 0)),
        scratch_shapes=[pltpu.VMEM((parts * points, chans), BF16)],
        out_shape=jax.ShapeDtypeStruct((cells, chans), F32),
        compiler_params=pltpu.CompilerParams(vmem_limit_bytes=12 * MIB),
        cost_estimate=SMALL,
        name="back_project",
    )(*residuals, tile, recip, partial)


def rotate(x, axis, shift, n):
    return lax.ppermute(x, axis, [(i, (i + shift) % n) for i in range(n)])


def body(frames, counts, point_ray, channel_pair_weights, tile_bin, image):
    n_scan = lax.axis_size("scan")
    n_chan = lax.axis_size("chan")
    nx = n_chan // 2
    points = counts.shape[0]
    cells, chans = image.shape
    angles = points * n_scan // NIMG
    chan_me = lax.axis_index("chan")
    x_me, core_me = chan_me // 2, chan_me % 2
    first_row = (lax.axis_index("scan") * (cells // NIMG)).astype(jnp.int32).reshape(1)

    own_rays = point_ray.reshape(points // LANES, LANES)
    rays = [own_rays] + [rotate(own_rays, "scan", -d, n_scan) for d in range(1, n_scan)]
    all_rays = jnp.concatenate(rays, axis=0)

    shares = project(all_rays, lower(image), first_row, angles, [F32] + [BF16] * (n_scan - 1))
    arrived = [rotate(shares[d], "scan", d, n_scan) for d in range(1, n_scan)]

    place = []
    for e in range(nx):
        xi = (x_me + e) % nx
        place += [2 * xi + 1 - core_me, 2 * xi + core_me]
    place = jnp.stack(place).astype(jnp.int32)
    send, keep_own, keep_rest = integrate(
        frames, counts, channel_pair_weights, tile_bin, place, shares[0], nx, chans
    )
    partner = [(i, i ^ 1) for i in range(n_chan)]
    got = lax.ppermute(send, "chan", partner)
    pattern = keep_own + got[0].astype(F32)
    for e in range(1, nx):
        joined = (keep_rest[e - 1] + got[e].astype(F32)).astype(BF16)
        pattern = pattern + rotate(joined, "chan", 2 * e, n_chan).astype(F32)

    row_total = row_totals(own_rays, angles, keep_own)
    scaled, recip = join(row_total, shares[0], arrived)
    residual = (pattern * (float(NIMG) * recip[:, :1]) - scaled).astype(BF16)
    others = [rotate(residual, "scan", -d, n_scan) for d in range(1, n_scan)]
    tile, col_recip, partial = prepare(all_rays, residual, image, first_row, angles)
    return back_project(others, tile, col_recip, partial)


def solution(mesh):
    in_specs = (
        P(("grp", "scan"), "chan"),
        P(("grp", "scan")),
        P(("grp", "scan")),
        P("chan", None, None),
        P("chan"),
        P(("grp", "scan"), "chan"),
    )
    out_specs = P(("grp", "scan"), "chan")
    return jax.shard_map(body, mesh=mesh, in_specs=in_specs, out_specs=out_specs, check_vma=False)
```

```python
import functools
import math

import jax
import jax.numpy as jnp
import numpy as np
from jax import lax
from jax.experimental import pallas as pl
from jax.experimental.pallas import tpu as pltpu
from jax.sharding import PartitionSpec as P

NIMG = 128
HALF = (NIMG - 1) / 2.0
LANES = 128
MIB = 1024 * 1024
F32 = jnp.float32
BF16 = jnp.bfloat16
SMALL = pl.CostEstimate(flops=1, bytes_accessed=1, transcendentals=0)
LARGE = pl.CostEstimate(flops=10**11, bytes_accessed=10**8, transcendentals=0)


def angle_tables(angles):
    theta = np.arange(angles, dtype=np.float32) * np.float32(math.pi / angles)
    return [float(c) for c in np.cos(theta)], [float(s) for s in np.sin(theta)]


def ray_geometry(rays, angles):
    cos_tab, sin_tab = angle_tables(angles)
    which = rays // NIMG
    offset = (rays - which * NIMG).astype(F32) - HALF
    cosine = jnp.zeros(rays.shape, F32)
    sine = jnp.zeros(rays.shape, F32)
    for a in range(angles):
        here = which == a
        cosine = jnp.where(here, cos_tab[a], cosine)
        sine = jnp.where(here, sin_tab[a], sine)
    return cosine, sine, offset


def hat(distance):
    return jnp.maximum((1.0 - jnp.abs(distance)).astype(BF16), jnp.zeros((), BF16))


def integrate_kernel(
    nx, per_chunk, tile_bin, place, after, counts, frames, weights, send, acc, member
):
    step = pl.program_id(0)
    points, slots = member.shape
    blocks = weights.shape[0]
    tile_bins = acc.shape[2]

    @pl.when(step == 0)
    def _():
        acc[...] = jnp.zeros_like(acc)
        count_row = counts[...].astype(F32)
        row = lax.broadcasted_iota(jnp.int32, (points, points), 0)
        col = lax.broadcasted_iota(jnp.int32, (points, points), 1)
        ends = jnp.sum(jnp.where(col <= row, count_row, 0.0), axis=1, keepdims=True)
        count = jnp.sum(jnp.where(col == row, count_row, 0.0), axis=1, keepdims=True)
        slot = lax.broadcasted_iota(jnp.int32, (points, slots), 1).astype(F32)
        inside = jnp.logical_and(slot >= ends - count, slot < ends)
        member[...] = jnp.where(inside, 1.0 / count, 0.0).astype(BF16)

    means = jnp.dot(member[...], frames[...], preferred_element_type=F32).astype(BF16)
    for b in range(blocks):
        value = jnp.dot(
            means[:, b * LANES : (b + 1) * LANES], weights[b], preferred_element_type=F32
        )
        k = tile_bin[step * blocks + b]
        acc[k] += value[:, :tile_bins]
        acc[k + 1] += value[:, tile_bins:]

    @pl.when(step == pl.num_programs(0) - 1)
    def _():
        for e in range(nx):
            for j in range(per_chunk):
                lanes = slice(j * tile_bins, (j + 1) * tile_bins)
                send[e, :, lanes] = acc[place[2 * e] * per_chunk + j].astype(BF16)


def integrate(frames, counts, weights, tile_bin, place, after, nx, chans):
    slots, pixels = frames.shape
    points = counts.shape[0]
    nblocks, tile_pix, pair = weights.shape
    tile_bins = pair // 2
    blocks = 16 if nblocks % 16 == 0 else 1
    channel_blocks = 2 * nx * chans // tile_bins
    whole = lambda shape: pl.BlockSpec(shape, lambda i, *_: (0,) * len(shape))
    return pl.pallas_call(
        functools.partial(integrate_kernel, nx, chans // tile_bins),
        grid_spec=pltpu.PrefetchScalarGridSpec(
            num_scalar_prefetch=2,
            grid=(nblocks // blocks,),
            in_specs=[
                pl.BlockSpec(memory_space=pl.ANY),
                whole((1, points)),
                pl.BlockSpec((slots, blocks * tile_pix), lambda i, *_: (0, i)),
                pl.BlockSpec((blocks, tile_pix, pair), lambda i, *_: (i, 0, 0)),
            ],
            out_specs=[
                whole((nx, points, chans)),
                whole((channel_blocks, points, tile_bins)),
            ],
            scratch_shapes=[pltpu.VMEM((points, slots), BF16)],
        ),
        out_shape=[
            jax.ShapeDtypeStruct((nx, points, chans), BF16),
            jax.ShapeDtypeStruct((channel_blocks, points, tile_bins), F32),
        ],
        compiler_params=pltpu.CompilerParams(vmem_limit_bytes=24 * MIB),
        cost_estimate=SMALL,
        name="integrate",
    )(tile_bin, place, after, counts.reshape(1, points), frames, weights)


def select_kernel(place, acc, own, *rest):
    _, points, tile_bins = acc.shape
    per_chunk = own.shape[1] // tile_bins
    for e, keep in enumerate((own,) + rest):
        for j in range(per_chunk):
            lanes = slice(j * tile_bins, (j + 1) * tile_bins)
            keep[:, lanes] = acc[place[2 * e + 1] * per_chunk + j]


def select(place, acc, nx, chans):
    points = acc.shape[1]
    vmem = pl.BlockSpec(memory_space=pltpu.VMEM)
    return pl.pallas_call(
        select_kernel,
        in_specs=[pl.BlockSpec(memory_space=pltpu.SMEM), vmem],
        out_specs=[vmem] * nx,
        out_shape=[jax.ShapeDtypeStruct((points, chans), F32)] * nx,
        compiler_params=pltpu.CompilerParams(vmem_limit_bytes=8 * MIB),
        cost_estimate=LARGE,
        name="select",
    )(place, acc)


def row_groups(rows):
    sizes = [min(4, rows)]
    while sum(sizes) < rows:
        sizes.append(min(8, rows - sum(sizes)))
    return sizes


def project_kernel(angles, first_row, after, rays, image, *refs):
    outs, (cosine, base, tile_a, tile_b, total) = refs[:-5], refs[-5:]
    parts = len(outs)
    points = total.shape[0] // parts
    tiles = (tile_a, tile_b)
    sizes = row_groups(image.shape[0] // LANES)

    def fill(group):
        first = first_row[0] + sum(sizes[:group])
        for i in range(sizes[group]):
            upos = (first + i).astype(F32) - HALF
            tiles[group % 2][:, i * LANES : (i + 1) * LANES] = hat(base[...] + cosine[...] * upos)

    cos_c, sin_c, off_c = ray_geometry(rays[...], angles)
    vpos = lax.broadcasted_iota(jnp.int32, (LANES, LANES), 1).astype(F32) - HALF
    for k in range(rays.shape[0]):
        here = slice(k * LANES, (k + 1) * LANES)
        column = lambda x: jnp.transpose(jnp.broadcast_to(x[k : k + 1, :], (LANES, LANES)))
        cosine[here, :] = column(cos_c)
        base[here, :] = column(sin_c) * vpos - column(off_c)
    fill(0)
    for group, size in enumerate(sizes):
        if group + 1 < len(sizes):
            fill(group + 1)
        start = sum(sizes[:group]) * LANES
        width = size * LANES
        product = jnp.dot(
            tiles[group % 2][:, :width],
            image[start : start + width, :].astype(BF16),
            preferred_element_type=F32,
        )
        if group == 0:
            total[...] = product
        elif group + 1 < len(sizes):
            total[...] += product
        else:
            product += total[...]
            for d in range(parts):
                here = slice(d * points, (d + 1) * points)
                outs[d][...] = product[here, :].astype(outs[d].dtype)


def project(rays, image, first_row, after, angles, kinds):
    cells, chans = image.shape
    all_points = rays.shape[0] * LANES
    points = all_points // len(kinds)
    widest = max(row_groups(cells // LANES)) * LANES
    vmem = pl.BlockSpec(memory_space=pltpu.VMEM)
    return pl.pallas_call(
        functools.partial(project_kernel, angles),
        in_specs=[
            pl.BlockSpec(memory_space=pltpu.SMEM),
            pl.BlockSpec(memory_space=pl.ANY),
            vmem,
            vmem,
        ],
        out_specs=[vmem] * len(kinds),
        scratch_shapes=[
            pltpu.VMEM((all_points, LANES), F32),
            pltpu.VMEM((all_points, LANES), F32),
            pltpu.VMEM((all_points, widest), BF16),
            pltpu.VMEM((all_points, widest), BF16),
            pltpu.VMEM((all_points, chans), F32),
        ],
        out_shape=[jax.ShapeDtypeStruct((points, chans), kind) for kind in kinds],
        compiler_params=pltpu.CompilerParams(vmem_limit_bytes=40 * MIB),
        cost_estimate=pl.CostEstimate(
            flops=4 * all_points * cells * chans, bytes_accessed=4 * cells * chans, transcendentals=0
        ),
        name="project",
    )(first_row, after, rays, image)


def row_total_kernel(angles, rays, row_total):
    cos_r, sin_r, off_r = ray_geometry(rays[...], angles)
    vpos = lax.broadcasted_iota(jnp.int32, (LANES, LANES), 0).astype(F32) - HALF
    for k in range(rays.shape[0]):
        base = sin_r[k : k + 1, :] * vpos - off_r[k : k + 1, :]
        slope = cos_r[k : k + 1, :]

        def add_row(i, sums):
            upos = i.astype(F32) - HALF
            return sums + hat(base + slope * upos).astype(F32)

        sums = lax.fori_loop(0, NIMG, add_row, jnp.zeros((LANES, LANES), F32), unroll=4)
        total = jnp.sum(sums, axis=0, keepdims=True)
        row_total[k * LANES : (k + 1) * LANES, :] = jnp.transpose(
            jnp.broadcast_to(total, (LANES, LANES))
        )


def row_totals(rays, angles):
    points = rays.shape[0] * LANES
    vmem = pl.BlockSpec(memory_space=pltpu.VMEM)
    return pl.pallas_call(
        functools.partial(row_total_kernel, angles),
        in_specs=[vmem],
        out_specs=vmem,
        out_shape=jax.ShapeDtypeStruct((points, LANES), F32),
        compiler_params=pltpu.CompilerParams(vmem_limit_bytes=8 * MIB),
        cost_estimate=LARGE,
        name="row_totals",
    )(rays)


def join_kernel(row_total, own, *refs):
    arrived, (scaled, recip) = refs[:-2], refs[-2:]
    total = own[...]
    for part in arrived:
        total += part[...].astype(F32)
    recip[...] = 1.0 / row_total[...]
    for j in range(own.shape[1] // LANES):
        lanes = slice(j * LANES, (j + 1) * LANES)
        scaled[:, lanes] = total[:, lanes] * recip[...]


def join(row_total, own, arrived):
    vmem = pl.BlockSpec(memory_space=pltpu.VMEM)
    return pl.pallas_call(
        join_kernel,
        in_specs=[vmem] * (2 + len(arrived)),
        out_specs=[vmem, vmem],
        out_shape=[
            jax.ShapeDtypeStruct(own.shape, F32),
            jax.ShapeDtypeStruct(row_total.shape, F32),
        ],
        compiler_params=pltpu.CompilerParams(vmem_limit_bytes=8 * MIB),
        cost_estimate=LARGE,
        name="join",
    )(row_total, own, *arrived)


def prepare_kernel(angles, first_row, rays, residual, image, tile, recip, partial, base, cosine):
    step = pl.program_id(0)
    chunks = rays.shape[0]
    points, chans = residual.shape
    rows = tile.shape[0] // LANES

    @pl.when(step == 0)
    def _():
        cos_c, sin_c, off_c = ray_geometry(rays[...], angles)
        cosine[...] = cos_c
        vpos = lax.broadcasted_iota(jnp.int32, (LANES, LANES), 0).astype(F32) - HALF
        for k in range(chunks):
            base[:, k * LANES : (k + 1) * LANES] = sin_c[k : k + 1, :] * vpos - off_c[k : k + 1, :]

    for i in range(rows):
        here = slice(i * LANES, (i + 1) * LANES)
        upos = (first_row[0] + step * rows + i).astype(F32) - HALF
        sums = jnp.zeros((LANES, LANES), F32)
        for k in range(chunks):
            lanes = slice(k * LANES, (k + 1) * LANES)
            value = hat(base[:, lanes] + cosine[k : k + 1, :] * upos)
            tile[here, lanes] = value
            sums += value.astype(F32)
        total = jnp.sum(sums, axis=1, keepdims=True)
        recip[here, :] = jnp.broadcast_to(1.0 / total, (LANES, LANES))
    back = jnp.dot(tile[:, :points], residual[...], preferred_element_type=F32)
    for j in range(chans // LANES):
        lanes = slice(j * LANES, (j + 1) * LANES)
        partial[:, lanes] = image[:, lanes] + back[:, lanes] * recip[...]


def prepare(rays, residual, image, first_row, angles):
    cells, chans = image.shape
    all_points = rays.shape[0] * LANES
    rows = min(4, cells // LANES)
    fixed = lambda shape: pl.BlockSpec(shape, lambda i, *_: (0, 0))
    sliding = lambda width: pl.BlockSpec((rows * LANES, width), lambda i, *_: (i, 0))
    return pl.pallas_call(
        functools.partial(prepare_kernel, angles),
        grid_spec=pltpu.PrefetchScalarGridSpec(
            num_scalar_prefetch=1,
            grid=(cells // (rows * LANES),),
            in_specs=[fixed(rays.shape), fixed(residual.shape), sliding(chans)],
            out_specs=[sliding(all_points), sliding(LANES), sliding(chans)],
            scratch_shapes=[pltpu.VMEM((LANES, all_points), F32), pltpu.VMEM(rays.shape, F32)],
        ),
        out_shape=[
            jax.ShapeDtypeStruct((cells, all_points), BF16),
            jax.ShapeDtypeStruct((cells, LANES), F32),
            jax.ShapeDtypeStruct((cells, chans), F32),
        ],
        compiler_params=pltpu.CompilerParams(vmem_limit_bytes=16 * MIB),
        cost_estimate=SMALL,
        name="prepare",
    )(first_row, rays, residual, image)


def back_kernel(parts, *refs):
    residuals, (tile, recip, partial, out, joined) = refs[:parts], refs[parts:]
    step = pl.program_id(0)
    points, chans = residuals[0].shape
    rows = out.shape[0]

    @pl.when(step == 0)
    def _():
        for d in range(parts):
            joined[d * points : (d + 1) * points, :] = residuals[d][...]

    here = pl.ds(pl.multiple_of(step * rows, rows), rows)
    back = jnp.dot(tile[here, points:], joined[...], preferred_element_type=F32)
    scale = recip[here, :]
    for j in range(chans // LANES):
        lanes = slice(j * LANES, (j + 1) * LANES)
        out[:, lanes] = partial[here, lanes] + back[:, lanes] * scale


def back_project(residuals, tile, recip, partial):
    cells, chans = partial.shape
    parts = len(residuals)
    points = residuals[0].shape[0]
    rows = min(1024, cells)
    vmem = pl.BlockSpec(memory_space=pltpu.VMEM)
    return pl.pallas_call(
        functools.partial(back_kernel, parts),
        grid=(cells // rows,),
        in_specs=[vmem] * (parts + 3),
        out_specs=pl.BlockSpec((rows, chans), lambda i: (i, 0)),
        scratch_shapes=[pltpu.VMEM((parts * points, chans), BF16)],
        out_shape=jax.ShapeDtypeStruct((cells, chans), F32),
        compiler_params=pltpu.CompilerParams(vmem_limit_bytes=12 * MIB),
        cost_estimate=SMALL,
        name="back_project",
    )(*residuals, tile, recip, partial)


def rotate(x, axis, shift, n):
    return lax.ppermute(x, axis, [(i, (i + shift) % n) for i in range(n)])


def body(frames, counts, point_ray, channel_pair_weights, tile_bin, image):
    n_scan = lax.axis_size("scan")
    n_chan = lax.axis_size("chan")
    nx = n_chan // 2
    points = counts.shape[0]
    cells, chans = image.shape
    angles = points * n_scan // NIMG
    chan_me = lax.axis_index("chan")
    x_me, core_me = chan_me // 2, chan_me % 2
    first_row = (lax.axis_index("scan") * (cells // NIMG)).astype(jnp.int32).reshape(1)

    own_rays = point_ray.reshape(points // LANES, LANES)
    rays = [own_rays] + [rotate(own_rays, "scan", -d, n_scan) for d in range(1, n_scan)]
    all_rays = jnp.concatenate(rays, axis=0)

    row_total = row_totals(own_rays, angles)
    kinds = [F32] + [BF16] * (n_scan - 1)
    shares = project(all_rays, image, first_row, row_total, angles, kinds)
    arrived = [rotate(shares[d], "scan", d, n_scan) for d in range(1, n_scan)]

    place = []
    for e in range(nx):
        xi = (x_me + e) % nx
        place += [2 * xi + 1 - core_me, 2 * xi + core_me]
    place = jnp.stack(place).astype(jnp.int32)
    send, sums = integrate(
        frames, counts, channel_pair_weights, tile_bin, place, shares[0], nx, chans
    )
    keep = select(place, sums, nx, chans)
    partner = [(i, i ^ 1) for i in range(n_chan)]
    got = lax.ppermute(send, "chan", partner)
    pattern = keep[0] + got[0].astype(F32)
    for e in range(1, nx):
        joined = (keep[e] + got[e].astype(F32)).astype(BF16)
        pattern = pattern + rotate(joined, "chan", 2 * e, n_chan).astype(F32)

    scaled, recip = join(row_total, shares[0], arrived)
    residual = (pattern * (float(NIMG) * recip[:, :1]) - scaled).astype(BF16)
    others = [rotate(residual, "scan", -d, n_scan) for d in range(1, n_scan)]
    tile, col_recip, partial = prepare(all_rays, residual, image, first_row, angles)
    return back_project(others, tile, col_recip, partial)


def solution(mesh):
    in_specs = (
        P(("grp", "scan"), "chan"),
        P(("grp", "scan")),
        P(("grp", "scan")),
        P("chan", None, None),
        P("chan"),
        P(("grp", "scan"), "chan"),
    )
    out_specs = P(("grp", "scan"), "chan")
    return jax.shard_map(body, mesh=mesh, in_specs=in_specs, out_specs=out_specs, check_vma=False)
```

```python
import functools
import math

import jax
import jax.numpy as jnp
import numpy as np
from jax import lax
from jax.experimental import pallas as pl
from jax.experimental.pallas import tpu as pltpu
from jax.sharding import PartitionSpec as P

NIMG = 128
HALF = (NIMG - 1) / 2.0
LANES = 128
MIB = 1024 * 1024
F32 = jnp.float32
BF16 = jnp.bfloat16
SMALL = pl.CostEstimate(flops=1, bytes_accessed=1, transcendentals=0)
LARGE = pl.CostEstimate(flops=10**11, bytes_accessed=10**8, transcendentals=0)


def angle_tables(angles):
    theta = np.arange(angles, dtype=np.float32) * np.float32(math.pi / angles)
    return [float(c) for c in np.cos(theta)], [float(s) for s in np.sin(theta)]


def ray_geometry(rays, angles):
    cos_tab, sin_tab = angle_tables(angles)
    which = rays // NIMG
    offset = (rays - which * NIMG).astype(F32) - HALF
    cosine = jnp.zeros(rays.shape, F32)
    sine = jnp.zeros(rays.shape, F32)
    for a in range(angles):
        here = which == a
        cosine = jnp.where(here, cos_tab[a], cosine)
        sine = jnp.where(here, sin_tab[a], sine)
    return cosine, sine, offset


def hat(distance):
    return jnp.maximum((1.0 - jnp.abs(distance)).astype(BF16), jnp.zeros((), BF16))


def integrate_kernel(
    nx, per_chunk, tile_bin, place, after, counts, frames, weights, send, acc, member
):
    step = pl.program_id(0)
    points, slots = member.shape
    blocks = weights.shape[0]
    tile_bins = acc.shape[2]

    @pl.when(step == 0)
    def _():
        acc[...] = jnp.zeros_like(acc)
        count_row = counts[...].astype(F32)
        row = lax.broadcasted_iota(jnp.int32, (points, points), 0)
        col = lax.broadcasted_iota(jnp.int32, (points, points), 1)
        ends = jnp.sum(jnp.where(col <= row, count_row, 0.0), axis=1, keepdims=True)
        count = jnp.sum(jnp.where(col == row, count_row, 0.0), axis=1, keepdims=True)
        slot = lax.broadcasted_iota(jnp.int32, (points, slots), 1).astype(F32)
        inside = jnp.logical_and(slot >= ends - count, slot < ends)
        member[...] = jnp.where(inside, 1.0 / count, 0.0).astype(BF16)

    means = jnp.dot(member[...], frames[...], preferred_element_type=F32).astype(BF16)
    for b in range(blocks):
        value = jnp.dot(
            means[:, b * LANES : (b + 1) * LANES], weights[b], preferred_element_type=F32
        )
        k = tile_bin[step * blocks + b]
        acc[k] += value[:, :tile_bins]
        acc[k + 1] += value[:, tile_bins:]

    @pl.when(step == pl.num_programs(0) - 1)
    def _():
        for e in range(nx):
            for j in range(per_chunk):
                lanes = slice(j * tile_bins, (j + 1) * tile_bins)
                send[e, :, lanes] = acc[place[2 * e] * per_chunk + j].astype(BF16)


def integrate(frames, counts, weights, tile_bin, place, after, nx, chans):
    slots, pixels = frames.shape
    points = counts.shape[0]
    nblocks, tile_pix, pair = weights.shape
    tile_bins = pair // 2
    blocks = 16 if nblocks % 16 == 0 else 1
    channel_blocks = 2 * nx * chans // tile_bins
    whole = lambda shape: pl.BlockSpec(shape, lambda i, *_: (0,) * len(shape))
    return pl.pallas_call(
        functools.partial(integrate_kernel, nx, chans // tile_bins),
        grid_spec=pltpu.PrefetchScalarGridSpec(
            num_scalar_prefetch=2,
            grid=(nblocks // blocks,),
            in_specs=[
                pl.BlockSpec(memory_space=pl.ANY),
                whole((1, points)),
                pl.BlockSpec((slots, blocks * tile_pix), lambda i, *_: (0, i)),
                pl.BlockSpec((blocks, tile_pix, pair), lambda i, *_: (i, 0, 0)),
            ],
            out_specs=[
                whole((nx, points, chans)),
                whole((channel_blocks, points, tile_bins)),
            ],
            scratch_shapes=[pltpu.VMEM((points, slots), BF16)],
        ),
        out_shape=[
            jax.ShapeDtypeStruct((nx, points, chans), BF16),
            jax.ShapeDtypeStruct((channel_blocks, points, tile_bins), F32),
        ],
        compiler_params=pltpu.CompilerParams(vmem_limit_bytes=24 * MIB),
        cost_estimate=SMALL,
        name="integrate",
    )(tile_bin, place, after, counts.reshape(1, points), frames, weights)


def select_kernel(place, acc, own, *rest):
    _, points, tile_bins = acc.shape
    per_chunk = own.shape[1] // tile_bins
    for e, keep in enumerate((own,) + rest):
        for j in range(per_chunk):
            lanes = slice(j * tile_bins, (j + 1) * tile_bins)
            keep[:, lanes] = acc[place[2 * e + 1] * per_chunk + j]


def select(place, acc, nx, chans):
    points = acc.shape[1]
    vmem = pl.BlockSpec(memory_space=pltpu.VMEM)
    return pl.pallas_call(
        select_kernel,
        in_specs=[pl.BlockSpec(memory_space=pltpu.SMEM), vmem],
        out_specs=[vmem] * nx,
        out_shape=[jax.ShapeDtypeStruct((points, chans), F32)] * nx,
        compiler_params=pltpu.CompilerParams(vmem_limit_bytes=8 * MIB),
        cost_estimate=LARGE,
        name="select",
    )(place, acc)


def row_groups(rows):
    sizes = [min(2, rows)]
    while sum(sizes) < rows:
        sizes.append(min(6, rows - sum(sizes)))
    return sizes


def project_kernel(angles, first_row, after, rays, image, *refs):
    outs, (staged, cosine, base, tile_a, tile_b, total, arrived) = refs[:-7], refs[-7:]
    parts = len(outs)
    points = total.shape[0] // parts
    tiles = (tile_a, tile_b)
    sizes = row_groups(image.shape[0] // LANES)

    def cells(group):
        return slice(sum(sizes[:group]) * LANES, sum(sizes[: group + 1]) * LANES)

    def load(group):
        here = cells(group)
        return pltpu.make_async_copy(
            image.at[here, :], staged.at[here, :], arrived.at[group]
        )

    def fill(group):
        first = first_row[0] + sum(sizes[:group])
        for i in range(sizes[group]):
            upos = (first + i).astype(F32) - HALF
            tiles[group % 2][:, i * LANES : (i + 1) * LANES] = hat(base[...] + cosine[...] * upos)

    for group in range(min(2, len(sizes))):
        load(group).start()
    cos_c, sin_c, off_c = ray_geometry(rays[...], angles)
    vpos = lax.broadcasted_iota(jnp.int32, (LANES, LANES), 1).astype(F32) - HALF
    for k in range(rays.shape[0]):
        here = slice(k * LANES, (k + 1) * LANES)
        column = lambda x: jnp.transpose(jnp.broadcast_to(x[k : k + 1, :], (LANES, LANES)))
        cosine[here, :] = column(cos_c)
        base[here, :] = column(sin_c) * vpos - column(off_c)
    fill(0)
    for group, size in enumerate(sizes):
        if group + 1 < len(sizes):
            fill(group + 1)
        load(group).wait()
        if group + 2 < len(sizes):
            load(group + 2).start()
        product = jnp.dot(
            tiles[group % 2][:, : size * LANES],
            staged[cells(group), :].astype(BF16),
            preferred_element_type=F32,
        )
        if group == 0:
            total[...] = product
        elif group + 1 < len(sizes):
            total[...] += product
        else:
            product += total[...]
            for d in range(parts):
                here = slice(d * points, (d + 1) * points)
                outs[d][...] = product[here, :].astype(outs[d].dtype)


def project(rays, image, first_row, after, angles, kinds):
    cells, chans = image.shape
    all_points = rays.shape[0] * LANES
    points = all_points // len(kinds)
    sizes = row_groups(cells // LANES)
    widest = max(sizes) * LANES
    vmem = pl.BlockSpec(memory_space=pltpu.VMEM)
    anywhere = pl.BlockSpec(memory_space=pl.ANY)
    return pl.pallas_call(
        functools.partial(project_kernel, angles),
        in_specs=[pl.BlockSpec(memory_space=pltpu.SMEM), anywhere, vmem, anywhere],
        out_specs=[vmem] * len(kinds),
        scratch_shapes=[
            pltpu.VMEM((cells, chans), F32),
            pltpu.VMEM((all_points, LANES), F32),
            pltpu.VMEM((all_points, LANES), F32),
            pltpu.VMEM((all_points, widest), BF16),
            pltpu.VMEM((all_points, widest), BF16),
            pltpu.VMEM((all_points, chans), F32),
            pltpu.SemaphoreType.DMA((len(sizes),)),
        ],
        out_shape=[jax.ShapeDtypeStruct((points, chans), kind) for kind in kinds],
        compiler_params=pltpu.CompilerParams(vmem_limit_bytes=40 * MIB),
        cost_estimate=pl.CostEstimate(
            flops=4 * all_points * cells * chans, bytes_accessed=4 * cells * chans, transcendentals=0
        ),
        name="project",
    )(first_row, after, rays, pltpu.with_memory_space_constraint(image, pltpu.HBM))


def row_total_kernel(angles, rays, row_total):
    cos_r, sin_r, off_r = ray_geometry(rays[...], angles)
    vpos = lax.broadcasted_iota(jnp.int32, (LANES, LANES), 0).astype(F32) - HALF
    for k in range(rays.shape[0]):
        base = sin_r[k : k + 1, :] * vpos - off_r[k : k + 1, :]
        slope = cos_r[k : k + 1, :]

        def add_row(i, sums):
            upos = i.astype(F32) - HALF
            return sums + hat(base + slope * upos).astype(F32)

        sums = lax.fori_loop(0, NIMG, add_row, jnp.zeros((LANES, LANES), F32), unroll=4)
        total = jnp.sum(sums, axis=0, keepdims=True)
        row_total[k * LANES : (k + 1) * LANES, :] = jnp.transpose(
            jnp.broadcast_to(total, (LANES, LANES))
        )


def row_totals(rays, angles):
    points = rays.shape[0] * LANES
    vmem = pl.BlockSpec(memory_space=pltpu.VMEM)
    return pl.pallas_call(
        functools.partial(row_total_kernel, angles),
        in_specs=[vmem],
        out_specs=vmem,
        out_shape=jax.ShapeDtypeStruct((points, LANES), F32),
        compiler_params=pltpu.CompilerParams(vmem_limit_bytes=8 * MIB),
        cost_estimate=LARGE,
        name="row_totals",
    )(rays)


def join_kernel(row_total, own, *refs):
    arrived, (scaled, recip) = refs[:-2], refs[-2:]
    total = own[...]
    for part in arrived:
        total += part[...].astype(F32)
    recip[...] = 1.0 / row_total[...]
    for j in range(own.shape[1] // LANES):
        lanes = slice(j * LANES, (j + 1) * LANES)
        scaled[:, lanes] = total[:, lanes] * recip[...]


def join(row_total, own, arrived):
    vmem = pl.BlockSpec(memory_space=pltpu.VMEM)
    return pl.pallas_call(
        join_kernel,
        in_specs=[vmem] * (2 + len(arrived)),
        out_specs=[vmem, vmem],
        out_shape=[
            jax.ShapeDtypeStruct(own.shape, F32),
            jax.ShapeDtypeStruct(row_total.shape, F32),
        ],
        compiler_params=pltpu.CompilerParams(vmem_limit_bytes=8 * MIB),
        cost_estimate=LARGE,
        name="join",
    )(row_total, own, *arrived)


def prepare_kernel(angles, early, first_row, rays, *refs):
    residuals, (image, tile, recip, partial, base, cosine) = refs[:early], refs[early:]
    step = pl.program_id(0)
    chunks = rays.shape[0]
    points, chans = residuals[0].shape
    rows = tile.shape[0] // LANES

    @pl.when(step == 0)
    def _():
        cos_c, sin_c, off_c = ray_geometry(rays[...], angles)
        cosine[...] = cos_c
        vpos = lax.broadcasted_iota(jnp.int32, (LANES, LANES), 0).astype(F32) - HALF
        for k in range(chunks):
            base[:, k * LANES : (k + 1) * LANES] = sin_c[k : k + 1, :] * vpos - off_c[k : k + 1, :]

    for i in range(rows):
        here = slice(i * LANES, (i + 1) * LANES)
        upos = (first_row[0] + step * rows + i).astype(F32) - HALF
        sums = jnp.zeros((LANES, LANES), F32)
        for k in range(chunks):
            lanes = slice(k * LANES, (k + 1) * LANES)
            value = hat(base[:, lanes] + cosine[k : k + 1, :] * upos)
            tile[here, lanes] = value
            sums += value.astype(F32)
        total = jnp.sum(sums, axis=1, keepdims=True)
        recip[here, :] = jnp.broadcast_to(1.0 / total, (LANES, LANES))
    joined = jnp.concatenate([r[...] for r in residuals], axis=0)
    back = jnp.dot(tile[:, : early * points], joined, preferred_element_type=F32)
    for j in range(chans // LANES):
        lanes = slice(j * LANES, (j + 1) * LANES)
        partial[:, lanes] = image[:, lanes] + back[:, lanes] * recip[...]


def prepare(rays, residuals, image, first_row, angles):
    cells, chans = image.shape
    all_points = rays.shape[0] * LANES
    rows = min(4, cells // LANES)
    fixed = lambda shape: pl.BlockSpec(shape, lambda i, *_: (0, 0))
    sliding = lambda width: pl.BlockSpec((rows * LANES, width), lambda i, *_: (i, 0))
    return pl.pallas_call(
        functools.partial(prepare_kernel, angles, len(residuals)),
        grid_spec=pltpu.PrefetchScalarGridSpec(
            num_scalar_prefetch=1,
            grid=(cells // (rows * LANES),),
            in_specs=[fixed(rays.shape)]
            + [fixed(r.shape) for r in residuals]
            + [sliding(chans)],
            out_specs=[sliding(all_points), sliding(LANES), sliding(chans)],
            scratch_shapes=[pltpu.VMEM((LANES, all_points), F32), pltpu.VMEM(rays.shape, F32)],
        ),
        out_shape=[
            jax.ShapeDtypeStruct((cells, all_points), BF16),
            jax.ShapeDtypeStruct((cells, LANES), F32),
            jax.ShapeDtypeStruct((cells, chans), F32),
        ],
        compiler_params=pltpu.CompilerParams(vmem_limit_bytes=16 * MIB),
        cost_estimate=SMALL,
        name="prepare",
    )(first_row, rays, *residuals, image)


def back_kernel(parts, *refs):
    residuals, (tile, recip, partial, out, joined, staged, sent) = refs[:parts], refs[parts:]
    points, chans = residuals[0].shape
    skip = tile.shape[1] - parts * points
    chunks = sent.shape[0]
    rows = out.shape[0] // chunks

    for d in range(parts):
        joined[d * points : (d + 1) * points, :] = residuals[d][...]
    copies = []
    for chunk in range(chunks):
        here = slice(chunk * rows, (chunk + 1) * rows)
        back = jnp.dot(tile[here, skip:], joined[...], preferred_element_type=F32)
        scale = recip[here, :]
        for j in range(chans // LANES):
            lanes = slice(j * LANES, (j + 1) * LANES)
            staged[here, lanes] = partial[here, lanes] + back[:, lanes] * scale
        copies.append(
            pltpu.make_async_copy(staged.at[here, :], out.at[here, :], sent.at[chunk])
        )
        copies[-1].start()
    for copy in copies:
        copy.wait()


def back_project(residuals, tile, recip, partial):
    cells, chans = partial.shape
    parts = len(residuals)
    points = residuals[0].shape[0]
    chunks = max(1, cells // 512)
    vmem = pl.BlockSpec(memory_space=pltpu.VMEM)
    return pl.pallas_call(
        functools.partial(back_kernel, parts),
        in_specs=[vmem] * (parts + 3),
        out_specs=pl.BlockSpec(memory_space=pl.ANY),
        scratch_shapes=[
            pltpu.VMEM((parts * points, chans), BF16),
            pltpu.VMEM((cells, chans), F32),
            pltpu.SemaphoreType.DMA((chunks,)),
        ],
        out_shape=jax.ShapeDtypeStruct((cells, chans), F32),
        compiler_params=pltpu.CompilerParams(vmem_limit_bytes=16 * MIB),
        cost_estimate=SMALL,
        name="back_project",
    )(*residuals, tile, recip, partial)


def rotate(x, axis, shift, n):
    return lax.ppermute(x, axis, [(i, (i + shift) % n) for i in range(n)])


def body(frames, counts, point_ray, channel_pair_weights, tile_bin, image):
    n_scan = lax.axis_size("scan")
    n_chan = lax.axis_size("chan")
    nx = n_chan // 2
    points = counts.shape[0]
    cells, chans = image.shape
    angles = points * n_scan // NIMG
    chan_me = lax.axis_index("chan")
    x_me, core_me = chan_me // 2, chan_me % 2
    first_row = (lax.axis_index("scan") * (cells // NIMG)).astype(jnp.int32).reshape(1)

    order = sorted(range(1, n_scan), key=lambda d: (2 * d != n_scan, d))
    own_rays = point_ray.reshape(points // LANES, LANES)
    rays = [own_rays] + [rotate(own_rays, "scan", -d, n_scan) for d in order]
    all_rays = jnp.concatenate(rays, axis=0)

    row_total = row_totals(own_rays, angles)
    kinds = [F32] + [BF16] * (n_scan - 1)
    own_share, *shares = project(all_rays, image, first_row, row_total, angles, kinds)
    arrived = [rotate(share, "scan", d, n_scan) for d, share in zip(order, shares)]

    place = []
    for e in range(nx):
        xi = (x_me + e) % nx
        place += [2 * xi + 1 - core_me, 2 * xi + core_me]
    place = jnp.stack(place).astype(jnp.int32)
    send, sums = integrate(
        frames, counts, channel_pair_weights, tile_bin, place, own_share, nx, chans
    )
    keep = select(place, sums, nx, chans)
    partner = [(i, i ^ 1) for i in range(n_chan)]
    got = lax.ppermute(send, "chan", partner)
    pattern = keep[0] + got[0].astype(F32)
    for e in range(1, nx):
        joined = (keep[e] + got[e].astype(F32)).astype(BF16)
        pattern = pattern + rotate(joined, "chan", 2 * e, n_chan).astype(F32)

    scaled, recip = join(row_total, own_share, arrived)
    residual = (pattern * (float(NIMG) * recip[:, :1]) - scaled).astype(BF16)
    others = [rotate(residual, "scan", -d, n_scan) for d in order]
    tile, col_recip, partial = prepare(all_rays, [residual, others[0]], image, first_row, angles)
    return back_project(others[1:], tile, col_recip, partial)


def solution(mesh):
    in_specs = (
        P(("grp", "scan"), "chan"),
        P(("grp", "scan")),
        P(("grp", "scan")),
        P("chan", None, None),
        P("chan"),
        P(("grp", "scan"), "chan"),
    )
    out_specs = P(("grp", "scan"), "chan")
    return jax.shard_map(body, mesh=mesh, in_specs=in_specs, out_specs=out_specs, check_vma=False)
```

```python
import functools
import math

import jax
import jax.numpy as jnp
import numpy as np
from jax import lax
from jax.experimental import pallas as pl
from jax.experimental.pallas import tpu as pltpu
from jax.sharding import PartitionSpec as P

NIMG = 128
HALF = (NIMG - 1) / 2.0
LANES = 128
MIB = 1024 * 1024
F32 = jnp.float32
BF16 = jnp.bfloat16
SMALL = pl.CostEstimate(flops=1, bytes_accessed=1, transcendentals=0)
LARGE = pl.CostEstimate(flops=10**11, bytes_accessed=10**8, transcendentals=0)


def angle_tables(angles):
    theta = np.arange(angles, dtype=np.float32) * np.float32(math.pi / angles)
    return [float(c) for c in np.cos(theta)], [float(s) for s in np.sin(theta)]


def ray_geometry(rays, angles):
    cos_tab, sin_tab = angle_tables(angles)
    which = rays // NIMG
    offset = (rays - which * NIMG).astype(F32) - HALF
    cosine = jnp.zeros(rays.shape, F32)
    sine = jnp.zeros(rays.shape, F32)
    for a in range(angles):
        here = which == a
        cosine = jnp.where(here, cos_tab[a], cosine)
        sine = jnp.where(here, sin_tab[a], sine)
    return cosine, sine, offset


def hat(distance):
    return jnp.maximum((1.0 - jnp.abs(distance)).astype(BF16), jnp.zeros((), BF16))


def integrate_kernel(
    nx, per_chunk, tile_bin, place, after, counts, frames, weights, send, acc, member
):
    step = pl.program_id(0)
    points, slots = member.shape
    blocks = weights.shape[0]
    tile_bins = acc.shape[2]

    @pl.when(step == 0)
    def _():
        acc[...] = jnp.zeros_like(acc)
        count_row = counts[...].astype(F32)
        row = lax.broadcasted_iota(jnp.int32, (points, points), 0)
        col = lax.broadcasted_iota(jnp.int32, (points, points), 1)
        ends = jnp.sum(jnp.where(col <= row, count_row, 0.0), axis=1, keepdims=True)
        count = jnp.sum(jnp.where(col == row, count_row, 0.0), axis=1, keepdims=True)
        slot = lax.broadcasted_iota(jnp.int32, (points, slots), 1).astype(F32)
        inside = jnp.logical_and(slot >= ends - count, slot < ends)
        member[...] = jnp.where(inside, 1.0 / count, 0.0).astype(BF16)

    means = jnp.dot(member[...], frames[...], preferred_element_type=F32).astype(BF16)
    for b in range(blocks):
        value = jnp.dot(
            means[:, b * LANES : (b + 1) * LANES], weights[b], preferred_element_type=F32
        )
        k = tile_bin[step * blocks + b]
        acc[k] += value[:, :tile_bins]
        acc[k + 1] += value[:, tile_bins:]

    @pl.when(step == pl.num_programs(0) - 1)
    def _():
        for e in range(nx):
            for j in range(per_chunk):
                lanes = slice(j * tile_bins, (j + 1) * tile_bins)
                send[e, :, lanes] = acc[place[2 * e] * per_chunk + j].astype(BF16)


def integrate(frames, counts, weights, tile_bin, place, after, nx, chans):
    slots, pixels = frames.shape
    points = counts.shape[0]
    nblocks, tile_pix, pair = weights.shape
    tile_bins = pair // 2
    blocks = 16 if nblocks % 16 == 0 else 1
    channel_blocks = 2 * nx * chans // tile_bins
    whole = lambda shape: pl.BlockSpec(shape, lambda i, *_: (0,) * len(shape))
    return pl.pallas_call(
        functools.partial(integrate_kernel, nx, chans // tile_bins),
        grid_spec=pltpu.PrefetchScalarGridSpec(
            num_scalar_prefetch=2,
            grid=(nblocks // blocks,),
            in_specs=[
                pl.BlockSpec(memory_space=pl.ANY),
                whole((1, points)),
                pl.BlockSpec((slots, blocks * tile_pix), lambda i, *_: (0, i)),
                pl.BlockSpec((blocks, tile_pix, pair), lambda i, *_: (i, 0, 0)),
            ],
            out_specs=[
                whole((nx, points, chans)),
                whole((channel_blocks, points, tile_bins)),
            ],
            scratch_shapes=[pltpu.VMEM((points, slots), BF16)],
        ),
        out_shape=[
            jax.ShapeDtypeStruct((nx, points, chans), BF16),
            jax.ShapeDtypeStruct((channel_blocks, points, tile_bins), F32),
        ],
        compiler_params=pltpu.CompilerParams(vmem_limit_bytes=24 * MIB),
        cost_estimate=SMALL,
        name="integrate",
    )(tile_bin, place, after, counts.reshape(1, points), frames, weights)


def select_kernel(place, acc, own, *rest):
    _, points, tile_bins = acc.shape
    per_chunk = own.shape[1] // tile_bins
    for e, keep in enumerate((own,) + rest):
        for j in range(per_chunk):
            lanes = slice(j * tile_bins, (j + 1) * tile_bins)
            keep[:, lanes] = acc[place[2 * e + 1] * per_chunk + j]


def select(place, acc, nx, chans):
    points = acc.shape[1]
    vmem = pl.BlockSpec(memory_space=pltpu.VMEM)
    return pl.pallas_call(
        select_kernel,
        in_specs=[pl.BlockSpec(memory_space=pltpu.SMEM), vmem],
        out_specs=[vmem] * nx,
        out_shape=[jax.ShapeDtypeStruct((points, chans), F32)] * nx,
        compiler_params=pltpu.CompilerParams(vmem_limit_bytes=8 * MIB),
        cost_estimate=LARGE,
        name="select",
    )(place, acc)


def row_groups(rows):
    sizes = [min(2, rows)]
    while sum(sizes) < rows:
        sizes.append(min(6, rows - sum(sizes)))
    return sizes


def project_kernel(angles, first_row, image, out, staged, base, tile_a, tile_b, total, arrived):
    cos_tab, sin_tab = angle_tables(angles)
    tiles = (tile_a, tile_b)
    sizes = row_groups(image.shape[0] // LANES)

    def cells(group):
        return slice(sum(sizes[:group]) * LANES, sum(sizes[: group + 1]) * LANES)

    def load(group):
        here = cells(group)
        return pltpu.make_async_copy(
            image.at[here, :], staged.at[here, :], arrived.at[group]
        )

    def fill(group):
        first = first_row[0] + sum(sizes[:group])
        for i in range(sizes[group]):
            upos = (first + i).astype(F32) - HALF
            lanes = slice(i * LANES, (i + 1) * LANES)
            for a in range(angles):
                here = slice(a * NIMG, (a + 1) * NIMG)
                tiles[group % 2][here, lanes] = hat(base[here, :] + upos * cos_tab[a])

    for group in range(min(2, len(sizes))):
        load(group).start()
    vpos = lax.broadcasted_iota(jnp.int32, (NIMG, LANES), 1).astype(F32) - HALF
    offset = lax.broadcasted_iota(jnp.int32, (NIMG, LANES), 0).astype(F32) - HALF
    for a in range(angles):
        base[a * NIMG : (a + 1) * NIMG, :] = sin_tab[a] * vpos - offset
    fill(0)
    for group, size in enumerate(sizes):
        if group + 1 < len(sizes):
            fill(group + 1)
        load(group).wait()
        if group + 2 < len(sizes):
            load(group + 2).start()
        product = jnp.dot(
            tiles[group % 2][:, : size * LANES],
            staged[cells(group), :].astype(BF16),
            preferred_element_type=F32,
        )
        if group == 0:
            total[...] = product
        elif group + 1 < len(sizes):
            total[...] += product
        else:
            out[...] = (total[...] + product).astype(out.dtype)


def project(image, first_row, angles):
    cells, chans = image.shape
    rays = angles * NIMG
    sizes = row_groups(cells // LANES)
    widest = max(sizes) * LANES
    vmem = pl.BlockSpec(memory_space=pltpu.VMEM)
    anywhere = pl.BlockSpec(memory_space=pl.ANY)
    return pl.pallas_call(
        functools.partial(project_kernel, angles),
        in_specs=[pl.BlockSpec(memory_space=pltpu.SMEM), anywhere],
        out_specs=vmem,
        scratch_shapes=[
            pltpu.VMEM((cells, chans), F32),
            pltpu.VMEM((rays, LANES), F32),
            pltpu.VMEM((rays, widest), BF16),
            pltpu.VMEM((rays, widest), BF16),
            pltpu.VMEM((rays, chans), F32),
            pltpu.SemaphoreType.DMA((len(sizes),)),
        ],
        out_shape=jax.ShapeDtypeStruct((rays, chans), BF16),
        compiler_params=pltpu.CompilerParams(vmem_limit_bytes=40 * MIB),
        cost_estimate=pl.CostEstimate(
            flops=4 * rays * cells * chans, bytes_accessed=4 * cells * chans, transcendentals=0
        ),
        name="project",
    )(first_row, pltpu.with_memory_space_constraint(image, pltpu.HBM))


def reorder_kernel(rays, rows, *refs):
    outs, hot = refs[:-1], refs[-1]
    all_rays = rows.shape[0]
    points = outs[0].shape[0]
    together = hot.shape[0]
    number = lax.broadcasted_iota(jnp.int32, (LANES, all_rays), 1)
    for start in range(0, len(outs) * points, together):
        for k in range(together // LANES):
            row = start // LANES + k
            wanted = jnp.transpose(jnp.broadcast_to(rays[row : row + 1, :], (LANES, LANES)))
            hot[k * LANES : (k + 1) * LANES, :] = (number == wanted[:, :1]).astype(F32).astype(BF16)
        picked = jnp.dot(hot[...], rows[...], preferred_element_type=F32).astype(BF16)
        for k in range(0, together, points):
            outs[(start + k) // points][...] = picked[k : k + points, :]


def reorder(rays, rows, parts):
    all_rays, chans = rows.shape
    points = rays.shape[0] * LANES // parts
    together = max(points, min(all_rays, MIB // all_rays))
    vmem = pl.BlockSpec(memory_space=pltpu.VMEM)
    return pl.pallas_call(
        reorder_kernel,
        in_specs=[vmem, vmem],
        out_specs=[vmem] * parts,
        scratch_shapes=[pltpu.VMEM((together, all_rays), BF16)],
        out_shape=[jax.ShapeDtypeStruct((points, chans), BF16)] * parts,
        compiler_params=pltpu.CompilerParams(vmem_limit_bytes=16 * MIB),
        cost_estimate=SMALL,
        name="reorder",
    )(rays, rows)


def row_total_kernel(angles, after, rays, row_total):
    cos_r, sin_r, off_r = ray_geometry(rays[...], angles)
    line = lax.broadcasted_iota(jnp.int32, (LANES, LANES), 0).astype(F32) - HALF
    for k in range(rays.shape[0]):
        cosine, sine, offset = (x[k : k + 1, :] for x in (cos_r, sin_r, off_r))
        along_u = jnp.abs(cosine) >= jnp.abs(sine)
        steep = jnp.where(along_u, cosine, sine)
        flat = jnp.where(along_u, sine, cosine)
        crossing = jnp.floor((offset - flat * line) / steep + HALF)
        sums = jnp.zeros((LANES, LANES), F32)
        for near in range(-1, 3):
            cell = crossing + float(near)
            weight = hat(flat * line + steep * (cell - HALF) - offset).astype(F32)
            inside = jnp.logical_and(cell >= 0.0, cell <= NIMG - 1.0)
            sums += jnp.where(inside, weight, 0.0)
        total = jnp.sum(sums, axis=0, keepdims=True)
        row_total[k * LANES : (k + 1) * LANES, :] = jnp.transpose(
            jnp.broadcast_to(total, (LANES, LANES))
        )


def row_totals(rays, after, angles):
    points = rays.shape[0] * LANES
    vmem = pl.BlockSpec(memory_space=pltpu.VMEM)
    return pl.pallas_call(
        functools.partial(row_total_kernel, angles),
        in_specs=[pl.BlockSpec(memory_space=pl.ANY), vmem],
        out_specs=vmem,
        out_shape=jax.ShapeDtypeStruct((points, LANES), F32),
        compiler_params=pltpu.CompilerParams(vmem_limit_bytes=8 * MIB),
        cost_estimate=SMALL,
        name="row_totals",
    )(after, rays)


def join_kernel(row_total, own, *refs):
    arrived, (scaled, recip) = refs[:-2], refs[-2:]
    total = own[...].astype(F32)
    for part in arrived:
        total += part[...].astype(F32)
    recip[...] = 1.0 / row_total[...]
    for j in range(own.shape[1] // LANES):
        lanes = slice(j * LANES, (j + 1) * LANES)
        scaled[:, lanes] = total[:, lanes] * recip[...]


def join(row_total, own, arrived):
    vmem = pl.BlockSpec(memory_space=pltpu.VMEM)
    return pl.pallas_call(
        join_kernel,
        in_specs=[vmem] * (2 + len(arrived)),
        out_specs=[vmem, vmem],
        out_shape=[
            jax.ShapeDtypeStruct(own.shape, F32),
            jax.ShapeDtypeStruct(row_total.shape, F32),
        ],
        compiler_params=pltpu.CompilerParams(vmem_limit_bytes=8 * MIB),
        cost_estimate=LARGE,
        name="join",
    )(row_total, own, *arrived)


def prepare_kernel(angles, early, first_row, rays, *refs):
    residuals, (image, tile, recip, partial, base, cosine) = refs[:early], refs[early:]
    step = pl.program_id(0)
    chunks = rays.shape[0]
    points, chans = residuals[0].shape
    rows = tile.shape[0] // LANES

    @pl.when(step == 0)
    def _():
        cos_c, sin_c, off_c = ray_geometry(rays[...], angles)
        cosine[...] = cos_c
        vpos = lax.broadcasted_iota(jnp.int32, (LANES, LANES), 0).astype(F32) - HALF
        for k in range(chunks):
            base[:, k * LANES : (k + 1) * LANES] = sin_c[k : k + 1, :] * vpos - off_c[k : k + 1, :]

    for i in range(rows):
        here = slice(i * LANES, (i + 1) * LANES)
        upos = (first_row[0] + step * rows + i).astype(F32) - HALF
        sums = jnp.zeros((LANES, LANES), F32)
        for k in range(chunks):
            lanes = slice(k * LANES, (k + 1) * LANES)
            value = hat(base[:, lanes] + cosine[k : k + 1, :] * upos)
            tile[here, lanes] = value
            sums += value.astype(F32)
        total = jnp.sum(sums, axis=1, keepdims=True)
        recip[here, :] = jnp.broadcast_to(1.0 / total, (LANES, LANES))
    joined = jnp.concatenate([r[...] for r in residuals], axis=0)
    back = jnp.dot(tile[:, : early * points], joined, preferred_element_type=F32)
    for j in range(chans // LANES):
        lanes = slice(j * LANES, (j + 1) * LANES)
        partial[:, lanes] = image[:, lanes] + back[:, lanes] * recip[...]


def prepare(rays, residuals, image, first_row, angles):
    cells, chans = image.shape
    all_points = rays.shape[0] * LANES
    rows = min(4, cells // LANES)
    fixed = lambda shape: pl.BlockSpec(shape, lambda i, *_: (0, 0))
    sliding = lambda width: pl.BlockSpec((rows * LANES, width), lambda i, *_: (i, 0))
    return pl.pallas_call(
        functools.partial(prepare_kernel, angles, len(residuals)),
        grid_spec=pltpu.PrefetchScalarGridSpec(
            num_scalar_prefetch=1,
            grid=(cells // (rows * LANES),),
            in_specs=[fixed(rays.shape)]
            + [fixed(r.shape) for r in residuals]
            + [sliding(chans)],
            out_specs=[sliding(all_points), sliding(LANES), sliding(chans)],
            scratch_shapes=[pltpu.VMEM((LANES, all_points), F32), pltpu.VMEM(rays.shape, F32)],
        ),
        out_shape=[
            jax.ShapeDtypeStruct((cells, all_points), BF16),
            jax.ShapeDtypeStruct((cells, LANES), F32),
            jax.ShapeDtypeStruct((cells, chans), F32),
        ],
        compiler_params=pltpu.CompilerParams(vmem_limit_bytes=16 * MIB),
        cost_estimate=SMALL,
        name="prepare",
    )(first_row, rays, *residuals, image)


def back_kernel(parts, *refs):
    residuals, (tile, recip, partial, out, joined, staged, sent) = refs[:parts], refs[parts:]
    points, chans = residuals[0].shape
    skip = tile.shape[1] - parts * points
    chunks = sent.shape[0]
    rows = out.shape[0] // chunks

    for d in range(parts):
        joined[d * points : (d + 1) * points, :] = residuals[d][...]
    copies = []
    for chunk in range(chunks):
        here = slice(chunk * rows, (chunk + 1) * rows)
        back = jnp.dot(tile[here, skip:], joined[...], preferred_element_type=F32)
        scale = recip[here, :]
        for j in range(chans // LANES):
            lanes = slice(j * LANES, (j + 1) * LANES)
            staged[here, lanes] = partial[here, lanes] + back[:, lanes] * scale
        copies.append(
            pltpu.make_async_copy(staged.at[here, :], out.at[here, :], sent.at[chunk])
        )
        copies[-1].start()
    for copy in copies:
        copy.wait()


def back_project(residuals, tile, recip, partial):
    cells, chans = partial.shape
    parts = len(residuals)
    points = residuals[0].shape[0]
    chunks = max(1, cells // 512)
    vmem = pl.BlockSpec(memory_space=pltpu.VMEM)
    return pl.pallas_call(
        functools.partial(back_kernel, parts),
        in_specs=[vmem] * (parts + 3),
        out_specs=pl.BlockSpec(memory_space=pl.ANY),
        scratch_shapes=[
            pltpu.VMEM((parts * points, chans), BF16),
            pltpu.VMEM((cells, chans), F32),
            pltpu.SemaphoreType.DMA((chunks,)),
        ],
        out_shape=jax.ShapeDtypeStruct((cells, chans), F32),
        compiler_params=pltpu.CompilerParams(vmem_limit_bytes=16 * MIB),
        cost_estimate=SMALL,
        name="back_project",
    )(*residuals, tile, recip, partial)


def rotate(x, axis, shift, n):
    return lax.ppermute(x, axis, [(i, (i + shift) % n) for i in range(n)])


def body(frames, counts, point_ray, channel_pair_weights, tile_bin, image):
    n_scan = lax.axis_size("scan")
    n_chan = lax.axis_size("chan")
    nx = n_chan // 2
    points = counts.shape[0]
    cells, chans = image.shape
    angles = points * n_scan // NIMG
    chan_me = lax.axis_index("chan")
    x_me, core_me = chan_me // 2, chan_me % 2
    first_row = (lax.axis_index("scan") * (cells // NIMG)).astype(jnp.int32).reshape(1)

    order = sorted(range(1, n_scan), key=lambda d: (2 * d != n_scan, d))
    own_rays = point_ray.reshape(points // LANES, LANES)
    rays = [own_rays] + [rotate(own_rays, "scan", -d, n_scan) for d in order]
    all_rays = jnp.concatenate(rays, axis=0)

    projected = project(image, first_row, angles)
    own_share, *shares = reorder(all_rays, projected, n_scan)
    arrived = [rotate(share, "scan", d, n_scan) for d, share in zip(order, shares)]

    place = []
    for e in range(nx):
        xi = (x_me + e) % nx
        place += [2 * xi + 1 - core_me, 2 * xi + core_me]
    place = jnp.stack(place).astype(jnp.int32)
    send, sums = integrate(
        frames, counts, channel_pair_weights, tile_bin, place, own_share, nx, chans
    )
    keep = select(place, sums, nx, chans)
    partner = [(i, i ^ 1) for i in range(n_chan)]
    got = lax.ppermute(send, "chan", partner)
    pattern = keep[0] + got[0].astype(F32)
    for e in range(1, nx):
        joined = (keep[e] + got[e].astype(F32)).astype(BF16)
        pattern = pattern + rotate(joined, "chan", 2 * e, n_chan).astype(F32)

    row_total = row_totals(own_rays, sums, angles)
    scaled, recip = join(row_total, own_share, arrived)
    residual = (pattern * (float(NIMG) * recip[:, :1]) - scaled).astype(BF16)
    others = [rotate(residual, "scan", -d, n_scan) for d in order]
    tile, col_recip, partial = prepare(all_rays, [residual], image, first_row, angles)
    return back_project(others, tile, col_recip, partial)


def solution(mesh):
    in_specs = (
        P(("grp", "scan"), "chan"),
        P(("grp", "scan")),
        P(("grp", "scan")),
        P("chan", None, None),
        P("chan"),
        P(("grp", "scan"), "chan"),
    )
    out_specs = P(("grp", "scan"), "chan")
    return jax.shard_map(body, mesh=mesh, in_specs=in_specs, out_specs=out_specs, check_vma=False)
```

```python
import functools
import math

import jax
import jax.numpy as jnp
import numpy as np
from jax import lax
from jax.experimental import pallas as pl
from jax.experimental.pallas import tpu as pltpu
from jax.sharding import PartitionSpec as P

NIMG = 128
HALF = (NIMG - 1) / 2.0
LANES = 128
MIB = 1024 * 1024
F32 = jnp.float32
BF16 = jnp.bfloat16
SMALL = pl.CostEstimate(flops=1, bytes_accessed=1, transcendentals=0)
LARGE = pl.CostEstimate(flops=10**11, bytes_accessed=10**8, transcendentals=0)


def angle_tables(angles):
    theta = np.arange(angles, dtype=np.float32) * np.float32(math.pi / angles)
    return [float(c) for c in np.cos(theta)], [float(s) for s in np.sin(theta)]


def ray_geometry(rays, angles):
    cos_tab, sin_tab = angle_tables(angles)
    which = rays // NIMG
    offset = (rays - which * NIMG).astype(F32) - HALF
    cosine = jnp.zeros(rays.shape, F32)
    sine = jnp.zeros(rays.shape, F32)
    for a in range(angles):
        here = which == a
        cosine = jnp.where(here, cos_tab[a], cosine)
        sine = jnp.where(here, sin_tab[a], sine)
    return cosine, sine, offset


def hat(distance):
    return jnp.maximum((1.0 - jnp.abs(distance)).astype(BF16), jnp.zeros((), BF16))


def integrate_kernel(
    nx, per_chunk, tile_bin, place, after, counts, frames, weights, send, acc, member
):
    step = pl.program_id(0)
    points, slots = member.shape
    blocks = weights.shape[0]
    tile_bins = acc.shape[2]

    @pl.when(step == 0)
    def _():
        acc[...] = jnp.zeros_like(acc)
        count_row = counts[...].astype(F32)
        row = lax.broadcasted_iota(jnp.int32, (points, points), 0)
        col = lax.broadcasted_iota(jnp.int32, (points, points), 1)
        ends = jnp.sum(jnp.where(col <= row, count_row, 0.0), axis=1, keepdims=True)
        count = jnp.sum(jnp.where(col == row, count_row, 0.0), axis=1, keepdims=True)
        slot = lax.broadcasted_iota(jnp.int32, (points, slots), 1).astype(F32)
        inside = jnp.logical_and(slot >= ends - count, slot < ends)
        member[...] = jnp.where(inside, 1.0 / count, 0.0).astype(BF16)

    means = jnp.dot(member[...], frames[...], preferred_element_type=F32).astype(BF16)
    for b in range(blocks):
        value = jnp.dot(
            means[:, b * LANES : (b + 1) * LANES], weights[b], preferred_element_type=F32
        )
        k = tile_bin[step * blocks + b]
        acc[k] += value[:, :tile_bins]
        acc[k + 1] += value[:, tile_bins:]

    @pl.when(step == pl.num_programs(0) - 1)
    def _():
        for e in range(nx):
            for j in range(per_chunk):
                lanes = slice(j * tile_bins, (j + 1) * tile_bins)
                send[e, :, lanes] = acc[place[2 * e] * per_chunk + j].astype(BF16)


def integrate(frames, counts, weights, tile_bin, place, after, nx, chans):
    slots, pixels = frames.shape
    points = counts.shape[0]
    nblocks, tile_pix, pair = weights.shape
    tile_bins = pair // 2
    blocks = 16 if nblocks % 16 == 0 else 1
    channel_blocks = 2 * nx * chans // tile_bins
    whole = lambda shape: pl.BlockSpec(shape, lambda i, *_: (0,) * len(shape))
    return pl.pallas_call(
        functools.partial(integrate_kernel, nx, chans // tile_bins),
        grid_spec=pltpu.PrefetchScalarGridSpec(
            num_scalar_prefetch=2,
            grid=(nblocks // blocks,),
            in_specs=[
                pl.BlockSpec(memory_space=pl.ANY),
                whole((1, points)),
                pl.BlockSpec((slots, blocks * tile_pix), lambda i, *_: (0, i)),
                pl.BlockSpec((blocks, tile_pix, pair), lambda i, *_: (i, 0, 0)),
            ],
            out_specs=[
                whole((nx, points, chans)),
                whole((channel_blocks, points, tile_bins)),
            ],
            scratch_shapes=[pltpu.VMEM((points, slots), BF16)],
        ),
        out_shape=[
            jax.ShapeDtypeStruct((nx, points, chans), BF16),
            jax.ShapeDtypeStruct((channel_blocks, points, tile_bins), F32),
        ],
        compiler_params=pltpu.CompilerParams(vmem_limit_bytes=24 * MIB),
        cost_estimate=SMALL,
        name="integrate",
    )(
        tile_bin,
        place,
        after,
        counts.reshape(1, points),
        pltpu.with_memory_space_constraint(frames, pltpu.HBM),
        pltpu.with_memory_space_constraint(weights, pltpu.HBM),
    )


def select_kernel(place, acc, own, *rest):
    _, points, tile_bins = acc.shape
    per_chunk = own.shape[1] // tile_bins
    for e, keep in enumerate((own,) + rest):
        for j in range(per_chunk):
            lanes = slice(j * tile_bins, (j + 1) * tile_bins)
            keep[:, lanes] = acc[place[2 * e + 1] * per_chunk + j]


def select(place, acc, nx, chans):
    points = acc.shape[1]
    vmem = pl.BlockSpec(memory_space=pltpu.VMEM)
    return pl.pallas_call(
        select_kernel,
        in_specs=[pl.BlockSpec(memory_space=pltpu.SMEM), vmem],
        out_specs=[vmem] * nx,
        out_shape=[jax.ShapeDtypeStruct((points, chans), F32)] * nx,
        compiler_params=pltpu.CompilerParams(vmem_limit_bytes=8 * MIB),
        cost_estimate=LARGE,
        name="select",
    )(place, acc)


def row_groups(rows):
    sizes = [min(2, rows)]
    while sum(sizes) < rows:
        sizes.append(min(6, rows - sum(sizes)))
    return sizes


def project_kernel(angles, first_row, image, out, staged, base, tile_a, tile_b, total, arrived):
    cos_tab, sin_tab = angle_tables(angles)
    tiles = (tile_a, tile_b)
    sizes = row_groups(image.shape[0] // LANES)

    def cells(group):
        return slice(sum(sizes[:group]) * LANES, sum(sizes[: group + 1]) * LANES)

    def load(group):
        here = cells(group)
        return pltpu.make_async_copy(
            image.at[here, :], staged.at[here, :], arrived.at[group]
        )

    def fill(group):
        first = first_row[0] + sum(sizes[:group])
        for i in range(sizes[group]):
            upos = (first + i).astype(F32) - HALF
            lanes = slice(i * LANES, (i + 1) * LANES)
            for a in range(angles):
                here = slice(a * NIMG, (a + 1) * NIMG)
                tiles[group % 2][here, lanes] = hat(base[here, :] + upos * cos_tab[a])

    for group in range(min(2, len(sizes))):
        load(group).start()
    vpos = lax.broadcasted_iota(jnp.int32, (NIMG, LANES), 1).astype(F32) - HALF
    offset = lax.broadcasted_iota(jnp.int32, (NIMG, LANES), 0).astype(F32) - HALF
    for a in range(angles):
        base[a * NIMG : (a + 1) * NIMG, :] = sin_tab[a] * vpos - offset
    fill(0)
    for group, size in enumerate(sizes):
        if group + 1 < len(sizes):
            fill(group + 1)
        load(group).wait()
        if group + 2 < len(sizes):
            load(group + 2).start()
        product = jnp.dot(
            tiles[group % 2][:, : size * LANES],
            staged[cells(group), :].astype(BF16),
            preferred_element_type=F32,
        )
        if group == 0:
            total[...] = product
        elif group + 1 < len(sizes):
            total[...] += product
        else:
            out[...] = (total[...] + product).astype(out.dtype)


def project(image, first_row, angles):
    cells, chans = image.shape
    rays = angles * NIMG
    sizes = row_groups(cells // LANES)
    widest = max(sizes) * LANES
    vmem = pl.BlockSpec(memory_space=pltpu.VMEM)
    anywhere = pl.BlockSpec(memory_space=pl.ANY)
    return pl.pallas_call(
        functools.partial(project_kernel, angles),
        in_specs=[pl.BlockSpec(memory_space=pltpu.SMEM), anywhere],
        out_specs=vmem,
        scratch_shapes=[
            pltpu.VMEM((cells, chans), F32),
            pltpu.VMEM((rays, LANES), F32),
            pltpu.VMEM((rays, widest), BF16),
            pltpu.VMEM((rays, widest), BF16),
            pltpu.VMEM((rays, chans), F32),
            pltpu.SemaphoreType.DMA((len(sizes),)),
        ],
        out_shape=jax.ShapeDtypeStruct((rays, chans), BF16),
        compiler_params=pltpu.CompilerParams(vmem_limit_bytes=40 * MIB),
        cost_estimate=pl.CostEstimate(
            flops=4 * rays * cells * chans, bytes_accessed=4 * cells * chans, transcendentals=0
        ),
        name="project",
    )(first_row, pltpu.with_memory_space_constraint(image, pltpu.HBM))


def reorder_kernel(rays, rows, *refs):
    outs, hot = refs[:-1], refs[-1]
    all_rays = rows.shape[0]
    points = outs[0].shape[0]
    together = hot.shape[0]
    number = lax.broadcasted_iota(jnp.int32, (LANES, all_rays), 1)
    for start in range(0, len(outs) * points, together):
        for k in range(together // LANES):
            row = start // LANES + k
            wanted = jnp.transpose(jnp.broadcast_to(rays[row : row + 1, :], (LANES, LANES)))
            hot[k * LANES : (k + 1) * LANES, :] = (number == wanted[:, :1]).astype(F32).astype(BF16)
        picked = jnp.dot(hot[...], rows[...], preferred_element_type=F32).astype(BF16)
        for k in range(0, together, points):
            outs[(start + k) // points][...] = picked[k : k + points, :]


def reorder(rays, rows, parts):
    all_rays, chans = rows.shape
    points = rays.shape[0] * LANES // parts
    together = max(points, min(all_rays, MIB // all_rays))
    vmem = pl.BlockSpec(memory_space=pltpu.VMEM)
    return pl.pallas_call(
        reorder_kernel,
        in_specs=[vmem, vmem],
        out_specs=[vmem] * parts,
        scratch_shapes=[pltpu.VMEM((together, all_rays), BF16)],
        out_shape=[jax.ShapeDtypeStruct((points, chans), BF16)] * parts,
        compiler_params=pltpu.CompilerParams(vmem_limit_bytes=16 * MIB),
        cost_estimate=SMALL,
        name="reorder",
    )(rays, rows)


def row_total_kernel(angles, after, rays, row_total):
    cos_r, sin_r, off_r = ray_geometry(rays[...], angles)
    line = lax.broadcasted_iota(jnp.int32, (LANES, LANES), 0).astype(F32) - HALF
    for k in range(rays.shape[0]):
        cosine, sine, offset = (x[k : k + 1, :] for x in (cos_r, sin_r, off_r))
        along_u = jnp.abs(cosine) >= jnp.abs(sine)
        steep = jnp.where(along_u, cosine, sine)
        flat = jnp.where(along_u, sine, cosine)
        crossing = jnp.floor((offset - flat * line) / steep + HALF)
        sums = jnp.zeros((LANES, LANES), F32)
        for near in range(-1, 3):
            cell = crossing + float(near)
            weight = hat(flat * line + steep * (cell - HALF) - offset).astype(F32)
            inside = jnp.logical_and(cell >= 0.0, cell <= NIMG - 1.0)
            sums += jnp.where(inside, weight, 0.0)
        total = jnp.sum(sums, axis=0, keepdims=True)
        row_total[k * LANES : (k + 1) * LANES, :] = jnp.transpose(
            jnp.broadcast_to(total, (LANES, LANES))
        )


def row_totals(rays, after, angles):
    points = rays.shape[0] * LANES
    vmem = pl.BlockSpec(memory_space=pltpu.VMEM)
    return pl.pallas_call(
        functools.partial(row_total_kernel, angles),
        in_specs=[pl.BlockSpec(memory_space=pl.ANY), vmem],
        out_specs=vmem,
        out_shape=jax.ShapeDtypeStruct((points, LANES), F32),
        compiler_params=pltpu.CompilerParams(vmem_limit_bytes=8 * MIB),
        cost_estimate=SMALL,
        name="row_totals",
    )(after, rays)


def join_kernel(row_total, own, *refs):
    arrived, (scaled, recip) = refs[:-2], refs[-2:]
    total = own[...].astype(F32)
    for part in arrived:
        total += part[...].astype(F32)
    recip[...] = 1.0 / row_total[...]
    for j in range(own.shape[1] // LANES):
        lanes = slice(j * LANES, (j + 1) * LANES)
        scaled[:, lanes] = total[:, lanes] * recip[...]


def join(row_total, own, arrived):
    vmem = pl.BlockSpec(memory_space=pltpu.VMEM)
    return pl.pallas_call(
        join_kernel,
        in_specs=[vmem] * (2 + len(arrived)),
        out_specs=[vmem, vmem],
        out_shape=[
            jax.ShapeDtypeStruct(own.shape, F32),
            jax.ShapeDtypeStruct(row_total.shape, F32),
        ],
        compiler_params=pltpu.CompilerParams(vmem_limit_bytes=8 * MIB),
        cost_estimate=LARGE,
        name="join",
    )(row_total, own, *arrived)


def prepare_kernel(angles, early, first_row, rays, *refs):
    residuals, (image, tile, recip, partial, base, cosine) = refs[:early], refs[early:]
    step = pl.program_id(0)
    chunks = rays.shape[0]
    points, chans = residuals[0].shape
    rows = tile.shape[0] // LANES

    @pl.when(step == 0)
    def _():
        cos_c, sin_c, off_c = ray_geometry(rays[...], angles)
        cosine[...] = cos_c
        vpos = lax.broadcasted_iota(jnp.int32, (LANES, LANES), 0).astype(F32) - HALF
        for k in range(chunks):
            base[:, k * LANES : (k + 1) * LANES] = sin_c[k : k + 1, :] * vpos - off_c[k : k + 1, :]

    for i in range(rows):
        here = slice(i * LANES, (i + 1) * LANES)
        upos = (first_row[0] + step * rows + i).astype(F32) - HALF
        sums = jnp.zeros((LANES, LANES), F32)
        for k in range(chunks):
            lanes = slice(k * LANES, (k + 1) * LANES)
            value = hat(base[:, lanes] + cosine[k : k + 1, :] * upos)
            tile[here, lanes] = value
            sums += value.astype(F32)
        total = jnp.sum(sums, axis=1, keepdims=True)
        recip[here, :] = jnp.broadcast_to(1.0 / total, (LANES, LANES))
    joined = jnp.concatenate([r[...] for r in residuals], axis=0)
    back = jnp.dot(tile[:, : early * points], joined, preferred_element_type=F32)
    for j in range(chans // LANES):
        lanes = slice(j * LANES, (j + 1) * LANES)
        partial[:, lanes] = image[:, lanes] + back[:, lanes] * recip[...]


def prepare(rays, residuals, image, first_row, angles):
    cells, chans = image.shape
    all_points = rays.shape[0] * LANES
    rows = min(4, cells // LANES)
    fixed = lambda shape: pl.BlockSpec(shape, lambda i, *_: (0, 0))
    sliding = lambda width: pl.BlockSpec((rows * LANES, width), lambda i, *_: (i, 0))
    return pl.pallas_call(
        functools.partial(prepare_kernel, angles, len(residuals)),
        grid_spec=pltpu.PrefetchScalarGridSpec(
            num_scalar_prefetch=1,
            grid=(cells // (rows * LANES),),
            in_specs=[fixed(rays.shape)]
            + [fixed(r.shape) for r in residuals]
            + [sliding(chans)],
            out_specs=[sliding(all_points), sliding(LANES), sliding(chans)],
            scratch_shapes=[pltpu.VMEM((LANES, all_points), F32), pltpu.VMEM(rays.shape, F32)],
        ),
        out_shape=[
            jax.ShapeDtypeStruct((cells, all_points), BF16),
            jax.ShapeDtypeStruct((cells, LANES), F32),
            jax.ShapeDtypeStruct((cells, chans), F32),
        ],
        compiler_params=pltpu.CompilerParams(vmem_limit_bytes=16 * MIB),
        cost_estimate=SMALL,
        name="prepare",
    )(first_row, rays, *residuals, image)


def back_kernel(parts, *refs):
    residuals, (tile, recip, partial, out, joined, staged, sent) = refs[:parts], refs[parts:]
    points, chans = residuals[0].shape
    skip = tile.shape[1] - parts * points
    chunks = sent.shape[0]
    rows = out.shape[0] // chunks

    for d in range(parts):
        joined[d * points : (d + 1) * points, :] = residuals[d][...]
    copies = []
    for chunk in range(chunks):
        here = slice(chunk * rows, (chunk + 1) * rows)
        back = jnp.dot(tile[here, skip:], joined[...], preferred_element_type=F32)
        scale = recip[here, :]
        for j in range(chans // LANES):
            lanes = slice(j * LANES, (j + 1) * LANES)
            staged[here, lanes] = partial[here, lanes] + back[:, lanes] * scale
        copies.append(
            pltpu.make_async_copy(staged.at[here, :], out.at[here, :], sent.at[chunk])
        )
        copies[-1].start()
    for copy in copies:
        copy.wait()


def back_project(residuals, tile, recip, partial):
    cells, chans = partial.shape
    parts = len(residuals)
    points = residuals[0].shape[0]
    chunks = max(1, cells // 512)
    vmem = pl.BlockSpec(memory_space=pltpu.VMEM)
    return pl.pallas_call(
        functools.partial(back_kernel, parts),
        in_specs=[vmem] * (parts + 3),
        out_specs=pl.BlockSpec(memory_space=pl.ANY),
        scratch_shapes=[
            pltpu.VMEM((parts * points, chans), BF16),
            pltpu.VMEM((cells, chans), F32),
            pltpu.SemaphoreType.DMA((chunks,)),
        ],
        out_shape=jax.ShapeDtypeStruct((cells, chans), F32),
        compiler_params=pltpu.CompilerParams(vmem_limit_bytes=16 * MIB),
        cost_estimate=SMALL,
        name="back_project",
    )(*residuals, tile, recip, partial)


def rotate(x, axis, shift, n):
    return lax.ppermute(x, axis, [(i, (i + shift) % n) for i in range(n)])


def swap(x, axis, mask, n):
    return lax.ppermute(x, axis, [(i, i ^ mask) for i in range(n)])


def body(frames, counts, point_ray, channel_pair_weights, tile_bin, image):
    n_scan = lax.axis_size("scan")
    n_chan = lax.axis_size("chan")
    nx = n_chan // 2
    points = counts.shape[0]
    cells, chans = image.shape
    angles = points * n_scan // NIMG
    chan_me = lax.axis_index("chan")
    x_me, core_me = chan_me // 2, chan_me % 2
    first_row = (lax.axis_index("scan") * (cells // NIMG)).astype(jnp.int32).reshape(1)

    order = sorted(range(n_scan), key=lambda r: (r != 0, 2 * r != n_scan, r))
    own_rays = point_ray.reshape(points // LANES, LANES)
    rays = [own_rays] + [swap(own_rays, "scan", r, n_scan) for r in order[1:]]
    all_rays = jnp.concatenate(rays, axis=0)

    projected = project(image, first_row, angles)
    own_share, *shares = reorder(all_rays, projected, n_scan)
    arrived = [swap(share, "scan", r, n_scan) for r, share in zip(order[1:], shares)]

    place = []
    for e in range(nx):
        xi = (x_me + e) % nx
        place += [2 * xi + 1 - core_me, 2 * xi + core_me]
    place = jnp.stack(place).astype(jnp.int32)
    send, sums = integrate(
        frames, counts, channel_pair_weights, tile_bin, place, own_share, nx, chans
    )
    keep = select(place, sums, nx, chans)
    got = swap(send, "chan", 1, n_chan)
    pattern = keep[0] + got[0].astype(F32)
    for e in range(1, nx):
        joined = (keep[e] + got[e].astype(F32)).astype(BF16)
        pattern = pattern + rotate(joined, "chan", 2 * e, n_chan).astype(F32)

    row_total = row_totals(own_rays, sums, angles)
    scaled, recip = join(row_total, own_share, arrived)
    residual = (pattern * (float(NIMG) * recip[:, :1]) - scaled).astype(BF16)
    gathered = {0: residual}
    bit = n_scan // 2
    while bit:
        gathered |= {r ^ bit: swap(x, "scan", bit, n_scan) for r, x in gathered.items()}
        bit //= 2
    blocks = [gathered[r] for r in order]
    tile, col_recip, partial = prepare(all_rays, blocks[:2], image, first_row, angles)
    return back_project(blocks[2:], tile, col_recip, partial)


def solution(mesh):
    in_specs = (
        P(("grp", "scan"), "chan"),
        P(("grp", "scan")),
        P(("grp", "scan")),
        P("chan", None, None),
        P("chan"),
        P(("grp", "scan"), "chan"),
    )
    out_specs = P(("grp", "scan"), "chan")
    return jax.shard_map(body, mesh=mesh, in_specs=in_specs, out_specs=out_specs, check_vma=False)
```

```python
import functools
import math

import jax
import jax.numpy as jnp
import numpy as np
from jax import lax
from jax.experimental import pallas as pl
from jax.experimental.pallas import tpu as pltpu
from jax.sharding import PartitionSpec as P

NIMG = 128
HALF = (NIMG - 1) / 2.0
LANES = 128
MIB = 1024 * 1024
F32 = jnp.float32
BF16 = jnp.bfloat16
SMALL = pl.CostEstimate(flops=1, bytes_accessed=1, transcendentals=0)
LARGE = pl.CostEstimate(flops=10**11, bytes_accessed=10**8, transcendentals=0)


def angle_tables(angles):
    theta = np.arange(angles, dtype=np.float32) * np.float32(math.pi / angles)
    return [float(c) for c in np.cos(theta)], [float(s) for s in np.sin(theta)]


def ray_geometry(rays, angles):
    cos_tab, sin_tab = angle_tables(angles)
    which = rays // NIMG
    offset = (rays - which * NIMG).astype(F32) - HALF
    cosine = jnp.zeros(rays.shape, F32)
    sine = jnp.zeros(rays.shape, F32)
    for a in range(angles):
        here = which == a
        cosine = jnp.where(here, cos_tab[a], cosine)
        sine = jnp.where(here, sin_tab[a], sine)
    return cosine, sine, offset


def hat(distance):
    return jnp.maximum((1.0 - jnp.abs(distance)).astype(BF16), jnp.zeros((), BF16))


def integrate_kernel(
    nx, per_chunk, tile_bin, place, after, counts, frames, weights, send, acc, member
):
    step = pl.program_id(0)
    points, slots = member.shape
    blocks = weights.shape[0]
    tile_bins = acc.shape[2]

    @pl.when(step == 0)
    def _():
        acc[...] = jnp.zeros_like(acc)
        count_row = counts[...].astype(F32)
        row = lax.broadcasted_iota(jnp.int32, (points, points), 0)
        col = lax.broadcasted_iota(jnp.int32, (points, points), 1)
        ends = jnp.sum(jnp.where(col <= row, count_row, 0.0), axis=1, keepdims=True)
        count = jnp.sum(jnp.where(col == row, count_row, 0.0), axis=1, keepdims=True)
        slot = lax.broadcasted_iota(jnp.int32, (points, slots), 1).astype(F32)
        inside = jnp.logical_and(slot >= ends - count, slot < ends)
        member[...] = jnp.where(inside, 1.0 / count, 0.0).astype(BF16)

    means = jnp.dot(member[...], frames[...], preferred_element_type=F32).astype(BF16)
    for b in range(blocks):
        value = jnp.dot(
            means[:, b * LANES : (b + 1) * LANES], weights[b], preferred_element_type=F32
        )
        k = tile_bin[step * blocks + b]
        acc[k] += value[:, :tile_bins]
        acc[k + 1] += value[:, tile_bins:]

    @pl.when(step == pl.num_programs(0) - 1)
    def _():
        for e in range(nx):
            for j in range(per_chunk):
                lanes = slice(j * tile_bins, (j + 1) * tile_bins)
                send[e, :, lanes] = acc[place[2 * e] * per_chunk + j].astype(BF16)


def integrate(frames, counts, weights, tile_bin, place, after, nx, chans):
    slots, pixels = frames.shape
    points = counts.shape[0]
    nblocks, tile_pix, pair = weights.shape
    tile_bins = pair // 2
    blocks = 16 if nblocks % 16 == 0 else 1
    channel_blocks = 2 * nx * chans // tile_bins
    whole = lambda shape: pl.BlockSpec(shape, lambda i, *_: (0,) * len(shape))
    return pl.pallas_call(
        functools.partial(integrate_kernel, nx, chans // tile_bins),
        grid_spec=pltpu.PrefetchScalarGridSpec(
            num_scalar_prefetch=2,
            grid=(nblocks // blocks,),
            in_specs=[
                pl.BlockSpec(memory_space=pl.ANY),
                whole((1, points)),
                pl.BlockSpec((slots, blocks * tile_pix), lambda i, *_: (0, i)),
                pl.BlockSpec((blocks, tile_pix, pair), lambda i, *_: (i, 0, 0)),
            ],
            out_specs=[
                whole((nx, points, chans)),
                whole((channel_blocks, points, tile_bins)),
            ],
            scratch_shapes=[pltpu.VMEM((points, slots), BF16)],
        ),
        out_shape=[
            jax.ShapeDtypeStruct((nx, points, chans), BF16),
            jax.ShapeDtypeStruct((channel_blocks, points, tile_bins), F32),
        ],
        compiler_params=pltpu.CompilerParams(vmem_limit_bytes=24 * MIB),
        cost_estimate=SMALL,
        name="integrate",
    )(
        tile_bin,
        place,
        after,
        counts.reshape(1, points),
        pltpu.with_memory_space_constraint(frames, pltpu.HBM),
        pltpu.with_memory_space_constraint(weights, pltpu.HBM),
    )


def select_kernel(place, acc, own, *rest):
    _, points, tile_bins = acc.shape
    per_chunk = own.shape[1] // tile_bins
    for e, keep in enumerate((own,) + rest):
        for j in range(per_chunk):
            lanes = slice(j * tile_bins, (j + 1) * tile_bins)
            keep[:, lanes] = acc[place[2 * e + 1] * per_chunk + j]


def select(place, acc, nx, chans):
    points = acc.shape[1]
    vmem = pl.BlockSpec(memory_space=pltpu.VMEM)
    return pl.pallas_call(
        select_kernel,
        in_specs=[pl.BlockSpec(memory_space=pltpu.SMEM), vmem],
        out_specs=[vmem] * nx,
        out_shape=[jax.ShapeDtypeStruct((points, chans), F32)] * nx,
        compiler_params=pltpu.CompilerParams(vmem_limit_bytes=8 * MIB),
        cost_estimate=LARGE,
        name="select",
    )(place, acc)


def row_groups(rows):
    sizes = [min(2, rows)]
    while sum(sizes) < rows:
        sizes.append(min(6, rows - sum(sizes)))
    return sizes


def project_kernel(angles, first_row, image, out, staged, base, tile_a, tile_b, total, arrived):
    cos_tab, sin_tab = angle_tables(angles)
    tiles = (tile_a, tile_b)
    sizes = row_groups(image.shape[0] // LANES)

    def cells(group):
        return slice(sum(sizes[:group]) * LANES, sum(sizes[: group + 1]) * LANES)

    def load(group):
        here = cells(group)
        return pltpu.make_async_copy(
            image.at[here, :], staged.at[here, :], arrived.at[group]
        )

    def fill(group):
        first = first_row[0] + sum(sizes[:group])
        for i in range(sizes[group]):
            upos = (first + i).astype(F32) - HALF
            lanes = slice(i * LANES, (i + 1) * LANES)
            for a in range(angles):
                here = slice(a * NIMG, (a + 1) * NIMG)
                tiles[group % 2][here, lanes] = hat(base[here, :] + upos * cos_tab[a])

    for group in range(min(2, len(sizes))):
        load(group).start()
    vpos = lax.broadcasted_iota(jnp.int32, (NIMG, LANES), 1).astype(F32) - HALF
    offset = lax.broadcasted_iota(jnp.int32, (NIMG, LANES), 0).astype(F32) - HALF
    for a in range(angles):
        base[a * NIMG : (a + 1) * NIMG, :] = sin_tab[a] * vpos - offset
    fill(0)
    for group, size in enumerate(sizes):
        if group + 1 < len(sizes):
            fill(group + 1)
        load(group).wait()
        if group + 2 < len(sizes):
            load(group + 2).start()
        product = jnp.dot(
            tiles[group % 2][:, : size * LANES],
            staged[cells(group), :].astype(BF16),
            preferred_element_type=F32,
        )
        if group == 0:
            total[...] = product
        elif group + 1 < len(sizes):
            total[...] += product
        else:
            out[...] = (total[...] + product).astype(out.dtype)


def project(image, first_row, angles):
    cells, chans = image.shape
    rays = angles * NIMG
    sizes = row_groups(cells // LANES)
    widest = max(sizes) * LANES
    vmem = pl.BlockSpec(memory_space=pltpu.VMEM)
    anywhere = pl.BlockSpec(memory_space=pl.ANY)
    return pl.pallas_call(
        functools.partial(project_kernel, angles),
        in_specs=[pl.BlockSpec(memory_space=pltpu.SMEM), anywhere],
        out_specs=vmem,
        scratch_shapes=[
            pltpu.VMEM((cells, chans), F32),
            pltpu.VMEM((rays, LANES), F32),
            pltpu.VMEM((rays, widest), BF16),
            pltpu.VMEM((rays, widest), BF16),
            pltpu.VMEM((rays, chans), F32),
            pltpu.SemaphoreType.DMA((len(sizes),)),
        ],
        out_shape=jax.ShapeDtypeStruct((rays, chans), BF16),
        compiler_params=pltpu.CompilerParams(vmem_limit_bytes=40 * MIB),
        cost_estimate=pl.CostEstimate(
            flops=4 * rays * cells * chans, bytes_accessed=4 * cells * chans, transcendentals=0
        ),
        name="project",
    )(first_row, pltpu.with_memory_space_constraint(image, pltpu.HBM))


def reorder_kernel(rays, rows, *refs):
    outs, hot = refs[:-1], refs[-1]
    all_rays = rows.shape[0]
    points = outs[0].shape[0]
    together = hot.shape[0]
    number = lax.broadcasted_iota(jnp.int32, (LANES, all_rays), 1)
    for start in range(0, len(outs) * points, together):
        for k in range(together // LANES):
            row = start // LANES + k
            wanted = jnp.transpose(jnp.broadcast_to(rays[row : row + 1, :], (LANES, LANES)))
            hot[k * LANES : (k + 1) * LANES, :] = (number == wanted[:, :1]).astype(F32).astype(BF16)
        picked = jnp.dot(hot[...], rows[...], preferred_element_type=F32).astype(BF16)
        for k in range(0, together, points):
            outs[(start + k) // points][...] = picked[k : k + points, :]


def reorder(rays, rows, parts):
    all_rays, chans = rows.shape
    points = rays.shape[0] * LANES // parts
    together = max(points, min(all_rays, MIB // all_rays))
    vmem = pl.BlockSpec(memory_space=pltpu.VMEM)
    return pl.pallas_call(
        reorder_kernel,
        in_specs=[vmem, vmem],
        out_specs=[vmem] * parts,
        scratch_shapes=[pltpu.VMEM((together, all_rays), BF16)],
        out_shape=[jax.ShapeDtypeStruct((points, chans), BF16)] * parts,
        compiler_params=pltpu.CompilerParams(vmem_limit_bytes=16 * MIB),
        cost_estimate=SMALL,
        name="reorder",
    )(rays, rows)


def row_total_kernel(angles, after, rays, row_total):
    cos_r, sin_r, off_r = ray_geometry(rays[...], angles)
    line = lax.broadcasted_iota(jnp.int32, (LANES, LANES), 0).astype(F32) - HALF
    for k in range(rays.shape[0]):
        cosine, sine, offset = (x[k : k + 1, :] for x in (cos_r, sin_r, off_r))
        along_u = jnp.abs(cosine) >= jnp.abs(sine)
        steep = jnp.where(along_u, cosine, sine)
        flat = jnp.where(along_u, sine, cosine)
        crossing = jnp.floor((offset - flat * line) / steep + HALF)
        sums = jnp.zeros((LANES, LANES), F32)
        for near in range(-1, 3):
            cell = crossing + float(near)
            weight = hat(flat * line + steep * (cell - HALF) - offset).astype(F32)
            inside = jnp.logical_and(cell >= 0.0, cell <= NIMG - 1.0)
            sums += jnp.where(inside, weight, 0.0)
        total = jnp.sum(sums, axis=0, keepdims=True)
        row_total[k * LANES : (k + 1) * LANES, :] = jnp.transpose(
            jnp.broadcast_to(total, (LANES, LANES))
        )


def row_totals(rays, after, angles):
    points = rays.shape[0] * LANES
    vmem = pl.BlockSpec(memory_space=pltpu.VMEM)
    return pl.pallas_call(
        functools.partial(row_total_kernel, angles),
        in_specs=[pl.BlockSpec(memory_space=pl.ANY), vmem],
        out_specs=vmem,
        out_shape=jax.ShapeDtypeStruct((points, LANES), F32),
        compiler_params=pltpu.CompilerParams(vmem_limit_bytes=8 * MIB),
        cost_estimate=SMALL,
        name="row_totals",
    )(after, rays)


def join_kernel(row_total, own, *refs):
    arrived, (scaled, recip) = refs[:-2], refs[-2:]
    total = own[...].astype(F32)
    for part in arrived:
        total += part[...].astype(F32)
    recip[...] = 1.0 / row_total[...]
    for j in range(own.shape[1] // LANES):
        lanes = slice(j * LANES, (j + 1) * LANES)
        scaled[:, lanes] = total[:, lanes] * recip[...]


def join(row_total, own, arrived):
    vmem = pl.BlockSpec(memory_space=pltpu.VMEM)
    return pl.pallas_call(
        join_kernel,
        in_specs=[vmem] * (2 + len(arrived)),
        out_specs=[vmem, vmem],
        out_shape=[
            jax.ShapeDtypeStruct(own.shape, F32),
            jax.ShapeDtypeStruct(row_total.shape, F32),
        ],
        compiler_params=pltpu.CompilerParams(vmem_limit_bytes=8 * MIB),
        cost_estimate=LARGE,
        name="join",
    )(row_total, own, *arrived)


def prepare_kernel(angles, early, first_row, rays, *refs):
    residuals, (image, tile, recip, partial, base, cosine) = refs[:early], refs[early:]
    step = pl.program_id(0)
    chunks = rays.shape[0]
    chans = image.shape[1]
    rows = tile.shape[0] // LANES

    @pl.when(step == 0)
    def _():
        cos_c, sin_c, off_c = ray_geometry(rays[...], angles)
        cosine[...] = cos_c
        vpos = lax.broadcasted_iota(jnp.int32, (LANES, LANES), 0).astype(F32) - HALF
        for k in range(chunks):
            base[:, k * LANES : (k + 1) * LANES] = sin_c[k : k + 1, :] * vpos - off_c[k : k + 1, :]

    for i in range(rows):
        here = slice(i * LANES, (i + 1) * LANES)
        upos = (first_row[0] + step * rows + i).astype(F32) - HALF
        sums = jnp.zeros((LANES, LANES), F32)
        for k in range(chunks):
            lanes = slice(k * LANES, (k + 1) * LANES)
            value = hat(base[:, lanes] + cosine[k : k + 1, :] * upos)
            tile[here, lanes] = value
            sums += value.astype(F32)
        total = jnp.sum(sums, axis=1, keepdims=True)
        recip[here, :] = jnp.broadcast_to(1.0 / total, (LANES, LANES))
    joined = jnp.concatenate([r[...] for r in residuals], axis=0)
    back = jnp.dot(tile[:, : joined.shape[0]], joined, preferred_element_type=F32)
    for j in range(chans // LANES):
        lanes = slice(j * LANES, (j + 1) * LANES)
        partial[:, lanes] = image[:, lanes] + back[:, lanes] * recip[...]


def prepare(rays, residuals, image, first_row, angles):
    cells, chans = image.shape
    all_points = rays.shape[0] * LANES
    rows = min(4, cells // LANES)
    fixed = lambda shape: pl.BlockSpec(shape, lambda i, *_: (0, 0))
    sliding = lambda width: pl.BlockSpec((rows * LANES, width), lambda i, *_: (i, 0))
    return pl.pallas_call(
        functools.partial(prepare_kernel, angles, len(residuals)),
        grid_spec=pltpu.PrefetchScalarGridSpec(
            num_scalar_prefetch=1,
            grid=(cells // (rows * LANES),),
            in_specs=[fixed(rays.shape)]
            + [fixed(r.shape) for r in residuals]
            + [sliding(chans)],
            out_specs=[sliding(all_points), sliding(LANES), sliding(chans)],
            scratch_shapes=[pltpu.VMEM((LANES, all_points), F32), pltpu.VMEM(rays.shape, F32)],
        ),
        out_shape=[
            jax.ShapeDtypeStruct((cells, all_points), BF16),
            jax.ShapeDtypeStruct((cells, LANES), F32),
            jax.ShapeDtypeStruct((cells, chans), F32),
        ],
        compiler_params=pltpu.CompilerParams(vmem_limit_bytes=16 * MIB),
        cost_estimate=SMALL,
        name="prepare",
    )(first_row, rays, *residuals, image)


def gather_rows(pieces, joined):
    start = 0
    for piece in pieces:
        joined[start : start + piece.shape[0], :] = piece[...]
        start += piece.shape[0]


def add_share(here, first, tile, recip, partial, joined, out):
    columns = slice(first, first + joined.shape[0])
    back = jnp.dot(tile[here, columns], joined[...], preferred_element_type=F32)
    scale = recip[here, :]
    for j in range(out.shape[1] // LANES):
        lanes = slice(j * LANES, (j + 1) * LANES)
        out[here, lanes] = partial[here, lanes] + back[:, lanes] * scale


def add_kernel(first, count, *refs):
    pieces, (tile, recip, partial, out, joined) = refs[:count], refs[count:]
    gather_rows(pieces, joined)
    rows = min(512, out.shape[0])
    for start in range(0, out.shape[0], rows):
        add_share(slice(start, start + rows), first, tile, recip, partial, joined, out)


def add_back(pieces, first, tile, recip, partial):
    cells, chans = partial.shape
    vmem = pl.BlockSpec(memory_space=pltpu.VMEM)
    return pl.pallas_call(
        functools.partial(add_kernel, first, len(pieces)),
        in_specs=[vmem] * (len(pieces) + 3),
        out_specs=vmem,
        scratch_shapes=[pltpu.VMEM((sum(x.shape[0] for x in pieces), chans), BF16)],
        out_shape=jax.ShapeDtypeStruct((cells, chans), F32),
        compiler_params=pltpu.CompilerParams(vmem_limit_bytes=8 * MIB),
        cost_estimate=LARGE,
        name="add_back",
    )(*pieces, tile, recip, partial)


def back_kernel(first, count, *refs):
    pieces, (tile, recip, partial, out, joined, staged, sent) = refs[:count], refs[count:]
    chunks = sent.shape[0]
    rows = out.shape[0] // chunks
    gather_rows(pieces, joined)
    copies = []
    for chunk in range(chunks):
        here = slice(chunk * rows, (chunk + 1) * rows)
        add_share(here, first, tile, recip, partial, joined, staged)
        copies.append(
            pltpu.make_async_copy(staged.at[here, :], out.at[here, :], sent.at[chunk])
        )
        copies[-1].start()
    for copy in copies:
        copy.wait()


def back_project(pieces, first, tile, recip, partial):
    cells, chans = partial.shape
    chunks = max(1, cells // 512)
    vmem = pl.BlockSpec(memory_space=pltpu.VMEM)
    return pl.pallas_call(
        functools.partial(back_kernel, first, len(pieces)),
        in_specs=[vmem] * (len(pieces) + 3),
        out_specs=pl.BlockSpec(memory_space=pl.ANY),
        scratch_shapes=[
            pltpu.VMEM((sum(x.shape[0] for x in pieces), chans), BF16),
            pltpu.VMEM((cells, chans), F32),
            pltpu.SemaphoreType.DMA((chunks,)),
        ],
        out_shape=jax.ShapeDtypeStruct((cells, chans), F32),
        compiler_params=pltpu.CompilerParams(vmem_limit_bytes=16 * MIB),
        cost_estimate=SMALL,
        name="back_project",
    )(*pieces, tile, recip, partial)


def rotate(x, axis, shift, n):
    return lax.ppermute(x, axis, [(i, (i + shift) % n) for i in range(n)])


def swap(x, axis, mask, n):
    return lax.ppermute(x, axis, [(i, i ^ mask) for i in range(n)])


def body(frames, counts, point_ray, channel_pair_weights, tile_bin, image):
    n_scan = lax.axis_size("scan")
    n_chan = lax.axis_size("chan")
    nx = n_chan // 2
    points = counts.shape[0]
    cells, chans = image.shape
    angles = points * n_scan // NIMG
    chan_me = lax.axis_index("chan")
    x_me, core_me = chan_me // 2, chan_me % 2
    first_row = (lax.axis_index("scan") * (cells // NIMG)).astype(jnp.int32).reshape(1)

    middle = [r for r in range(1, n_scan) if r % 2 == 0] + [1]
    late = [r for r in range(3, n_scan, 2)]
    order = [0] + middle + late
    own_rays = point_ray.reshape(points // LANES, LANES)
    rays = [own_rays] + [swap(own_rays, "scan", r, n_scan) for r in order[1:]]
    all_rays = jnp.concatenate(rays, axis=0)

    projected = project(image, first_row, angles)
    own_share, *shares = reorder(all_rays, projected, n_scan)
    share_of = dict(zip(order[1:], shares))
    sending = sorted(share_of, key=lambda r: (2 * r != n_scan, -r))
    arrived = [swap(share_of[r], "scan", r, n_scan) for r in sending]

    place = []
    for e in range(nx):
        xi = (x_me + e) % nx
        place += [2 * xi + 1 - core_me, 2 * xi + core_me]
    place = jnp.stack(place).astype(jnp.int32)
    send, sums = integrate(
        frames, counts, channel_pair_weights, tile_bin, place, own_share, nx, chans
    )
    keep = select(place, sums, nx, chans)
    got = swap(send, "chan", 1, n_chan)
    pattern = keep[0] + got[0].astype(F32)
    for e in range(1, nx):
        joined = (keep[e] + got[e].astype(F32)).astype(BF16)
        pattern = pattern + rotate(joined, "chan", 2 * e, n_chan).astype(F32)

    row_total = row_totals(own_rays, sums, angles)
    scaled, recip = join(row_total, own_share, arrived)
    residual = (-scaled + pattern * (float(NIMG) * recip[:, :1])).astype(BF16)
    half = points // 2
    gathered = {0: [residual[:half], residual[half:]]}
    bit = n_scan // 2
    while bit:
        for r, pieces in list(gathered.items()):
            gathered[r ^ bit] = [swap(x, "scan", bit, n_scan) for x in pieces]
        bit //= 2
    tile, col_recip, partial = prepare(all_rays, gathered[0], image, first_row, angles)
    pieces = [x for r in middle for x in gathered[r]]
    partial = add_back(pieces, points, tile, col_recip, partial)
    pieces = [x for r in late for x in gathered[r]]
    return back_project(pieces, points * (1 + len(middle)), tile, col_recip, partial)


def solution(mesh):
    in_specs = (
        P(("grp", "scan"), "chan"),
        P(("grp", "scan")),
        P(("grp", "scan")),
        P("chan", None, None),
        P("chan"),
        P(("grp", "scan"), "chan"),
    )
    out_specs = P(("grp", "scan"), "chan")
    return jax.shard_map(body, mesh=mesh, in_specs=in_specs, out_specs=out_specs, check_vma=False)
```

```python
import functools
import math

import jax
import jax.numpy as jnp
import numpy as np
from jax import lax
from jax.experimental import pallas as pl
from jax.experimental.pallas import tpu as pltpu
from jax.sharding import PartitionSpec as P

NIMG = 128
HALF = (NIMG - 1) / 2.0
LANES = 128
MIB = 1024 * 1024
F32 = jnp.float32
BF16 = jnp.bfloat16
SMALL = pl.CostEstimate(flops=1, bytes_accessed=1, transcendentals=0)
LARGE = pl.CostEstimate(flops=10**11, bytes_accessed=10**8, transcendentals=0)


def angle_tables(angles):
    theta = np.arange(angles, dtype=np.float32) * np.float32(math.pi / angles)
    return [float(c) for c in np.cos(theta)], [float(s) for s in np.sin(theta)]


def ray_geometry(rays, angles):
    cos_tab, sin_tab = angle_tables(angles)
    which = rays // NIMG
    offset = (rays - which * NIMG).astype(F32) - HALF
    cosine = jnp.zeros(rays.shape, F32)
    sine = jnp.zeros(rays.shape, F32)
    for a in range(angles):
        here = which == a
        cosine = jnp.where(here, cos_tab[a], cosine)
        sine = jnp.where(here, sin_tab[a], sine)
    return cosine, sine, offset


def hat(distance):
    return jnp.maximum((1.0 - jnp.abs(distance)).astype(BF16), jnp.zeros((), BF16))


def integrate_kernel(
    nx, per_chunk, tile_bin, place, after, counts, frames, weights, send, acc, *scratch
):
    member, frame_buf, weight_buf, frame_sem, weight_sem = scratch
    points, slots = member.shape
    tile_bins = acc.shape[2]
    chunks = frame_sem.shape[0]
    width = frame_buf.shape[1] // chunks
    blocks = width // LANES

    def loads(chunk):
        here = slice(chunk * width, (chunk + 1) * width)
        return (
            pltpu.make_async_copy(frames.at[:, here], frame_buf.at[:, here], frame_sem.at[chunk]),
            pltpu.make_async_copy(weights.at[here, :], weight_buf.at[here, :], weight_sem.at[chunk]),
        )

    def add(mean, block, k):
        rows = slice(block * LANES, (block + 1) * LANES)
        lanes = slice(block % blocks * LANES, (block % blocks + 1) * LANES)
        value = jnp.dot(mean[:, lanes], weight_buf[rows, :], preferred_element_type=F32)
        acc[k] += value[:, :tile_bins]
        acc[k + 1] += value[:, tile_bins:]

    for chunk in range(min(2, chunks)):
        for load in loads(chunk):
            load.start()
    acc[...] = jnp.zeros_like(acc)
    count_row = counts[...].astype(F32)
    row = lax.broadcasted_iota(jnp.int32, (points, points), 0)
    col = lax.broadcasted_iota(jnp.int32, (points, points), 1)
    ends = jnp.sum(jnp.where(col <= row, count_row, 0.0), axis=1, keepdims=True)
    count = jnp.sum(jnp.where(col == row, count_row, 0.0), axis=1, keepdims=True)
    slot = lax.broadcasted_iota(jnp.int32, (points, slots), 1).astype(F32)
    inside = jnp.logical_and(slot >= ends - count, slot < ends)
    member[...] = jnp.where(inside, 1.0 / count, 0.0).astype(BF16)

    for chunk in range(chunks):
        for load in loads(chunk):
            load.wait()
        if chunk + 2 < chunks:
            for load in loads(chunk + 2):
                load.start()
        here = slice(chunk * width, (chunk + 1) * width)
        mean = jnp.dot(member[...], frame_buf[:, here], preferred_element_type=F32).astype(BF16)
        for block in range(chunk * blocks, (chunk + 1) * blocks):
            add(mean, block, tile_bin[block])

    for e in range(nx):
        for j in range(per_chunk):
            lanes = slice(j * tile_bins, (j + 1) * tile_bins)
            send[e, :, lanes] = acc[place[2 * e] * per_chunk + j].astype(BF16)


def integrate(frames, counts, weights, tile_bin, place, after, nx, chans):
    slots, pixels = frames.shape
    points = counts.shape[0]
    nblocks, tile_pix, pair = weights.shape
    tile_bins = pair // 2
    chunks = nblocks // 16 if nblocks % 16 == 0 else nblocks
    channel_blocks = 2 * nx * chans // tile_bins
    vmem = pl.BlockSpec(memory_space=pltpu.VMEM)
    smem = pl.BlockSpec(memory_space=pltpu.SMEM)
    anywhere = pl.BlockSpec(memory_space=pl.ANY)
    return pl.pallas_call(
        functools.partial(integrate_kernel, nx, chans // tile_bins),
        in_specs=[smem, smem, anywhere, vmem, anywhere, anywhere],
        out_specs=[vmem, vmem],
        scratch_shapes=[
            pltpu.VMEM((points, slots), BF16),
            pltpu.VMEM((slots, pixels), BF16),
            pltpu.VMEM((pixels, pair), BF16),
            pltpu.SemaphoreType.DMA((chunks,)),
            pltpu.SemaphoreType.DMA((chunks,)),
        ],
        out_shape=[
            jax.ShapeDtypeStruct((nx, points, chans), BF16),
            jax.ShapeDtypeStruct((channel_blocks, points, tile_bins), F32),
        ],
        compiler_params=pltpu.CompilerParams(vmem_limit_bytes=24 * MIB),
        cost_estimate=SMALL,
        name="integrate",
    )(
        tile_bin,
        place,
        after,
        counts.reshape(1, points),
        pltpu.with_memory_space_constraint(frames, pltpu.HBM),
        pltpu.with_memory_space_constraint(weights.reshape(pixels, pair), pltpu.HBM),
    )


def select_kernel(place, acc, own, *rest):
    _, points, tile_bins = acc.shape
    per_chunk = own.shape[1] // tile_bins
    for e, keep in enumerate((own,) + rest):
        for j in range(per_chunk):
            lanes = slice(j * tile_bins, (j + 1) * tile_bins)
            keep[:, lanes] = acc[place[2 * e + 1] * per_chunk + j]


def select(place, acc, nx, chans):
    points = acc.shape[1]
    vmem = pl.BlockSpec(memory_space=pltpu.VMEM)
    return pl.pallas_call(
        select_kernel,
        in_specs=[pl.BlockSpec(memory_space=pltpu.SMEM), vmem],
        out_specs=[vmem] * nx,
        out_shape=[jax.ShapeDtypeStruct((points, chans), F32)] * nx,
        compiler_params=pltpu.CompilerParams(vmem_limit_bytes=8 * MIB),
        cost_estimate=LARGE,
        name="select",
    )(place, acc)


def row_groups(rows):
    sizes = [min(2, rows)]
    while sum(sizes) < rows:
        sizes.append(min(6, rows - sum(sizes)))
    return sizes


def project_kernel(angles, first_row, image, out, staged, base, tile_a, tile_b, total, arrived):
    cos_tab, sin_tab = angle_tables(angles)
    tiles = (tile_a, tile_b)
    sizes = row_groups(image.shape[0] // LANES)

    def cells(group):
        return slice(sum(sizes[:group]) * LANES, sum(sizes[: group + 1]) * LANES)

    def load(group):
        here = cells(group)
        return pltpu.make_async_copy(
            image.at[here, :], staged.at[here, :], arrived.at[group]
        )

    def fill(group):
        first = first_row[0] + sum(sizes[:group])
        for i in range(sizes[group]):
            upos = (first + i).astype(F32) - HALF
            lanes = slice(i * LANES, (i + 1) * LANES)
            for a in range(angles):
                here = slice(a * NIMG, (a + 1) * NIMG)
                tiles[group % 2][here, lanes] = hat(base[here, :] + upos * cos_tab[a])

    for group in range(min(2, len(sizes))):
        load(group).start()
    vpos = lax.broadcasted_iota(jnp.int32, (NIMG, LANES), 1).astype(F32) - HALF
    offset = lax.broadcasted_iota(jnp.int32, (NIMG, LANES), 0).astype(F32) - HALF
    for a in range(angles):
        base[a * NIMG : (a + 1) * NIMG, :] = sin_tab[a] * vpos - offset
    fill(0)
    for group, size in enumerate(sizes):
        if group + 1 < len(sizes):
            fill(group + 1)
        load(group).wait()
        if group + 2 < len(sizes):
            load(group + 2).start()
        product = jnp.dot(
            tiles[group % 2][:, : size * LANES],
            staged[cells(group), :].astype(BF16),
            preferred_element_type=F32,
        )
        if group == 0:
            total[...] = product
        elif group + 1 < len(sizes):
            total[...] += product
        else:
            out[...] = (total[...] + product).astype(out.dtype)


def project(image, first_row, angles):
    cells, chans = image.shape
    rays = angles * NIMG
    sizes = row_groups(cells // LANES)
    widest = max(sizes) * LANES
    vmem = pl.BlockSpec(memory_space=pltpu.VMEM)
    anywhere = pl.BlockSpec(memory_space=pl.ANY)
    return pl.pallas_call(
        functools.partial(project_kernel, angles),
        in_specs=[pl.BlockSpec(memory_space=pltpu.SMEM), anywhere],
        out_specs=vmem,
        scratch_shapes=[
            pltpu.VMEM((cells, chans), F32),
            pltpu.VMEM((rays, LANES), F32),
            pltpu.VMEM((rays, widest), BF16),
            pltpu.VMEM((rays, widest), BF16),
            pltpu.VMEM((rays, chans), F32),
            pltpu.SemaphoreType.DMA((len(sizes),)),
        ],
        out_shape=jax.ShapeDtypeStruct((rays, chans), BF16),
        compiler_params=pltpu.CompilerParams(vmem_limit_bytes=40 * MIB),
        cost_estimate=pl.CostEstimate(
            flops=4 * rays * cells * chans, bytes_accessed=4 * cells * chans, transcendentals=0
        ),
        name="project",
    )(first_row, pltpu.with_memory_space_constraint(image, pltpu.HBM))


def reorder_kernel(rays, rows, *refs):
    outs, hot = refs[:-1], refs[-1]
    all_rays = rows.shape[0]
    points = outs[0].shape[0]
    together = hot.shape[0]
    number = lax.broadcasted_iota(jnp.int32, (LANES, all_rays), 1)
    for start in range(0, len(outs) * points, together):
        for k in range(together // LANES):
            row = start // LANES + k
            wanted = jnp.transpose(jnp.broadcast_to(rays[row : row + 1, :], (LANES, LANES)))
            hot[k * LANES : (k + 1) * LANES, :] = (number == wanted[:, :1]).astype(F32).astype(BF16)
        picked = jnp.dot(hot[...], rows[...], preferred_element_type=F32).astype(BF16)
        for k in range(0, together, points):
            outs[(start + k) // points][...] = picked[k : k + points, :]


def reorder(rays, rows, parts):
    all_rays, chans = rows.shape
    points = rays.shape[0] * LANES // parts
    together = max(points, min(all_rays, MIB // all_rays))
    vmem = pl.BlockSpec(memory_space=pltpu.VMEM)
    return pl.pallas_call(
        reorder_kernel,
        in_specs=[vmem, vmem],
        out_specs=[vmem] * parts,
        scratch_shapes=[pltpu.VMEM((together, all_rays), BF16)],
        out_shape=[jax.ShapeDtypeStruct((points, chans), BF16)] * parts,
        compiler_params=pltpu.CompilerParams(vmem_limit_bytes=16 * MIB),
        cost_estimate=SMALL,
        name="reorder",
    )(rays, rows)


def merge_kernel(count, after, *refs):
    for own, other, out in zip(refs[:count], refs[count : 2 * count], refs[2 * count :]):
        out[...] = (own[...].astype(F32) + other[...].astype(F32)).astype(BF16)


def merge(after, shares, received):
    count = len(shares)
    vmem = pl.BlockSpec(memory_space=pltpu.VMEM)
    return pl.pallas_call(
        functools.partial(merge_kernel, count),
        in_specs=[pl.BlockSpec(memory_space=pl.ANY)] + [vmem] * (2 * count),
        out_specs=[vmem] * count,
        out_shape=[jax.ShapeDtypeStruct(x.shape, BF16) for x in shares],
        compiler_params=pltpu.CompilerParams(vmem_limit_bytes=8 * MIB),
        cost_estimate=SMALL,
        name="merge",
    )(after, *shares, *received)


def row_total_kernel(angles, after, rays, row_total):
    cos_r, sin_r, off_r = ray_geometry(rays[...], angles)
    line = lax.broadcasted_iota(jnp.int32, (LANES, LANES), 0).astype(F32) - HALF
    for k in range(rays.shape[0]):
        cosine, sine, offset = (x[k : k + 1, :] for x in (cos_r, sin_r, off_r))
        along_u = jnp.abs(cosine) >= jnp.abs(sine)
        steep = jnp.where(along_u, cosine, sine)
        flat = jnp.where(along_u, sine, cosine)
        crossing = jnp.floor((offset - flat * line) / steep + HALF)
        sums = jnp.zeros((LANES, LANES), F32)
        for near in range(-1, 3):
            cell = crossing + float(near)
            weight = hat(flat * line + steep * (cell - HALF) - offset).astype(F32)
            inside = jnp.logical_and(cell >= 0.0, cell <= NIMG - 1.0)
            sums += jnp.where(inside, weight, 0.0)
        total = jnp.sum(sums, axis=0, keepdims=True)
        row_total[k * LANES : (k + 1) * LANES, :] = jnp.transpose(
            jnp.broadcast_to(total, (LANES, LANES))
        )


def row_totals(rays, after, angles):
    points = rays.shape[0] * LANES
    vmem = pl.BlockSpec(memory_space=pltpu.VMEM)
    return pl.pallas_call(
        functools.partial(row_total_kernel, angles),
        in_specs=[pl.BlockSpec(memory_space=pl.ANY), vmem],
        out_specs=vmem,
        out_shape=jax.ShapeDtypeStruct((points, LANES), F32),
        compiler_params=pltpu.CompilerParams(vmem_limit_bytes=8 * MIB),
        cost_estimate=SMALL,
        name="row_totals",
    )(after, rays)


def join_kernel(row_total, own, *refs):
    arrived, (scaled, recip) = refs[:-2], refs[-2:]
    total = own[...].astype(F32)
    for part in arrived:
        total += part[...].astype(F32)
    recip[...] = 1.0 / row_total[...]
    for j in range(own.shape[1] // LANES):
        lanes = slice(j * LANES, (j + 1) * LANES)
        scaled[:, lanes] = total[:, lanes] * recip[...]


def join(row_total, own, arrived):
    vmem = pl.BlockSpec(memory_space=pltpu.VMEM)
    return pl.pallas_call(
        join_kernel,
        in_specs=[vmem] * (2 + len(arrived)),
        out_specs=[vmem, vmem],
        out_shape=[
            jax.ShapeDtypeStruct(own.shape, F32),
            jax.ShapeDtypeStruct(row_total.shape, F32),
        ],
        compiler_params=pltpu.CompilerParams(vmem_limit_bytes=8 * MIB),
        cost_estimate=LARGE,
        name="join",
    )(row_total, own, *arrived)


def prepare_kernel(angles, early, first_row, rays, *refs):
    residuals, (image, tile, recip, partial, base, cosine) = refs[:early], refs[early:]
    step = pl.program_id(0)
    chunks = rays.shape[0]
    chans = image.shape[1]
    rows = tile.shape[0] // LANES

    @pl.when(step == 0)
    def _():
        cos_c, sin_c, off_c = ray_geometry(rays[...], angles)
        cosine[...] = cos_c
        vpos = lax.broadcasted_iota(jnp.int32, (LANES, LANES), 0).astype(F32) - HALF
        for k in range(chunks):
            base[:, k * LANES : (k + 1) * LANES] = sin_c[k : k + 1, :] * vpos - off_c[k : k + 1, :]

    for i in range(rows):
        here = slice(i * LANES, (i + 1) * LANES)
        upos = (first_row[0] + step * rows + i).astype(F32) - HALF
        sums = jnp.zeros((LANES, LANES), F32)
        for k in range(chunks):
            lanes = slice(k * LANES, (k + 1) * LANES)
            value = hat(base[:, lanes] + cosine[k : k + 1, :] * upos)
            tile[here, lanes] = value
            sums += value.astype(F32)
        total = jnp.sum(sums, axis=1, keepdims=True)
        recip[here, :] = jnp.broadcast_to(1.0 / total, (LANES, LANES))
    joined = jnp.concatenate([r[...] for r in residuals], axis=0)
    back = jnp.dot(tile[:, : joined.shape[0]], joined, preferred_element_type=F32)
    for j in range(chans // LANES):
        lanes = slice(j * LANES, (j + 1) * LANES)
        partial[:, lanes] = image[:, lanes] + back[:, lanes] * recip[...]


def prepare(rays, residuals, image, first_row, angles):
    cells, chans = image.shape
    all_points = rays.shape[0] * LANES
    rows = min(4, cells // LANES)
    fixed = lambda shape: pl.BlockSpec(shape, lambda i, *_: (0, 0))
    sliding = lambda width: pl.BlockSpec((rows * LANES, width), lambda i, *_: (i, 0))
    return pl.pallas_call(
        functools.partial(prepare_kernel, angles, len(residuals)),
        grid_spec=pltpu.PrefetchScalarGridSpec(
            num_scalar_prefetch=1,
            grid=(cells // (rows * LANES),),
            in_specs=[fixed(rays.shape)]
            + [fixed(r.shape) for r in residuals]
            + [sliding(chans)],
            out_specs=[sliding(all_points), sliding(LANES), sliding(chans)],
            scratch_shapes=[pltpu.VMEM((LANES, all_points), F32), pltpu.VMEM(rays.shape, F32)],
        ),
        out_shape=[
            jax.ShapeDtypeStruct((cells, all_points), BF16),
            jax.ShapeDtypeStruct((cells, LANES), F32),
            jax.ShapeDtypeStruct((cells, chans), F32),
        ],
        compiler_params=pltpu.CompilerParams(vmem_limit_bytes=16 * MIB),
        cost_estimate=SMALL,
        name="prepare",
    )(first_row, rays, *residuals, image)


def gather_rows(pieces, joined):
    start = 0
    for piece in pieces:
        joined[start : start + piece.shape[0], :] = piece[...]
        start += piece.shape[0]


def add_share(here, first, tile, recip, partial, joined, out):
    columns = slice(first, first + joined.shape[0])
    back = jnp.dot(tile[here, columns], joined[...], preferred_element_type=F32)
    scale = recip[here, :]
    for j in range(out.shape[1] // LANES):
        lanes = slice(j * LANES, (j + 1) * LANES)
        out[here, lanes] = partial[here, lanes] + back[:, lanes] * scale


def add_kernel(first, count, *refs):
    pieces, (tile, recip, partial, out, joined) = refs[:count], refs[count:]
    gather_rows(pieces, joined)
    rows = min(512, out.shape[0])
    for start in range(0, out.shape[0], rows):
        add_share(slice(start, start + rows), first, tile, recip, partial, joined, out)


def add_back(pieces, first, tile, recip, partial):
    cells, chans = partial.shape
    vmem = pl.BlockSpec(memory_space=pltpu.VMEM)
    return pl.pallas_call(
        functools.partial(add_kernel, first, len(pieces)),
        in_specs=[vmem] * (len(pieces) + 3),
        out_specs=vmem,
        scratch_shapes=[pltpu.VMEM((sum(x.shape[0] for x in pieces), chans), BF16)],
        out_shape=jax.ShapeDtypeStruct((cells, chans), F32),
        compiler_params=pltpu.CompilerParams(vmem_limit_bytes=8 * MIB),
        cost_estimate=LARGE,
        name="add_back",
    )(*pieces, tile, recip, partial)


def back_kernel(first, count, *refs):
    pieces, (tile, recip, partial, out, joined, staged, sent) = refs[:count], refs[count:]
    chunks = sent.shape[0]
    rows = out.shape[0] // chunks
    gather_rows(pieces, joined)
    copies = []
    for chunk in range(chunks):
        here = slice(chunk * rows, (chunk + 1) * rows)
        add_share(here, first, tile, recip, partial, joined, staged)
        copies.append(
            pltpu.make_async_copy(staged.at[here, :], out.at[here, :], sent.at[chunk])
        )
        copies[-1].start()
    for copy in copies:
        copy.wait()


def back_project(pieces, first, tile, recip, partial):
    cells, chans = partial.shape
    chunks = max(1, cells // 512)
    vmem = pl.BlockSpec(memory_space=pltpu.VMEM)
    return pl.pallas_call(
        functools.partial(back_kernel, first, len(pieces)),
        in_specs=[vmem] * (len(pieces) + 3),
        out_specs=pl.BlockSpec(memory_space=pl.ANY),
        scratch_shapes=[
            pltpu.VMEM((sum(x.shape[0] for x in pieces), chans), BF16),
            pltpu.VMEM((cells, chans), F32),
            pltpu.SemaphoreType.DMA((chunks,)),
        ],
        out_shape=jax.ShapeDtypeStruct((cells, chans), F32),
        compiler_params=pltpu.CompilerParams(vmem_limit_bytes=16 * MIB),
        cost_estimate=SMALL,
        name="back_project",
    )(*pieces, tile, recip, partial)


def rotate(x, axis, shift, n):
    return lax.ppermute(x, axis, [(i, (i + shift) % n) for i in range(n)])


def swap(x, axis, mask, n):
    return lax.ppermute(x, axis, [(i, i ^ mask) for i in range(n)])


def body(frames, counts, point_ray, channel_pair_weights, tile_bin, image):
    n_scan = lax.axis_size("scan")
    n_chan = lax.axis_size("chan")
    nx = n_chan // 2
    points = counts.shape[0]
    cells, chans = image.shape
    angles = points * n_scan // NIMG
    chan_me = lax.axis_index("chan")
    x_me, core_me = chan_me // 2, chan_me % 2
    first_row = (lax.axis_index("scan") * (cells // NIMG)).astype(jnp.int32).reshape(1)

    middle = [r for r in range(1, n_scan) if r % 2 == 0] + [1]
    late = [r for r in range(3, n_scan, 2)]
    order = [0] + middle + late
    own_rays = point_ray.reshape(points // LANES, LANES)
    rays = [own_rays] + [swap(own_rays, "scan", r, n_scan) for r in order[1:]]
    all_rays = jnp.concatenate(rays, axis=0)

    projected = project(image, first_row, angles)
    own_share, *shares = reorder(all_rays, projected, n_scan)
    share_of = dict(zip(order[1:], shares))
    relayed = {r ^ 1: swap(share_of[r], "scan", 1, n_scan) for r in late}

    place = []
    for e in range(nx):
        xi = (x_me + e) % nx
        place += [2 * xi + 1 - core_me, 2 * xi + core_me]
    place = jnp.stack(place).astype(jnp.int32)
    send, sums = integrate(
        frames, counts, channel_pair_weights, tile_bin, place, own_share, nx, chans
    )
    keep = select(place, sums, nx, chans)
    even = sorted(relayed)
    merged = merge(sums, [share_of[r] for r in even], [relayed[r] for r in even])
    arrived = [swap(x, "scan", r, n_scan) for r, x in zip(even, merged)]
    arrived.append(swap(share_of[1], "scan", 1, n_scan))
    got = swap(send, "chan", 1, n_chan)
    pattern = keep[0] + got[0].astype(F32)
    for e in range(1, nx):
        joined = (keep[e] + got[e].astype(F32)).astype(BF16)
        pattern = pattern + rotate(joined, "chan", 2 * e, n_chan).astype(F32)

    row_total = row_totals(own_rays, sums, angles)
    scaled, recip = join(row_total, own_share, arrived)
    residual = (-scaled + pattern * (float(NIMG) * recip[:, :1])).astype(BF16)
    half = points // 2
    gathered = {0: [residual[:half], residual[half:]]}
    bit = n_scan // 2
    while bit:
        for r, pieces in list(gathered.items()):
            gathered[r ^ bit] = [swap(x, "scan", bit, n_scan) for x in pieces]
        bit //= 2
    tile, col_recip, partial = prepare(all_rays, gathered[0], image, first_row, angles)
    pieces = [x for r in middle for x in gathered[r]]
    partial = add_back(pieces, points, tile, col_recip, partial)
    pieces = [x for r in late for x in gathered[r]]
    return back_project(pieces, points * (1 + len(middle)), tile, col_recip, partial)


def solution(mesh):
    in_specs = (
        P(("grp", "scan"), "chan"),
        P(("grp", "scan")),
        P(("grp", "scan")),
        P("chan", None, None),
        P("chan"),
        P(("grp", "scan"), "chan"),
    )
    out_specs = P(("grp", "scan"), "chan")
    return jax.shard_map(body, mesh=mesh, in_specs=in_specs, out_specs=out_specs, check_vma=False)
```

```python
import functools
import math

import jax
import jax.numpy as jnp
import numpy as np
from jax import lax
from jax.experimental import pallas as pl
from jax.experimental.pallas import tpu as pltpu
from jax.sharding import PartitionSpec as P

NIMG = 128
HALF = (NIMG - 1) / 2.0
LANES = 128
MIB = 1024 * 1024
F32 = jnp.float32
BF16 = jnp.bfloat16
SMALL = pl.CostEstimate(flops=1, bytes_accessed=1, transcendentals=0)
LARGE = pl.CostEstimate(flops=10**11, bytes_accessed=10**8, transcendentals=0)


def angle_tables(angles):
    theta = np.arange(angles, dtype=np.float32) * np.float32(math.pi / angles)
    return [float(c) for c in np.cos(theta)], [float(s) for s in np.sin(theta)]


def ray_geometry(rays, angles):
    cos_tab, sin_tab = angle_tables(angles)
    which = rays // NIMG
    offset = (rays - which * NIMG).astype(F32) - HALF
    cosine = jnp.zeros(rays.shape, F32)
    sine = jnp.zeros(rays.shape, F32)
    for a in range(angles):
        here = which == a
        cosine = jnp.where(here, cos_tab[a], cosine)
        sine = jnp.where(here, sin_tab[a], sine)
    return cosine, sine, offset


def hat(distance):
    return jnp.maximum((1.0 - jnp.abs(distance)).astype(BF16), jnp.zeros((), BF16))


def integrate_kernel(
    nx, per_chunk, tile_bin, place, after, counts, frames, weights, send, acc, *scratch
):
    member, frame_buf, weight_buf, frame_sem, weight_sem = scratch
    points, slots = member.shape
    tile_bins = acc.shape[2]
    chunks = frame_sem.shape[0]
    width = frame_buf.shape[1] // chunks
    blocks = width // LANES

    def loads(chunk):
        here = slice(chunk * width, (chunk + 1) * width)
        return (
            pltpu.make_async_copy(frames.at[:, here], frame_buf.at[:, here], frame_sem.at[chunk]),
            pltpu.make_async_copy(weights.at[here, :], weight_buf.at[here, :], weight_sem.at[chunk]),
        )

    def add(mean, block, k):
        rows = slice(block * LANES, (block + 1) * LANES)
        lanes = slice(block % blocks * LANES, (block % blocks + 1) * LANES)
        value = jnp.dot(mean[:, lanes], weight_buf[rows, :], preferred_element_type=F32)
        acc[k] += value[:, :tile_bins]
        acc[k + 1] += value[:, tile_bins:]

    for chunk in range(min(2, chunks)):
        for load in loads(chunk):
            load.start()
    acc[...] = jnp.zeros_like(acc)
    count_row = counts[...].astype(F32)
    row = lax.broadcasted_iota(jnp.int32, (points, points), 0)
    col = lax.broadcasted_iota(jnp.int32, (points, points), 1)
    ends = jnp.sum(jnp.where(col <= row, count_row, 0.0), axis=1, keepdims=True)
    count = jnp.sum(jnp.where(col == row, count_row, 0.0), axis=1, keepdims=True)
    slot = lax.broadcasted_iota(jnp.int32, (points, slots), 1).astype(F32)
    inside = jnp.logical_and(slot >= ends - count, slot < ends)
    member[...] = jnp.where(inside, 1.0 / count, 0.0).astype(BF16)

    for chunk in range(chunks):
        for load in loads(chunk):
            load.wait()
        if chunk + 2 < chunks:
            for load in loads(chunk + 2):
                load.start()
        here = slice(chunk * width, (chunk + 1) * width)
        mean = jnp.dot(member[...], frame_buf[:, here], preferred_element_type=F32).astype(BF16)
        for block in range(chunk * blocks, (chunk + 1) * blocks):
            add(mean, block, tile_bin[block])

    for e in range(nx):
        for j in range(per_chunk):
            lanes = slice(j * tile_bins, (j + 1) * tile_bins)
            send[e, :, lanes] = acc[place[2 * e] * per_chunk + j].astype(BF16)


def integrate(frames, counts, weights, tile_bin, place, after, nx, chans):
    slots, pixels = frames.shape
    points = counts.shape[0]
    nblocks, tile_pix, pair = weights.shape
    tile_bins = pair // 2
    chunks = nblocks // 16 if nblocks % 16 == 0 else nblocks
    channel_blocks = 2 * nx * chans // tile_bins
    vmem = pl.BlockSpec(memory_space=pltpu.VMEM)
    smem = pl.BlockSpec(memory_space=pltpu.SMEM)
    anywhere = pl.BlockSpec(memory_space=pl.ANY)
    return pl.pallas_call(
        functools.partial(integrate_kernel, nx, chans // tile_bins),
        in_specs=[smem, smem, anywhere, vmem, anywhere, anywhere],
        out_specs=[vmem, vmem],
        scratch_shapes=[
            pltpu.VMEM((points, slots), BF16),
            pltpu.VMEM((slots, pixels), BF16),
            pltpu.VMEM((pixels, pair), BF16),
            pltpu.SemaphoreType.DMA((chunks,)),
            pltpu.SemaphoreType.DMA((chunks,)),
        ],
        out_shape=[
            jax.ShapeDtypeStruct((nx, points, chans), BF16),
            jax.ShapeDtypeStruct((channel_blocks, points, tile_bins), F32),
        ],
        compiler_params=pltpu.CompilerParams(vmem_limit_bytes=24 * MIB),
        cost_estimate=SMALL,
        name="integrate",
    )(
        tile_bin,
        place,
        after,
        counts.reshape(1, points),
        pltpu.with_memory_space_constraint(frames, pltpu.HBM),
        pltpu.with_memory_space_constraint(weights.reshape(pixels, pair), pltpu.HBM),
    )


def select_kernel(place, acc, own, *rest):
    _, points, tile_bins = acc.shape
    per_chunk = own.shape[1] // tile_bins
    for e, keep in enumerate((own,) + rest):
        for j in range(per_chunk):
            lanes = slice(j * tile_bins, (j + 1) * tile_bins)
            keep[:, lanes] = acc[place[2 * e + 1] * per_chunk + j]


def select(place, acc, nx, chans):
    points = acc.shape[1]
    vmem = pl.BlockSpec(memory_space=pltpu.VMEM)
    return pl.pallas_call(
        select_kernel,
        in_specs=[pl.BlockSpec(memory_space=pltpu.SMEM), vmem],
        out_specs=[vmem] * nx,
        out_shape=[jax.ShapeDtypeStruct((points, chans), F32)] * nx,
        compiler_params=pltpu.CompilerParams(vmem_limit_bytes=8 * MIB),
        cost_estimate=LARGE,
        name="select",
    )(place, acc)


def row_groups(rows):
    sizes = [min(2, rows)]
    while sum(sizes) < rows:
        sizes.append(min(6, rows - sum(sizes)))
    return sizes


def project_kernel(angles, first_row, image, out, staged, base, tile_a, tile_b, total, arrived):
    cos_tab, sin_tab = angle_tables(angles)
    tiles = (tile_a, tile_b)
    sizes = row_groups(image.shape[0] // LANES)

    def cells(group):
        return slice(sum(sizes[:group]) * LANES, sum(sizes[: group + 1]) * LANES)

    def load(group):
        here = cells(group)
        return pltpu.make_async_copy(
            image.at[here, :], staged.at[here, :], arrived.at[group]
        )

    def fill(group):
        first = first_row[0] + sum(sizes[:group])
        for i in range(sizes[group]):
            upos = (first + i).astype(F32) - HALF
            lanes = slice(i * LANES, (i + 1) * LANES)
            for a in range(angles):
                here = slice(a * NIMG, (a + 1) * NIMG)
                tiles[group % 2][here, lanes] = hat(base[here, :] + upos * cos_tab[a])

    for group in range(min(2, len(sizes))):
        load(group).start()
    vpos = lax.broadcasted_iota(jnp.int32, (NIMG, LANES), 1).astype(F32) - HALF
    offset = lax.broadcasted_iota(jnp.int32, (NIMG, LANES), 0).astype(F32) - HALF
    for a in range(angles):
        base[a * NIMG : (a + 1) * NIMG, :] = sin_tab[a] * vpos - offset
    fill(0)
    for group, size in enumerate(sizes):
        if group + 1 < len(sizes):
            fill(group + 1)
        load(group).wait()
        if group + 2 < len(sizes):
            load(group + 2).start()
        product = jnp.dot(
            tiles[group % 2][:, : size * LANES],
            staged[cells(group), :].astype(BF16),
            preferred_element_type=F32,
        )
        if group == 0:
            total[...] = product
        elif group + 1 < len(sizes):
            total[...] += product
        else:
            out[...] = (total[...] + product).astype(out.dtype)


def project(image, first_row, angles):
    cells, chans = image.shape
    rays = angles * NIMG
    sizes = row_groups(cells // LANES)
    widest = max(sizes) * LANES
    vmem = pl.BlockSpec(memory_space=pltpu.VMEM)
    anywhere = pl.BlockSpec(memory_space=pl.ANY)
    return pl.pallas_call(
        functools.partial(project_kernel, angles),
        in_specs=[pl.BlockSpec(memory_space=pltpu.SMEM), anywhere],
        out_specs=vmem,
        scratch_shapes=[
            pltpu.VMEM((cells, chans), F32),
            pltpu.VMEM((rays, LANES), F32),
            pltpu.VMEM((rays, widest), BF16),
            pltpu.VMEM((rays, widest), BF16),
            pltpu.VMEM((rays, chans), F32),
            pltpu.SemaphoreType.DMA((len(sizes),)),
        ],
        out_shape=jax.ShapeDtypeStruct((rays, chans), BF16),
        compiler_params=pltpu.CompilerParams(vmem_limit_bytes=40 * MIB),
        cost_estimate=pl.CostEstimate(
            flops=4 * rays * cells * chans, bytes_accessed=4 * cells * chans, transcendentals=0
        ),
        name="project",
    )(first_row, pltpu.with_memory_space_constraint(image, pltpu.HBM))


def reorder_kernel(rays, rows, *refs):
    outs, hot = refs[:-1], refs[-1]
    all_rays = rows.shape[0]
    points = outs[0].shape[0]
    together = hot.shape[0]
    number = lax.broadcasted_iota(jnp.int32, (LANES, all_rays), 1)
    for start in range(0, len(outs) * points, together):
        for k in range(together // LANES):
            row = start // LANES + k
            wanted = jnp.transpose(jnp.broadcast_to(rays[row : row + 1, :], (LANES, LANES)))
            hot[k * LANES : (k + 1) * LANES, :] = jnp.where(number == jnp.tile(wanted, (1, all_rays // LANES)), 1.0, 0.0).astype(BF16)
        picked = jnp.dot(hot[...], rows[...], preferred_element_type=F32).astype(BF16)
        for k in range(0, together, points):
            outs[(start + k) // points][...] = picked[k : k + points, :]


def reorder(rays, rows, parts):
    all_rays, chans = rows.shape
    points = rays.shape[0] * LANES // parts
    together = points
    vmem = pl.BlockSpec(memory_space=pltpu.VMEM)
    return pl.pallas_call(
        reorder_kernel,
        in_specs=[vmem, vmem],
        out_specs=[vmem] * parts,
        scratch_shapes=[pltpu.VMEM((together, all_rays), BF16)],
        out_shape=[jax.ShapeDtypeStruct((points, chans), BF16)] * parts,
        compiler_params=pltpu.CompilerParams(vmem_limit_bytes=16 * MIB),
        cost_estimate=SMALL,
        name="reorder",
    )(rays, rows)


def merge_kernel(count, after, *refs):
    for own, other, out in zip(refs[:count], refs[count : 2 * count], refs[2 * count :]):
        out[...] = (own[...].astype(F32) + other[...].astype(F32)).astype(BF16)


def merge(after, shares, received):
    count = len(shares)
    vmem = pl.BlockSpec(memory_space=pltpu.VMEM)
    return pl.pallas_call(
        functools.partial(merge_kernel, count),
        in_specs=[pl.BlockSpec(memory_space=pl.ANY)] + [vmem] * (2 * count),
        out_specs=[vmem] * count,
        out_shape=[jax.ShapeDtypeStruct(x.shape, BF16) for x in shares],
        compiler_params=pltpu.CompilerParams(vmem_limit_bytes=8 * MIB),
        cost_estimate=SMALL,
        name="merge",
    )(after, *shares, *received)


def row_total_kernel(angles, after, rays, row_total):
    cos_r, sin_r, off_r = ray_geometry(rays[...], angles)
    line = lax.broadcasted_iota(jnp.int32, (LANES, LANES), 0).astype(F32) - HALF
    for k in range(rays.shape[0]):
        cosine, sine, offset = (x[k : k + 1, :] for x in (cos_r, sin_r, off_r))
        along_u = jnp.abs(cosine) >= jnp.abs(sine)
        steep = jnp.where(along_u, cosine, sine)
        flat = jnp.where(along_u, sine, cosine)
        crossing = jnp.floor((offset - flat * line) / steep + HALF)
        sums = jnp.zeros((LANES, LANES), F32)
        for near in range(-1, 3):
            cell = crossing + float(near)
            weight = hat(flat * line + steep * (cell - HALF) - offset).astype(F32)
            inside = jnp.logical_and(cell >= 0.0, cell <= NIMG - 1.0)
            sums += jnp.where(inside, weight, 0.0)
        total = jnp.sum(sums, axis=0, keepdims=True)
        row_total[k * LANES : (k + 1) * LANES, :] = jnp.transpose(
            jnp.broadcast_to(total, (LANES, LANES))
        )


def row_totals(rays, after, angles):
    points = rays.shape[0] * LANES
    vmem = pl.BlockSpec(memory_space=pltpu.VMEM)
    return pl.pallas_call(
        functools.partial(row_total_kernel, angles),
        in_specs=[pl.BlockSpec(memory_space=pl.ANY), vmem],
        out_specs=vmem,
        out_shape=jax.ShapeDtypeStruct((points, LANES), F32),
        compiler_params=pltpu.CompilerParams(vmem_limit_bytes=8 * MIB),
        cost_estimate=SMALL,
        name="row_totals",
    )(after, rays)


def join_kernel(row_total, own, *refs):
    arrived, (scaled, recip) = refs[:-2], refs[-2:]
    total = own[...].astype(F32)
    for part in arrived:
        total += part[...].astype(F32)
    recip[...] = 1.0 / row_total[...]
    for j in range(own.shape[1] // LANES):
        lanes = slice(j * LANES, (j + 1) * LANES)
        scaled[:, lanes] = total[:, lanes] * recip[...]


def join(row_total, own, arrived):
    vmem = pl.BlockSpec(memory_space=pltpu.VMEM)
    return pl.pallas_call(
        join_kernel,
        in_specs=[vmem] * (2 + len(arrived)),
        out_specs=[vmem, vmem],
        out_shape=[
            jax.ShapeDtypeStruct(own.shape, F32),
            jax.ShapeDtypeStruct(row_total.shape, F32),
        ],
        compiler_params=pltpu.CompilerParams(vmem_limit_bytes=8 * MIB),
        cost_estimate=LARGE,
        name="join",
    )(row_total, own, *arrived)


def prepare_kernel(angles, early, first_row, rays, *refs):
    residuals, (image, tile, recip, partial, base, cosine) = refs[:early], refs[early:]
    step = pl.program_id(0)
    chunks = rays.shape[0]
    chans = image.shape[1]
    rows = tile.shape[0] // LANES

    @pl.when(step == 0)
    def _():
        cos_c, sin_c, off_c = ray_geometry(rays[...], angles)
        cosine[...] = cos_c
        vpos = lax.broadcasted_iota(jnp.int32, (LANES, LANES), 0).astype(F32) - HALF
        for k in range(chunks):
            base[:, k * LANES : (k + 1) * LANES] = sin_c[k : k + 1, :] * vpos - off_c[k : k + 1, :]

    for i in range(rows):
        here = slice(i * LANES, (i + 1) * LANES)
        upos = (first_row[0] + step * rows + i).astype(F32) - HALF
        sums = jnp.zeros((LANES, LANES), F32)
        for k in range(chunks):
            lanes = slice(k * LANES, (k + 1) * LANES)
            value = hat(base[:, lanes] + cosine[k : k + 1, :] * upos)
            tile[here, lanes] = value
            sums += value.astype(F32)
        total = jnp.sum(sums, axis=1, keepdims=True)
        recip[here, :] = jnp.broadcast_to(1.0 / total, (LANES, LANES))
    joined = jnp.concatenate([r[...] for r in residuals], axis=0)
    back = jnp.dot(tile[:, : joined.shape[0]], joined, preferred_element_type=F32)
    for j in range(chans // LANES):
        lanes = slice(j * LANES, (j + 1) * LANES)
        partial[:, lanes] = image[:, lanes] + back[:, lanes] * recip[...]


def prepare(rays, residuals, image, first_row, angles):
    cells, chans = image.shape
    all_points = rays.shape[0] * LANES
    rows = min(4, cells // LANES)
    fixed = lambda shape: pl.BlockSpec(shape, lambda i, *_: (0, 0))
    sliding = lambda width: pl.BlockSpec((rows * LANES, width), lambda i, *_: (i, 0))
    return pl.pallas_call(
        functools.partial(prepare_kernel, angles, len(residuals)),
        grid_spec=pltpu.PrefetchScalarGridSpec(
            num_scalar_prefetch=1,
            grid=(cells // (rows * LANES),),
            in_specs=[fixed(rays.shape)]
            + [fixed(r.shape) for r in residuals]
            + [sliding(chans)],
            out_specs=[sliding(all_points), sliding(LANES), sliding(chans)],
            scratch_shapes=[pltpu.VMEM((LANES, all_points), F32), pltpu.VMEM(rays.shape, F32)],
        ),
        out_shape=[
            jax.ShapeDtypeStruct((cells, all_points), BF16),
            jax.ShapeDtypeStruct((cells, LANES), F32),
            jax.ShapeDtypeStruct((cells, chans), F32),
        ],
        compiler_params=pltpu.CompilerParams(vmem_limit_bytes=16 * MIB),
        cost_estimate=SMALL,
        name="prepare",
    )(first_row, rays, *residuals, image)


def gather_rows(pieces, joined):
    start = 0
    for piece in pieces:
        joined[start : start + piece.shape[0], :] = piece[...]
        start += piece.shape[0]


def add_share(here, first, tile, recip, partial, joined, out):
    columns = slice(first, first + joined.shape[0])
    back = jnp.dot(tile[here, columns], joined[...], preferred_element_type=F32)
    scale = recip[here, :]
    for j in range(out.shape[1] // LANES):
        lanes = slice(j * LANES, (j + 1) * LANES)
        out[here, lanes] = partial[here, lanes] + back[:, lanes] * scale


def add_kernel(first, count, *refs):
    pieces, (tile, recip, partial, out, joined) = refs[:count], refs[count:]
    gather_rows(pieces, joined)
    rows = min(512, out.shape[0])
    for start in range(0, out.shape[0], rows):
        add_share(slice(start, start + rows), first, tile, recip, partial, joined, out)


def add_back(pieces, first, tile, recip, partial):
    cells, chans = partial.shape
    vmem = pl.BlockSpec(memory_space=pltpu.VMEM)
    return pl.pallas_call(
        functools.partial(add_kernel, first, len(pieces)),
        in_specs=[vmem] * (len(pieces) + 3),
        out_specs=vmem,
        scratch_shapes=[pltpu.VMEM((sum(x.shape[0] for x in pieces), chans), BF16)],
        out_shape=jax.ShapeDtypeStruct((cells, chans), F32),
        compiler_params=pltpu.CompilerParams(vmem_limit_bytes=8 * MIB),
        cost_estimate=LARGE,
        name="add_back",
    )(*pieces, tile, recip, partial)


def back_kernel(first, count, *refs):
    pieces, (tile, recip, partial, out, joined, staged, sent) = refs[:count], refs[count:]
    chunks = sent.shape[0]
    rows = out.shape[0] // chunks
    gather_rows(pieces, joined)
    copies = []
    for chunk in range(chunks):
        here = slice(chunk * rows, (chunk + 1) * rows)
        add_share(here, first, tile, recip, partial, joined, staged)
        copies.append(
            pltpu.make_async_copy(staged.at[here, :], out.at[here, :], sent.at[chunk])
        )
        copies[-1].start()
    for copy in copies:
        copy.wait()


def back_project(pieces, first, tile, recip, partial):
    cells, chans = partial.shape
    chunks = max(1, cells // 512)
    vmem = pl.BlockSpec(memory_space=pltpu.VMEM)
    return pl.pallas_call(
        functools.partial(back_kernel, first, len(pieces)),
        in_specs=[vmem] * (len(pieces) + 3),
        out_specs=pl.BlockSpec(memory_space=pl.ANY),
        scratch_shapes=[
            pltpu.VMEM((sum(x.shape[0] for x in pieces), chans), BF16),
            pltpu.VMEM((cells, chans), F32),
            pltpu.SemaphoreType.DMA((chunks,)),
        ],
        out_shape=jax.ShapeDtypeStruct((cells, chans), F32),
        compiler_params=pltpu.CompilerParams(vmem_limit_bytes=16 * MIB),
        cost_estimate=SMALL,
        name="back_project",
    )(*pieces, tile, recip, partial)


def rotate(x, axis, shift, n):
    return lax.ppermute(x, axis, [(i, (i + shift) % n) for i in range(n)])


def swap(x, axis, mask, n):
    return lax.ppermute(x, axis, [(i, i ^ mask) for i in range(n)])


def body(frames, counts, point_ray, channel_pair_weights, tile_bin, image):
    n_scan = lax.axis_size("scan")
    n_chan = lax.axis_size("chan")
    nx = n_chan // 2
    points = counts.shape[0]
    cells, chans = image.shape
    angles = points * n_scan // NIMG
    chan_me = lax.axis_index("chan")
    x_me, core_me = chan_me // 2, chan_me % 2
    first_row = (lax.axis_index("scan") * (cells // NIMG)).astype(jnp.int32).reshape(1)

    middle = [r for r in range(1, n_scan) if r % 2 == 0] + [1]
    late = [r for r in range(3, n_scan, 2)]
    order = [0] + middle + late
    own_rays = point_ray.reshape(points // LANES, LANES)
    rays = [own_rays] + [swap(own_rays, "scan", r, n_scan) for r in order[1:]]
    all_rays = jnp.concatenate(rays, axis=0)

    projected = project(image, first_row, angles)
    own_share, *shares = reorder(all_rays, projected, n_scan)
    share_of = dict(zip(order[1:], shares))
    relayed = {r ^ 1: swap(share_of[r], "scan", 1, n_scan) for r in late}

    place = []
    for e in range(nx):
        xi = (x_me + e) % nx
        place += [2 * xi + 1 - core_me, 2 * xi + core_me]
    place = jnp.stack(place).astype(jnp.int32)
    send, sums = integrate(
        frames, counts, channel_pair_weights, tile_bin, place, own_share, nx, chans
    )
    keep = select(place, sums, nx, chans)
    even = sorted(relayed)
    merged = merge(sums, [share_of[r] for r in even], [relayed[r] for r in even])
    arrived = [swap(x, "scan", r, n_scan) for r, x in zip(even, merged)]
    arrived.append(swap(share_of[1], "scan", 1, n_scan))
    got = swap(send, "chan", 1, n_chan)
    pattern = keep[0] + got[0].astype(F32)
    for e in range(1, nx):
        joined = (keep[e] + got[e].astype(F32)).astype(BF16)
        pattern = pattern + rotate(joined, "chan", 2 * e, n_chan).astype(F32)

    row_total = row_totals(own_rays, sums, angles)
    scaled, recip = join(row_total, own_share, arrived)
    residual = (-scaled + pattern * (float(NIMG) * recip[:, :1])).astype(BF16)
    half = points // 2
    gathered = {0: [residual[:half], residual[half:]]}
    bit = n_scan // 2
    while bit:
        for r, pieces in list(gathered.items()):
            gathered[r ^ bit] = [swap(x, "scan", bit, n_scan) for x in pieces]
        bit //= 2
    tile, col_recip, partial = prepare(all_rays, gathered[0], image, first_row, angles)
    pieces = [x for r in middle for x in gathered[r]]
    partial = add_back(pieces, points, tile, col_recip, partial)
    pieces = [x for r in late for x in gathered[r]]
    return back_project(pieces, points * (1 + len(middle)), tile, col_recip, partial)


def solution(mesh):
    in_specs = (
        P(("grp", "scan"), "chan"),
        P(("grp", "scan")),
        P(("grp", "scan")),
        P("chan", None, None),
        P("chan"),
        P(("grp", "scan"), "chan"),
    )
    out_specs = P(("grp", "scan"), "chan")
    return jax.shard_map(body, mesh=mesh, in_specs=in_specs, out_specs=out_specs, check_vma=False)
```

```python
import functools
import math

import jax
import jax.numpy as jnp
import numpy as np
from jax import lax
from jax.experimental import pallas as pl
from jax.experimental.pallas import tpu as pltpu
from jax.sharding import PartitionSpec as P

NIMG = 128
HALF = (NIMG - 1) / 2.0
LANES = 128
MIB = 1024 * 1024
F32 = jnp.float32
BF16 = jnp.bfloat16
SMALL = pl.CostEstimate(flops=1, bytes_accessed=1, transcendentals=0)
LARGE = pl.CostEstimate(flops=10**11, bytes_accessed=10**8, transcendentals=0)


def angle_tables(angles):
    theta = np.arange(angles, dtype=np.float32) * np.float32(math.pi / angles)
    return [float(c) for c in np.cos(theta)], [float(s) for s in np.sin(theta)]


def ray_geometry(rays, angles):
    cos_tab, sin_tab = angle_tables(angles)
    which = rays // NIMG
    offset = (rays - which * NIMG).astype(F32) - HALF
    cosine = jnp.zeros(rays.shape, F32)
    sine = jnp.zeros(rays.shape, F32)
    for a in range(angles):
        here = which == a
        cosine = jnp.where(here, cos_tab[a], cosine)
        sine = jnp.where(here, sin_tab[a], sine)
    return cosine, sine, offset


def hat(distance):
    return jnp.maximum((1.0 - jnp.abs(distance)).astype(BF16), jnp.zeros((), BF16))


def integrate_kernel(
    nx, per_chunk, tile_bin, place, after, counts, frames, weights, send, acc, *scratch
):
    member, frame_buf, weight_buf, frame_sem, weight_sem = scratch
    points, slots = member.shape
    tile_bins = acc.shape[2]
    chunks = frame_sem.shape[0]
    width = frame_buf.shape[1] // chunks
    blocks = width // LANES

    def loads(chunk):
        here = slice(chunk * width, (chunk + 1) * width)
        return (
            pltpu.make_async_copy(frames.at[:, here], frame_buf.at[:, here], frame_sem.at[chunk]),
            pltpu.make_async_copy(weights.at[here, :], weight_buf.at[here, :], weight_sem.at[chunk]),
        )

    def add(mean, block, k):
        rows = slice(block * LANES, (block + 1) * LANES)
        lanes = slice(block % blocks * LANES, (block % blocks + 1) * LANES)
        value = jnp.dot(mean[:, lanes], weight_buf[rows, :], preferred_element_type=F32)
        acc[k] += value[:, :tile_bins]
        acc[k + 1] += value[:, tile_bins:]

    for chunk in range(min(2, chunks)):
        for load in loads(chunk):
            load.start()
    acc[...] = jnp.zeros_like(acc)
    count_row = counts[...].astype(F32)
    row = lax.broadcasted_iota(jnp.int32, (points, points), 0)
    col = lax.broadcasted_iota(jnp.int32, (points, points), 1)
    ends = jnp.sum(jnp.where(col <= row, count_row, 0.0), axis=1, keepdims=True)
    count = jnp.sum(jnp.where(col == row, count_row, 0.0), axis=1, keepdims=True)
    slot = lax.broadcasted_iota(jnp.int32, (points, slots), 1).astype(F32)
    inside = jnp.logical_and(slot >= ends - count, slot < ends)
    member[...] = jnp.where(inside, 1.0 / count, 0.0).astype(BF16)

    for chunk in range(chunks):
        for load in loads(chunk):
            load.wait()
        if chunk + 2 < chunks:
            for load in loads(chunk + 2):
                load.start()
        here = slice(chunk * width, (chunk + 1) * width)
        mean = jnp.dot(member[...], frame_buf[:, here], preferred_element_type=F32).astype(BF16)
        for block in range(chunk * blocks, (chunk + 1) * blocks):
            add(mean, block, tile_bin[block])

    for e in range(nx):
        for j in range(per_chunk):
            lanes = slice(j * tile_bins, (j + 1) * tile_bins)
            send[e, :, lanes] = acc[place[2 * e] * per_chunk + j].astype(BF16)


def integrate(frames, counts, weights, tile_bin, place, after, nx, chans):
    slots, pixels = frames.shape
    points = counts.shape[0]
    nblocks, tile_pix, pair = weights.shape
    tile_bins = pair // 2
    chunks = nblocks // 16 if nblocks % 16 == 0 else nblocks
    channel_blocks = 2 * nx * chans // tile_bins
    vmem = pl.BlockSpec(memory_space=pltpu.VMEM)
    smem = pl.BlockSpec(memory_space=pltpu.SMEM)
    anywhere = pl.BlockSpec(memory_space=pl.ANY)
    return pl.pallas_call(
        functools.partial(integrate_kernel, nx, chans // tile_bins),
        in_specs=[smem, smem, anywhere, vmem, anywhere, anywhere],
        out_specs=[vmem, vmem],
        scratch_shapes=[
            pltpu.VMEM((points, slots), BF16),
            pltpu.VMEM((slots, pixels), BF16),
            pltpu.VMEM((pixels, pair), BF16),
            pltpu.SemaphoreType.DMA((chunks,)),
            pltpu.SemaphoreType.DMA((chunks,)),
        ],
        out_shape=[
            jax.ShapeDtypeStruct((nx, points, chans), BF16),
            jax.ShapeDtypeStruct((channel_blocks, points, tile_bins), F32),
        ],
        compiler_params=pltpu.CompilerParams(vmem_limit_bytes=24 * MIB),
        cost_estimate=SMALL,
        name="integrate",
    )(
        tile_bin,
        place,
        after,
        counts.reshape(1, points),
        pltpu.with_memory_space_constraint(frames, pltpu.HBM),
        pltpu.with_memory_space_constraint(weights.reshape(pixels, pair), pltpu.HBM),
    )


def select_kernel(place, acc, own, *rest):
    _, points, tile_bins = acc.shape
    per_chunk = own.shape[1] // tile_bins
    for e, keep in enumerate((own,) + rest):
        for j in range(per_chunk):
            lanes = slice(j * tile_bins, (j + 1) * tile_bins)
            keep[:, lanes] = acc[place[2 * e + 1] * per_chunk + j]


def select(place, acc, nx, chans):
    points = acc.shape[1]
    vmem = pl.BlockSpec(memory_space=pltpu.VMEM)
    return pl.pallas_call(
        select_kernel,
        in_specs=[pl.BlockSpec(memory_space=pltpu.SMEM), vmem],
        out_specs=[vmem] * nx,
        out_shape=[jax.ShapeDtypeStruct((points, chans), F32)] * nx,
        compiler_params=pltpu.CompilerParams(vmem_limit_bytes=8 * MIB),
        cost_estimate=LARGE,
        name="select",
    )(place, acc)


def row_groups(rows):
    sizes = [min(2, rows)]
    while sum(sizes) < rows:
        sizes.append(min(6, rows - sum(sizes)))
    return sizes


def project_kernel(angles, first_row, image, out, staged, base, tile_a, tile_b, total, arrived):
    cos_tab, sin_tab = angle_tables(angles)
    tiles = (tile_a, tile_b)
    sizes = row_groups(image.shape[0] // LANES)

    def cells(group):
        return slice(sum(sizes[:group]) * LANES, sum(sizes[: group + 1]) * LANES)

    def load(group):
        here = cells(group)
        return pltpu.make_async_copy(
            image.at[here, :], staged.at[here, :], arrived.at[group]
        )

    def fill(group):
        first = first_row[0] + sum(sizes[:group])
        for i in range(sizes[group]):
            upos = (first + i).astype(F32) - HALF
            lanes = slice(i * LANES, (i + 1) * LANES)
            for a in range(angles):
                here = slice(a * NIMG, (a + 1) * NIMG)
                tiles[group % 2][here, lanes] = hat(base[here, :] + upos * cos_tab[a])

    for group in range(min(2, len(sizes))):
        load(group).start()
    vpos = lax.broadcasted_iota(jnp.int32, (NIMG, LANES), 1).astype(F32) - HALF
    offset = lax.broadcasted_iota(jnp.int32, (NIMG, LANES), 0).astype(F32) - HALF
    for a in range(angles):
        base[a * NIMG : (a + 1) * NIMG, :] = sin_tab[a] * vpos - offset
    fill(0)
    for group, size in enumerate(sizes):
        if group + 1 < len(sizes):
            fill(group + 1)
        load(group).wait()
        if group + 2 < len(sizes):
            load(group + 2).start()
        product = jnp.dot(
            tiles[group % 2][:, : size * LANES],
            staged[cells(group), :].astype(BF16),
            preferred_element_type=F32,
        )
        if group == 0:
            total[...] = product
        elif group + 1 < len(sizes):
            total[...] += product
        else:
            out[...] = (total[...] + product).astype(out.dtype)


def project(image, first_row, angles):
    cells, chans = image.shape
    rays = angles * NIMG
    sizes = row_groups(cells // LANES)
    widest = max(sizes) * LANES
    vmem = pl.BlockSpec(memory_space=pltpu.VMEM)
    anywhere = pl.BlockSpec(memory_space=pl.ANY)
    return pl.pallas_call(
        functools.partial(project_kernel, angles),
        in_specs=[pl.BlockSpec(memory_space=pltpu.SMEM), anywhere],
        out_specs=vmem,
        scratch_shapes=[
            pltpu.VMEM((cells, chans), F32),
            pltpu.VMEM((rays, LANES), F32),
            pltpu.VMEM((rays, widest), BF16),
            pltpu.VMEM((rays, widest), BF16),
            pltpu.VMEM((rays, chans), F32),
            pltpu.SemaphoreType.DMA((len(sizes),)),
        ],
        out_shape=jax.ShapeDtypeStruct((rays, chans), BF16),
        compiler_params=pltpu.CompilerParams(vmem_limit_bytes=40 * MIB),
        cost_estimate=pl.CostEstimate(
            flops=4 * rays * cells * chans, bytes_accessed=4 * cells * chans, transcendentals=0
        ),
        name="project",
    )(first_row, pltpu.with_memory_space_constraint(image, pltpu.HBM))


def reorder_kernel(rays, rows, *refs):
    outs, hot = refs[:-1], refs[-1]
    all_rays = rows.shape[0]
    points = outs[0].shape[0]
    together = hot.shape[0]
    number = lax.broadcasted_iota(jnp.int32, (LANES, all_rays), 1)
    for start in range(0, len(outs) * points, together):
        for k in range(together // LANES):
            row = start // LANES + k
            wanted = jnp.transpose(jnp.broadcast_to(rays[row : row + 1, :], (LANES, LANES)))
            hot[k * LANES : (k + 1) * LANES, :] = jnp.where(number == jnp.tile(wanted, (1, all_rays // LANES)), 1.0, 0.0).astype(BF16)
        picked = jnp.dot(hot[...], rows[...], preferred_element_type=F32).astype(BF16)
        for k in range(0, together, points):
            outs[(start + k) // points][...] = picked[k : k + points, :]


def reorder(rays, rows, parts):
    all_rays, chans = rows.shape
    points = rays.shape[0] * LANES // parts
    together = points
    vmem = pl.BlockSpec(memory_space=pltpu.VMEM)
    return pl.pallas_call(
        reorder_kernel,
        in_specs=[vmem, vmem],
        out_specs=[vmem] * parts,
        scratch_shapes=[pltpu.VMEM((together, all_rays), BF16)],
        out_shape=[jax.ShapeDtypeStruct((points, chans), BF16)] * parts,
        compiler_params=pltpu.CompilerParams(vmem_limit_bytes=16 * MIB),
        cost_estimate=SMALL,
        name="reorder",
    )(rays, rows)


def merge_kernel(count, after, *refs):
    for own, other, out in zip(refs[:count], refs[count : 2 * count], refs[2 * count :]):
        out[...] = (own[...].astype(F32) + other[...].astype(F32)).astype(BF16)


def merge(after, shares, received):
    count = len(shares)
    vmem = pl.BlockSpec(memory_space=pltpu.VMEM)
    return pl.pallas_call(
        functools.partial(merge_kernel, count),
        in_specs=[pl.BlockSpec(memory_space=pl.ANY)] + [vmem] * (2 * count),
        out_specs=[vmem] * count,
        out_shape=[jax.ShapeDtypeStruct(x.shape, BF16) for x in shares],
        compiler_params=pltpu.CompilerParams(vmem_limit_bytes=8 * MIB),
        cost_estimate=SMALL,
        name="merge",
    )(after, *shares, *received)


def row_total_kernel(angles, after, rays, row_total):
    cos_r, sin_r, off_r = ray_geometry(rays[...], angles)
    line = lax.broadcasted_iota(jnp.int32, (LANES, LANES), 0).astype(F32) - HALF
    for k in range(rays.shape[0]):
        cosine, sine, offset = (x[k : k + 1, :] for x in (cos_r, sin_r, off_r))
        along_u = jnp.abs(cosine) >= jnp.abs(sine)
        steep = jnp.where(along_u, cosine, sine)
        flat = jnp.where(along_u, sine, cosine)
        crossing = jnp.floor((offset - flat * line) / steep + HALF)
        sums = jnp.zeros((LANES, LANES), F32)
        for near in range(-1, 3):
            cell = crossing + float(near)
            weight = hat(flat * line + steep * (cell - HALF) - offset).astype(F32)
            inside = jnp.logical_and(cell >= 0.0, cell <= NIMG - 1.0)
            sums += jnp.where(inside, weight, 0.0)
        total = jnp.sum(sums, axis=0, keepdims=True)
        row_total[k * LANES : (k + 1) * LANES, :] = jnp.transpose(
            jnp.broadcast_to(total, (LANES, LANES))
        )


def row_totals(rays, after, angles):
    points = rays.shape[0] * LANES
    vmem = pl.BlockSpec(memory_space=pltpu.VMEM)
    return pl.pallas_call(
        functools.partial(row_total_kernel, angles),
        in_specs=[pl.BlockSpec(memory_space=pl.ANY), vmem],
        out_specs=vmem,
        out_shape=jax.ShapeDtypeStruct((points, LANES), F32),
        compiler_params=pltpu.CompilerParams(vmem_limit_bytes=8 * MIB),
        cost_estimate=SMALL,
        name="row_totals",
    )(after, rays)


def join_kernel(row_total, own, *refs):
    arrived, (scaled, recip) = refs[:-2], refs[-2:]
    total = own[...].astype(F32)
    for part in arrived:
        total += part[...].astype(F32)
    recip[...] = 1.0 / row_total[...]
    for j in range(own.shape[1] // LANES):
        lanes = slice(j * LANES, (j + 1) * LANES)
        scaled[:, lanes] = total[:, lanes] * recip[...]


def join(row_total, own, arrived):
    vmem = pl.BlockSpec(memory_space=pltpu.VMEM)
    return pl.pallas_call(
        join_kernel,
        in_specs=[vmem] * (2 + len(arrived)),
        out_specs=[vmem, vmem],
        out_shape=[
            jax.ShapeDtypeStruct(own.shape, F32),
            jax.ShapeDtypeStruct(row_total.shape, F32),
        ],
        compiler_params=pltpu.CompilerParams(vmem_limit_bytes=8 * MIB),
        cost_estimate=LARGE,
        name="join",
    )(row_total, own, *arrived)


def prepare_kernel(angles, early, first_row, rays, *refs):
    residuals, (image, tile, recip, partial, base, cosine) = refs[:early], refs[early:]
    step = pl.program_id(0)
    chunks = rays.shape[0]
    chans = image.shape[1]
    rows = tile.shape[0] // LANES

    @pl.when(step == 0)
    def _():
        cos_c, sin_c, off_c = ray_geometry(rays[...], angles)
        cosine[...] = cos_c
        vpos = lax.broadcasted_iota(jnp.int32, (LANES, LANES), 0).astype(F32) - HALF
        for k in range(chunks):
            base[:, k * LANES : (k + 1) * LANES] = sin_c[k : k + 1, :] * vpos - off_c[k : k + 1, :]

    for i in range(rows):
        here = slice(i * LANES, (i + 1) * LANES)
        upos = (first_row[0] + step * rows + i).astype(F32) - HALF
        sums = jnp.zeros((LANES, LANES), F32)
        for k in range(chunks):
            lanes = slice(k * LANES, (k + 1) * LANES)
            value = hat(base[:, lanes] + cosine[k : k + 1, :] * upos)
            tile[here, lanes] = value
            sums += value.astype(F32)
        total = jnp.sum(sums, axis=1, keepdims=True)
        recip[here, :] = jnp.broadcast_to(1.0 / total, (LANES, LANES))
    joined = jnp.concatenate([r[...] for r in residuals], axis=0)
    back = jnp.dot(tile[:, : joined.shape[0]], joined, preferred_element_type=F32)
    for j in range(chans // LANES):
        lanes = slice(j * LANES, (j + 1) * LANES)
        partial[:, lanes] = image[:, lanes] + back[:, lanes] * recip[...]


def prepare(rays, residuals, image, first_row, angles):
    cells, chans = image.shape
    all_points = rays.shape[0] * LANES
    rows = min(4, cells // LANES)
    fixed = lambda shape: pl.BlockSpec(shape, lambda i, *_: (0, 0))
    sliding = lambda width: pl.BlockSpec((rows * LANES, width), lambda i, *_: (i, 0))
    return pl.pallas_call(
        functools.partial(prepare_kernel, angles, len(residuals)),
        grid_spec=pltpu.PrefetchScalarGridSpec(
            num_scalar_prefetch=1,
            grid=(cells // (rows * LANES),),
            in_specs=[fixed(rays.shape)]
            + [fixed(r.shape) for r in residuals]
            + [sliding(chans)],
            out_specs=[sliding(all_points), sliding(LANES), sliding(chans)],
            scratch_shapes=[pltpu.VMEM((LANES, all_points), F32), pltpu.VMEM(rays.shape, F32)],
        ),
        out_shape=[
            jax.ShapeDtypeStruct((cells, all_points), BF16),
            jax.ShapeDtypeStruct((cells, LANES), F32),
            jax.ShapeDtypeStruct((cells, chans), F32),
        ],
        compiler_params=pltpu.CompilerParams(vmem_limit_bytes=16 * MIB),
        cost_estimate=SMALL,
        name="prepare",
    )(first_row, rays, *residuals, image)


def gather_rows(pieces, joined):
    start = 0
    for piece in pieces:
        joined[start : start + piece.shape[0], :] = piece[...]
        start += piece.shape[0]


def add_share(here, first, tile, recip, partial, joined, out):
    columns = slice(first, first + joined.shape[0])
    back = jnp.dot(tile[here, columns], joined[...], preferred_element_type=F32)
    scale = recip[here, :]
    for j in range(out.shape[1] // LANES):
        lanes = slice(j * LANES, (j + 1) * LANES)
        out[here, lanes] = partial[here, lanes] + back[:, lanes] * scale


def add_kernel(first, count, *refs):
    pieces, (tile, recip, partial, out, joined) = refs[:count], refs[count:]
    gather_rows(pieces, joined)
    rows = min(512, out.shape[0])
    for start in range(0, out.shape[0], rows):
        add_share(slice(start, start + rows), first, tile, recip, partial, joined, out)


def add_back(pieces, first, tile, recip, partial):
    cells, chans = partial.shape
    vmem = pl.BlockSpec(memory_space=pltpu.VMEM)
    return pl.pallas_call(
        functools.partial(add_kernel, first, len(pieces)),
        in_specs=[vmem] * (len(pieces) + 3),
        out_specs=vmem,
        scratch_shapes=[pltpu.VMEM((sum(x.shape[0] for x in pieces), chans), BF16)],
        out_shape=jax.ShapeDtypeStruct((cells, chans), F32),
        compiler_params=pltpu.CompilerParams(vmem_limit_bytes=8 * MIB),
        cost_estimate=LARGE,
        name="add_back",
    )(*pieces, tile, recip, partial)


def back_kernel(first, count, *refs):
    pieces, (tile, recip, partial, out, joined, staged, sent) = refs[:count], refs[count:]
    chunks = sent.shape[0]
    rows = out.shape[0] // chunks
    gather_rows(pieces, joined)
    copies = []
    for chunk in range(chunks):
        here = slice(chunk * rows, (chunk + 1) * rows)
        add_share(here, first, tile, recip, partial, joined, staged)
        copies.append(
            pltpu.make_async_copy(staged.at[here, :], out.at[here, :], sent.at[chunk])
        )
        copies[-1].start()
    for copy in copies:
        copy.wait()


def back_project(pieces, first, tile, recip, partial):
    cells, chans = partial.shape
    chunks = max(1, cells // 512)
    vmem = pl.BlockSpec(memory_space=pltpu.VMEM)
    return pl.pallas_call(
        functools.partial(back_kernel, first, len(pieces)),
        in_specs=[vmem] * (len(pieces) + 3),
        out_specs=pl.BlockSpec(memory_space=pl.ANY),
        scratch_shapes=[
            pltpu.VMEM((sum(x.shape[0] for x in pieces), chans), BF16),
            pltpu.VMEM((cells, chans), F32),
            pltpu.SemaphoreType.DMA((chunks,)),
        ],
        out_shape=jax.ShapeDtypeStruct((cells, chans), F32),
        compiler_params=pltpu.CompilerParams(vmem_limit_bytes=16 * MIB),
        cost_estimate=SMALL,
        name="back_project",
    )(*pieces, tile, recip, partial)


def rotate(x, axis, shift, n):
    return lax.ppermute(x, axis, [(i, (i + shift) % n) for i in range(n)])


def swap(x, axis, mask, n):
    return lax.ppermute(x, axis, [(i, i ^ mask) for i in range(n)])


def onward(i):
    return i - i % 4 + (1, 3, 0, 2)[i % 4]


def backward(i):
    return i - i % 4 + (2, 0, 3, 1)[i % 4]


def pick_kernel(start, flag, first, second, out):
    @pl.when(flag[0] == 1)
    def _():
        out[...] = first[start : start + out.shape[0], :]

    @pl.when(flag[0] != 1)
    def _():
        out[...] = second[...]


def pick(flag, first, second, start):
    vmem = pl.BlockSpec(memory_space=pltpu.VMEM)
    return pl.pallas_call(
        functools.partial(pick_kernel, start),
        in_specs=[pl.BlockSpec(memory_space=pltpu.SMEM), vmem, vmem],
        out_specs=vmem,
        out_shape=jax.ShapeDtypeStruct(second.shape, second.dtype),
        compiler_params=pltpu.CompilerParams(vmem_limit_bytes=8 * MIB),
        cost_estimate=SMALL,
        name="pick",
    )(flag, first, second)


def body(frames, counts, point_ray, channel_pair_weights, tile_bin, image):
    n_scan = lax.axis_size("scan")
    n_chan = lax.axis_size("chan")
    nx = n_chan // 2
    points = counts.shape[0]
    cells, chans = image.shape
    angles = points * n_scan // NIMG
    chan_me = lax.axis_index("chan")
    x_me, core_me = chan_me // 2, chan_me % 2
    first_row = (lax.axis_index("scan") * (cells // NIMG)).astype(jnp.int32).reshape(1)

    middle = [r for r in range(1, n_scan) if r % 2 == 0] + [1]
    late = [r for r in range(3, n_scan, 2)]
    order = [0] + middle + late
    own_rays = point_ray.reshape(points // LANES, LANES)
    rays = {r: own_rays if r == 0 else swap(own_rays, "scan", r, n_scan) for r in order}
    all_rays = jnp.concatenate([rays[r] for r in order], axis=0)

    projected = project(image, first_row, angles)
    own_share, *shares = reorder(all_rays, projected, n_scan)
    share_of = dict(zip(order[1:], shares))
    relayed = {r ^ 1: swap(share_of[r], "scan", 1, n_scan) for r in late}

    place = []
    for e in range(nx):
        xi = (x_me + e) % nx
        place += [2 * xi + 1 - core_me, 2 * xi + core_me]
    place = jnp.stack(place).astype(jnp.int32)
    send, sums = integrate(
        frames, counts, channel_pair_weights, tile_bin, place, own_share, nx, chans
    )
    keep = select(place, sums, nx, chans)
    even = sorted(relayed)
    merged = merge(sums, [share_of[r] for r in even], [relayed[r] for r in even])
    arrived = [swap(x, "scan", r, n_scan) for r, x in zip(even, merged)]
    arrived.append(swap(share_of[1], "scan", 1, n_scan))
    got = swap(send, "chan", 1, n_chan)
    pattern = keep[0] + got[0].astype(F32)
    for e in range(1, nx):
        joined = (keep[e] + got[e].astype(F32)).astype(BF16)
        pattern = pattern + rotate(joined, "chan", 2 * e, n_chan).astype(F32)

    row_total = row_totals(own_rays, sums, angles)
    scaled, recip = join(row_total, own_share, arrived)
    residual = (-scaled + pattern * (float(NIMG) * recip[:, :1])).astype(BF16)
    half = points // 2
    masks = range(0, n_scan, 4)
    gathered = {0: residual}
    bit = n_scan // 2
    while bit >= 4:
        gathered |= {mask ^ bit: swap(x, "scan", bit, n_scan) for mask, x in gathered.items()}
        bit //= 2
    scan_low = lax.axis_index("scan") % 4
    outer = jnp.logical_or(scan_low == 0, scan_low == 3)
    flag = outer.astype(jnp.int32).reshape(1)
    columns = [rays[mask] for mask in masks]
    pieces = [gathered[mask] for mask in masks if mask]
    last = []
    for mask in masks:
        block = gathered[mask]
        first = lax.ppermute(block, "scan", [(i, onward(i)) for i in range(n_scan)])
        second = [
            lax.ppermute(x, "scan", [(i, backward(i)) for i in range(n_scan)])
            for x in (block[:half], block[half:])
        ]
        pieces += [first] + second
        last += [swap(pick(flag, first, x, k * half), "scan", 1, n_scan) for k, x in enumerate(second)]
        two, one = rays[mask ^ 2], rays[mask ^ 1]
        columns += [jnp.where(outer, two, one), jnp.where(outer, one, two)]
    columns = jnp.concatenate(columns + [rays[mask ^ 3] for mask in masks], axis=0)
    tile, col_recip, partial = prepare(columns, [residual], image, first_row, angles)
    partial = add_back(pieces, points, tile, col_recip, partial)
    return back_project(last, points * (n_scan - len(masks)), tile, col_recip, partial)


def solution(mesh):
    in_specs = (
        P(("grp", "scan"), "chan"),
        P(("grp", "scan")),
        P(("grp", "scan")),
        P("chan", None, None),
        P("chan"),
        P(("grp", "scan"), "chan"),
    )
    out_specs = P(("grp", "scan"), "chan")
    return jax.shard_map(body, mesh=mesh, in_specs=in_specs, out_specs=out_specs, check_vma=False)
```

```python
import functools
import math

import jax
import jax.numpy as jnp
import numpy as np
from jax import lax
from jax.experimental import pallas as pl
from jax.experimental.pallas import tpu as pltpu
from jax.sharding import PartitionSpec as P

NIMG = 128
HALF = (NIMG - 1) / 2.0
LANES = 128
MIB = 1024 * 1024
F32 = jnp.float32
BF16 = jnp.bfloat16
SMALL = pl.CostEstimate(flops=1, bytes_accessed=1, transcendentals=0)
LARGE = pl.CostEstimate(flops=10**11, bytes_accessed=10**8, transcendentals=0)


def angle_tables(angles):
    theta = np.arange(angles, dtype=np.float32) * np.float32(math.pi / angles)
    return [float(c) for c in np.cos(theta)], [float(s) for s in np.sin(theta)]


def ray_geometry(rays, angles):
    cos_tab, sin_tab = angle_tables(angles)
    which = rays // NIMG
    offset = (rays - which * NIMG).astype(F32) - HALF
    cosine = jnp.zeros(rays.shape, F32)
    sine = jnp.zeros(rays.shape, F32)
    for a in range(angles):
        here = which == a
        cosine = jnp.where(here, cos_tab[a], cosine)
        sine = jnp.where(here, sin_tab[a], sine)
    return cosine, sine, offset


def hat(distance):
    return jnp.maximum((1.0 - jnp.abs(distance)).astype(BF16), jnp.zeros((), BF16))


def integrate_kernel(
    nx, per_chunk, tile_bin, place, after, counts, frames, weights, send, acc, *scratch
):
    member, frame_buf, weight_buf, frame_sem, weight_sem = scratch
    points, slots = member.shape
    tile_bins = acc.shape[2]
    chunks = frame_sem.shape[0]
    width = frame_buf.shape[1] // chunks
    blocks = width // LANES

    def loads(chunk):
        here = slice(chunk * width, (chunk + 1) * width)
        return (
            pltpu.make_async_copy(frames.at[:, here], frame_buf.at[:, here], frame_sem.at[chunk]),
            pltpu.make_async_copy(weights.at[here, :], weight_buf.at[here, :], weight_sem.at[chunk]),
        )

    def add(mean, block, k):
        rows = slice(block * LANES, (block + 1) * LANES)
        lanes = slice(block % blocks * LANES, (block % blocks + 1) * LANES)
        value = jnp.dot(mean[:, lanes], weight_buf[rows, :], preferred_element_type=F32)
        acc[k] += value[:, :tile_bins]
        acc[k + 1] += value[:, tile_bins:]

    for chunk in range(min(2, chunks)):
        for load in loads(chunk):
            load.start()
    acc[...] = jnp.zeros_like(acc)
    count_row = counts[...].astype(F32)
    row = lax.broadcasted_iota(jnp.int32, (points, points), 0)
    col = lax.broadcasted_iota(jnp.int32, (points, points), 1)
    ends = jnp.sum(jnp.where(col <= row, count_row, 0.0), axis=1, keepdims=True)
    count = jnp.sum(jnp.where(col == row, count_row, 0.0), axis=1, keepdims=True)
    slot = lax.broadcasted_iota(jnp.int32, (points, slots), 1).astype(F32)
    inside = jnp.logical_and(slot >= ends - count, slot < ends)
    member[...] = jnp.where(inside, 1.0 / count, 0.0).astype(BF16)

    for chunk in range(chunks):
        for load in loads(chunk):
            load.wait()
        if chunk + 2 < chunks:
            for load in loads(chunk + 2):
                load.start()
        here = slice(chunk * width, (chunk + 1) * width)
        mean = jnp.dot(member[...], frame_buf[:, here], preferred_element_type=F32).astype(BF16)
        for block in range(chunk * blocks, (chunk + 1) * blocks):
            add(mean, block, tile_bin[block])

    for e in range(nx):
        for j in range(per_chunk):
            lanes = slice(j * tile_bins, (j + 1) * tile_bins)
            send[e, :, lanes] = acc[place[2 * e] * per_chunk + j].astype(BF16)


def integrate(frames, counts, weights, tile_bin, place, after, nx, chans):
    slots, pixels = frames.shape
    points = counts.shape[0]
    nblocks, tile_pix, pair = weights.shape
    tile_bins = pair // 2
    chunks = nblocks // 16 if nblocks % 16 == 0 else nblocks
    channel_blocks = 2 * nx * chans // tile_bins
    vmem = pl.BlockSpec(memory_space=pltpu.VMEM)
    smem = pl.BlockSpec(memory_space=pltpu.SMEM)
    anywhere = pl.BlockSpec(memory_space=pl.ANY)
    return pl.pallas_call(
        functools.partial(integrate_kernel, nx, chans // tile_bins),
        in_specs=[smem, smem, anywhere, vmem, anywhere, anywhere],
        out_specs=[vmem, vmem],
        scratch_shapes=[
            pltpu.VMEM((points, slots), BF16),
            pltpu.VMEM((slots, pixels), BF16),
            pltpu.VMEM((pixels, pair), BF16),
            pltpu.SemaphoreType.DMA((chunks,)),
            pltpu.SemaphoreType.DMA((chunks,)),
        ],
        out_shape=[
            jax.ShapeDtypeStruct((nx, points, chans), BF16),
            jax.ShapeDtypeStruct((channel_blocks, points, tile_bins), F32),
        ],
        compiler_params=pltpu.CompilerParams(vmem_limit_bytes=24 * MIB),
        cost_estimate=SMALL,
        name="integrate",
    )(
        tile_bin,
        place,
        after,
        counts.reshape(1, points),
        pltpu.with_memory_space_constraint(frames, pltpu.HBM),
        pltpu.with_memory_space_constraint(weights.reshape(pixels, pair), pltpu.HBM),
    )


def select_kernel(place, acc, own, *rest):
    _, points, tile_bins = acc.shape
    per_chunk = own.shape[1] // tile_bins
    for e, keep in enumerate((own,) + rest):
        for j in range(per_chunk):
            lanes = slice(j * tile_bins, (j + 1) * tile_bins)
            keep[:, lanes] = acc[place[2 * e + 1] * per_chunk + j]


def select(place, acc, nx, chans):
    points = acc.shape[1]
    vmem = pl.BlockSpec(memory_space=pltpu.VMEM)
    return pl.pallas_call(
        select_kernel,
        in_specs=[pl.BlockSpec(memory_space=pltpu.SMEM), vmem],
        out_specs=[vmem] * nx,
        out_shape=[jax.ShapeDtypeStruct((points, chans), F32)] * nx,
        compiler_params=pltpu.CompilerParams(vmem_limit_bytes=8 * MIB),
        cost_estimate=LARGE,
        name="select",
    )(place, acc)


def row_groups(rows):
    sizes = [min(2, rows)]
    while sum(sizes) < rows:
        sizes.append(min(6, rows - sum(sizes)))
    return sizes


def project_kernel(angles, first_row, image, out, staged, base, tile_a, tile_b, total, arrived):
    cos_tab, sin_tab = angle_tables(angles)
    tiles = (tile_a, tile_b)
    sizes = row_groups(image.shape[0] // LANES)

    def cells(group):
        return slice(sum(sizes[:group]) * LANES, sum(sizes[: group + 1]) * LANES)

    def load(group):
        here = cells(group)
        return pltpu.make_async_copy(
            image.at[here, :], staged.at[here, :], arrived.at[group]
        )

    def fill(group):
        first = first_row[0] + sum(sizes[:group])
        for i in range(sizes[group]):
            upos = (first + i).astype(F32) - HALF
            lanes = slice(i * LANES, (i + 1) * LANES)
            for a in range(angles):
                here = slice(a * NIMG, (a + 1) * NIMG)
                tiles[group % 2][here, lanes] = hat(base[here, :] + upos * cos_tab[a])

    for group in range(min(2, len(sizes))):
        load(group).start()
    vpos = lax.broadcasted_iota(jnp.int32, (NIMG, LANES), 1).astype(F32) - HALF
    offset = lax.broadcasted_iota(jnp.int32, (NIMG, LANES), 0).astype(F32) - HALF
    for a in range(angles):
        base[a * NIMG : (a + 1) * NIMG, :] = sin_tab[a] * vpos - offset
    fill(0)
    for group, size in enumerate(sizes):
        if group + 1 < len(sizes):
            fill(group + 1)
        load(group).wait()
        if group + 2 < len(sizes):
            load(group + 2).start()
        product = jnp.dot(
            tiles[group % 2][:, : size * LANES],
            staged[cells(group), :].astype(BF16),
            preferred_element_type=F32,
        )
        if group == 0:
            total[...] = product
        elif group + 1 < len(sizes):
            total[...] += product
        else:
            out[...] = (total[...] + product).astype(out.dtype)


def project(image, first_row, angles):
    cells, chans = image.shape
    rays = angles * NIMG
    sizes = row_groups(cells // LANES)
    widest = max(sizes) * LANES
    vmem = pl.BlockSpec(memory_space=pltpu.VMEM)
    anywhere = pl.BlockSpec(memory_space=pl.ANY)
    return pl.pallas_call(
        functools.partial(project_kernel, angles),
        in_specs=[pl.BlockSpec(memory_space=pltpu.SMEM), anywhere],
        out_specs=vmem,
        scratch_shapes=[
            pltpu.VMEM((cells, chans), F32),
            pltpu.VMEM((rays, LANES), F32),
            pltpu.VMEM((rays, widest), BF16),
            pltpu.VMEM((rays, widest), BF16),
            pltpu.VMEM((rays, chans), F32),
            pltpu.SemaphoreType.DMA((len(sizes),)),
        ],
        out_shape=jax.ShapeDtypeStruct((rays, chans), BF16),
        compiler_params=pltpu.CompilerParams(vmem_limit_bytes=40 * MIB),
        cost_estimate=pl.CostEstimate(
            flops=4 * rays * cells * chans, bytes_accessed=4 * cells * chans, transcendentals=0
        ),
        name="project",
    )(first_row, pltpu.with_memory_space_constraint(image, pltpu.HBM))


def reorder_kernel(rays, rows, *refs):
    outs, hot = refs[:-1], refs[-1]
    all_rays = rows.shape[0]
    points = outs[0].shape[0]
    together = hot.shape[0]
    number = lax.broadcasted_iota(jnp.int32, (LANES, all_rays), 1)
    for start in range(0, len(outs) * points, together):
        for k in range(together // LANES):
            row = start // LANES + k
            wanted = jnp.transpose(jnp.broadcast_to(rays[row : row + 1, :], (LANES, LANES)))
            hot[k * LANES : (k + 1) * LANES, :] = jnp.where(number == jnp.tile(wanted, (1, all_rays // LANES)), 1.0, 0.0).astype(BF16)
        picked = jnp.dot(hot[...], rows[...], preferred_element_type=F32).astype(BF16)
        for k in range(0, together, points):
            outs[(start + k) // points][...] = picked[k : k + points, :]


def reorder(rays, rows, parts):
    all_rays, chans = rows.shape
    points = rays.shape[0] * LANES // parts
    together = points
    vmem = pl.BlockSpec(memory_space=pltpu.VMEM)
    return pl.pallas_call(
        reorder_kernel,
        in_specs=[vmem, vmem],
        out_specs=[vmem] * parts,
        scratch_shapes=[pltpu.VMEM((together, all_rays), BF16)],
        out_shape=[jax.ShapeDtypeStruct((points, chans), BF16)] * parts,
        compiler_params=pltpu.CompilerParams(vmem_limit_bytes=16 * MIB),
        cost_estimate=SMALL,
        name="reorder",
    )(rays, rows)


def merge_kernel(count, after, *refs):
    for own, other, out in zip(refs[:count], refs[count : 2 * count], refs[2 * count :]):
        out[...] = (own[...].astype(F32) + other[...].astype(F32)).astype(BF16)


def merge(after, shares, received):
    count = len(shares)
    vmem = pl.BlockSpec(memory_space=pltpu.VMEM)
    return pl.pallas_call(
        functools.partial(merge_kernel, count),
        in_specs=[pl.BlockSpec(memory_space=pl.ANY)] + [vmem] * (2 * count),
        out_specs=[vmem] * count,
        out_shape=[jax.ShapeDtypeStruct(x.shape, BF16) for x in shares],
        compiler_params=pltpu.CompilerParams(vmem_limit_bytes=8 * MIB),
        cost_estimate=SMALL,
        name="merge",
    )(after, *shares, *received)


def row_total_kernel(angles, after, rays, row_total):
    cos_r, sin_r, off_r = ray_geometry(rays[...], angles)
    line = lax.broadcasted_iota(jnp.int32, (LANES, LANES), 0).astype(F32) - HALF
    for k in range(rays.shape[0]):
        cosine, sine, offset = (x[k : k + 1, :] for x in (cos_r, sin_r, off_r))
        along_u = jnp.abs(cosine) >= jnp.abs(sine)
        steep = jnp.where(along_u, cosine, sine)
        flat = jnp.where(along_u, sine, cosine)
        crossing = jnp.floor((offset - flat * line) / steep + HALF)
        sums = jnp.zeros((LANES, LANES), F32)
        for near in range(-1, 3):
            cell = crossing + float(near)
            weight = hat(flat * line + steep * (cell - HALF) - offset).astype(F32)
            inside = jnp.logical_and(cell >= 0.0, cell <= NIMG - 1.0)
            sums += jnp.where(inside, weight, 0.0)
        total = jnp.sum(sums, axis=0, keepdims=True)
        row_total[k * LANES : (k + 1) * LANES, :] = jnp.transpose(
            jnp.broadcast_to(total, (LANES, LANES))
        )


def row_totals(rays, after, angles):
    points = rays.shape[0] * LANES
    vmem = pl.BlockSpec(memory_space=pltpu.VMEM)
    return pl.pallas_call(
        functools.partial(row_total_kernel, angles),
        in_specs=[pl.BlockSpec(memory_space=pl.ANY), vmem],
        out_specs=vmem,
        out_shape=jax.ShapeDtypeStruct((points, LANES), F32),
        compiler_params=pltpu.CompilerParams(vmem_limit_bytes=8 * MIB),
        cost_estimate=SMALL,
        name="row_totals",
    )(after, rays)


def join_kernel(row_total, own, *refs):
    arrived, (scaled, recip) = refs[:-2], refs[-2:]
    total = own[...].astype(F32)
    for part in arrived:
        total += part[...].astype(F32)
    recip[...] = 1.0 / row_total[...]
    for j in range(own.shape[1] // LANES):
        lanes = slice(j * LANES, (j + 1) * LANES)
        scaled[:, lanes] = total[:, lanes] * recip[...]


def join(row_total, own, arrived):
    vmem = pl.BlockSpec(memory_space=pltpu.VMEM)
    return pl.pallas_call(
        join_kernel,
        in_specs=[vmem] * (2 + len(arrived)),
        out_specs=[vmem, vmem],
        out_shape=[
            jax.ShapeDtypeStruct(own.shape, F32),
            jax.ShapeDtypeStruct(row_total.shape, F32),
        ],
        compiler_params=pltpu.CompilerParams(vmem_limit_bytes=8 * MIB),
        cost_estimate=LARGE,
        name="join",
    )(row_total, own, *arrived)


def prepare_kernel(angles, early, first_row, rays, *refs):
    residuals, (image, tile, recip, partial, base, cosine) = refs[:early], refs[early:]
    step = pl.program_id(0)
    chunks = rays.shape[0]
    chans = image.shape[1]
    rows = tile.shape[0] // LANES

    @pl.when(step == 0)
    def _():
        cos_c, sin_c, off_c = ray_geometry(rays[...], angles)
        cosine[...] = cos_c
        vpos = lax.broadcasted_iota(jnp.int32, (LANES, LANES), 0).astype(F32) - HALF
        for k in range(chunks):
            base[:, k * LANES : (k + 1) * LANES] = sin_c[k : k + 1, :] * vpos - off_c[k : k + 1, :]

    for i in range(rows):
        here = slice(i * LANES, (i + 1) * LANES)
        upos = (first_row[0] + step * rows + i).astype(F32) - HALF
        sums = jnp.zeros((LANES, LANES), F32)
        for k in range(chunks):
            lanes = slice(k * LANES, (k + 1) * LANES)
            value = hat(base[:, lanes] + cosine[k : k + 1, :] * upos)
            tile[here, lanes] = value
            sums += value.astype(F32)
        total = jnp.sum(sums, axis=1, keepdims=True)
        recip[here, :] = jnp.broadcast_to(1.0 / total, (LANES, LANES))
    joined = jnp.concatenate([r[...] for r in residuals], axis=0)
    back = jnp.dot(tile[:, : joined.shape[0]], joined, preferred_element_type=F32)
    for j in range(chans // LANES):
        lanes = slice(j * LANES, (j + 1) * LANES)
        partial[:, lanes] = image[:, lanes] + back[:, lanes] * recip[...]


def prepare(rays, residuals, image, first_row, angles):
    cells, chans = image.shape
    all_points = rays.shape[0] * LANES
    rows = min(4, cells // LANES)
    fixed = lambda shape: pl.BlockSpec(shape, lambda i, *_: (0, 0))
    sliding = lambda width: pl.BlockSpec((rows * LANES, width), lambda i, *_: (i, 0))
    return pl.pallas_call(
        functools.partial(prepare_kernel, angles, len(residuals)),
        grid_spec=pltpu.PrefetchScalarGridSpec(
            num_scalar_prefetch=1,
            grid=(cells // (rows * LANES),),
            in_specs=[fixed(rays.shape)]
            + [fixed(r.shape) for r in residuals]
            + [sliding(chans)],
            out_specs=[sliding(all_points), sliding(LANES), sliding(chans)],
            scratch_shapes=[pltpu.VMEM((LANES, all_points), F32), pltpu.VMEM(rays.shape, F32)],
        ),
        out_shape=[
            jax.ShapeDtypeStruct((cells, all_points), BF16),
            jax.ShapeDtypeStruct((cells, LANES), F32),
            jax.ShapeDtypeStruct((cells, chans), F32),
        ],
        compiler_params=pltpu.CompilerParams(vmem_limit_bytes=16 * MIB),
        cost_estimate=SMALL,
        name="prepare",
    )(first_row, rays, *residuals, pltpu.with_memory_space_constraint(image, pltpu.HBM))


def gather_rows(pieces, joined):
    start = 0
    for piece in pieces:
        joined[start : start + piece.shape[0], :] = piece[...]
        start += piece.shape[0]


def add_share(here, first, tile, recip, partial, joined, out):
    columns = slice(first, first + joined.shape[0])
    back = jnp.dot(tile[here, columns], joined[...], preferred_element_type=F32)
    scale = recip[here, :]
    for j in range(out.shape[1] // LANES):
        lanes = slice(j * LANES, (j + 1) * LANES)
        out[here, lanes] = partial[here, lanes] + back[:, lanes] * scale


def add_kernel(first, count, *refs):
    pieces, (tile, recip, partial, out, joined) = refs[:count], refs[count:]
    gather_rows(pieces, joined)
    rows = min(512, out.shape[0])
    for start in range(0, out.shape[0], rows):
        add_share(slice(start, start + rows), first, tile, recip, partial, joined, out)


def add_back(pieces, first, tile, recip, partial):
    cells, chans = partial.shape
    vmem = pl.BlockSpec(memory_space=pltpu.VMEM)
    return pl.pallas_call(
        functools.partial(add_kernel, first, len(pieces)),
        in_specs=[vmem] * (len(pieces) + 3),
        out_specs=vmem,
        scratch_shapes=[pltpu.VMEM((sum(x.shape[0] for x in pieces), chans), BF16)],
        out_shape=jax.ShapeDtypeStruct((cells, chans), F32),
        compiler_params=pltpu.CompilerParams(vmem_limit_bytes=8 * MIB),
        cost_estimate=LARGE,
        name="add_back",
    )(*pieces, tile, recip, partial)


def back_kernel(first, count, *refs):
    pieces, (tile, recip, partial, out, joined, staged, sent) = refs[:count], refs[count:]
    chunks = sent.shape[0]
    rows = out.shape[0] // chunks
    gather_rows(pieces, joined)
    copies = []
    for chunk in range(chunks):
        here = slice(chunk * rows, (chunk + 1) * rows)
        add_share(here, first, tile, recip, partial, joined, staged)
        copies.append(
            pltpu.make_async_copy(staged.at[here, :], out.at[here, :], sent.at[chunk])
        )
        copies[-1].start()
    for copy in copies:
        copy.wait()


def back_project(pieces, first, tile, recip, partial):
    cells, chans = partial.shape
    chunks = max(1, cells // 512)
    vmem = pl.BlockSpec(memory_space=pltpu.VMEM)
    return pl.pallas_call(
        functools.partial(back_kernel, first, len(pieces)),
        in_specs=[vmem] * (len(pieces) + 3),
        out_specs=pl.BlockSpec(memory_space=pl.ANY),
        scratch_shapes=[
            pltpu.VMEM((sum(x.shape[0] for x in pieces), chans), BF16),
            pltpu.VMEM((cells, chans), F32),
            pltpu.SemaphoreType.DMA((chunks,)),
        ],
        out_shape=jax.ShapeDtypeStruct((cells, chans), F32),
        compiler_params=pltpu.CompilerParams(vmem_limit_bytes=16 * MIB),
        cost_estimate=SMALL,
        name="back_project",
    )(*pieces, tile, recip, partial)


def rotate(x, axis, shift, n):
    return lax.ppermute(x, axis, [(i, (i + shift) % n) for i in range(n)])


def swap(x, axis, mask, n):
    return lax.ppermute(x, axis, [(i, i ^ mask) for i in range(n)])


def onward(i):
    return i - i % 4 + (1, 3, 0, 2)[i % 4]


def backward(i):
    return i - i % 4 + (2, 0, 3, 1)[i % 4]


def pick_kernel(start, flag, first, second, out):
    @pl.when(flag[0] == 1)
    def _():
        out[...] = first[start : start + out.shape[0], :]

    @pl.when(flag[0] != 1)
    def _():
        out[...] = second[...]


def pick(flag, first, second, start):
    vmem = pl.BlockSpec(memory_space=pltpu.VMEM)
    return pl.pallas_call(
        functools.partial(pick_kernel, start),
        in_specs=[pl.BlockSpec(memory_space=pltpu.SMEM), vmem, vmem],
        out_specs=vmem,
        out_shape=jax.ShapeDtypeStruct(second.shape, second.dtype),
        compiler_params=pltpu.CompilerParams(vmem_limit_bytes=8 * MIB),
        cost_estimate=SMALL,
        name="pick",
    )(flag, first, second)


def body(frames, counts, point_ray, channel_pair_weights, tile_bin, image):
    n_scan = lax.axis_size("scan")
    n_chan = lax.axis_size("chan")
    nx = n_chan // 2
    points = counts.shape[0]
    cells, chans = image.shape
    angles = points * n_scan // NIMG
    chan_me = lax.axis_index("chan")
    x_me, core_me = chan_me // 2, chan_me % 2
    first_row = (lax.axis_index("scan") * (cells // NIMG)).astype(jnp.int32).reshape(1)

    middle = [r for r in range(1, n_scan) if r % 2 == 0] + [1]
    late = [r for r in range(3, n_scan, 2)]
    order = [0] + middle + late
    own_rays = point_ray.reshape(points // LANES, LANES)
    rays = {r: own_rays if r == 0 else swap(own_rays, "scan", r, n_scan) for r in order}
    all_rays = jnp.concatenate([rays[r] for r in order], axis=0)

    projected = project(image, first_row, angles)
    own_share, *shares = reorder(all_rays, projected, n_scan)
    share_of = dict(zip(order[1:], shares))
    relayed = {r ^ 1: swap(share_of[r], "scan", 1, n_scan) for r in late}

    place = []
    for e in range(nx):
        xi = (x_me + e) % nx
        place += [2 * xi + 1 - core_me, 2 * xi + core_me]
    place = jnp.stack(place).astype(jnp.int32)
    send, sums = integrate(
        frames, counts, channel_pair_weights, tile_bin, place, own_share, nx, chans
    )
    keep = select(place, sums, nx, chans)
    even = sorted(relayed)
    merged = merge(sums, [share_of[r] for r in even], [relayed[r] for r in even])
    arrived = [swap(x, "scan", r, n_scan) for r, x in zip(even, merged)]
    arrived.append(swap(share_of[1], "scan", 1, n_scan))
    got = swap(send, "chan", 1, n_chan)
    pattern = keep[0] + got[0].astype(F32)
    for e in range(1, nx):
        joined = (keep[e] + got[e].astype(F32)).astype(BF16)
        pattern = pattern + rotate(joined, "chan", 2 * e, n_chan).astype(F32)

    row_total = row_totals(own_rays, sums, angles)
    scaled, recip = join(row_total, own_share, arrived)
    residual = (-scaled + pattern * (float(NIMG) * recip[:, :1])).astype(BF16)
    half = points // 2
    masks = range(0, n_scan, 4)
    gathered = {0: residual}
    bit = n_scan // 2
    while bit >= 4:
        gathered |= {mask ^ bit: swap(x, "scan", bit, n_scan) for mask, x in gathered.items()}
        bit //= 2
    scan_low = lax.axis_index("scan") % 4
    outer = jnp.logical_or(scan_low == 0, scan_low == 3)
    flag = outer.astype(jnp.int32).reshape(1)
    columns = [rays[mask] for mask in masks]
    pieces = [gathered[mask] for mask in masks if mask]
    last = []
    for mask in masks:
        block = gathered[mask]
        first = lax.ppermute(block, "scan", [(i, onward(i)) for i in range(n_scan)])
        second = [
            lax.ppermute(x, "scan", [(i, backward(i)) for i in range(n_scan)])
            for x in (block[:half], block[half:])
        ]
        pieces += [first] + second
        last += [swap(pick(flag, first, x, k * half), "scan", 1, n_scan) for k, x in enumerate(second)]
        two, one = rays[mask ^ 2], rays[mask ^ 1]
        columns += [jnp.where(outer, two, one), jnp.where(outer, one, two)]
    columns = jnp.concatenate(columns + [rays[mask ^ 3] for mask in masks], axis=0)
    tile, col_recip, partial = prepare(columns, [residual], image, first_row, angles)
    partial = add_back(pieces, points, tile, col_recip, partial)
    return back_project(last, points * (n_scan - len(masks)), tile, col_recip, partial)


def solution(mesh):
    in_specs = (
        P(("grp", "scan"), "chan"),
        P(("grp", "scan")),
        P(("grp", "scan")),
        P("chan", None, None),
        P("chan"),
        P(("grp", "scan"), "chan"),
    )
    out_specs = P(("grp", "scan"), "chan")
    return jax.shard_map(body, mesh=mesh, in_specs=in_specs, out_specs=out_specs, check_vma=False)
```

```python
import functools
import math

import jax
import jax.numpy as jnp
import numpy as np
from jax import lax
from jax.experimental import pallas as pl
from jax.experimental.pallas import tpu as pltpu
from jax.sharding import PartitionSpec as P

NIMG = 128
HALF = (NIMG - 1) / 2.0
LANES = 128
MIB = 1024 * 1024
F32 = jnp.float32
BF16 = jnp.bfloat16
SMALL = pl.CostEstimate(flops=1, bytes_accessed=1, transcendentals=0)
LARGE = pl.CostEstimate(flops=10**11, bytes_accessed=10**8, transcendentals=0)


def angle_tables(angles):
    theta = np.arange(angles, dtype=np.float32) * np.float32(math.pi / angles)
    return [float(c) for c in np.cos(theta)], [float(s) for s in np.sin(theta)]


def ray_geometry(rays, angles):
    cos_tab, sin_tab = angle_tables(angles)
    which = rays // NIMG
    offset = (rays - which * NIMG).astype(F32) - HALF
    cosine = jnp.zeros(rays.shape, F32)
    sine = jnp.zeros(rays.shape, F32)
    for a in range(angles):
        here = which == a
        cosine = jnp.where(here, cos_tab[a], cosine)
        sine = jnp.where(here, sin_tab[a], sine)
    return cosine, sine, offset


def hat(distance):
    return jnp.maximum((1.0 - jnp.abs(distance)).astype(BF16), jnp.zeros((), BF16))


def integrate_kernel(
    nx, per_chunk, tile_bin, place, after, counts, frames, weights, send, acc, *scratch
):
    member, frame_buf, weight_buf, frame_sem, weight_sem = scratch
    points, slots = member.shape
    tile_bins = acc.shape[2]
    chunks = frame_sem.shape[0]
    width = frame_buf.shape[1] // chunks
    blocks = width // LANES

    def loads(chunk):
        here = slice(chunk * width, (chunk + 1) * width)
        return (
            pltpu.make_async_copy(frames.at[:, here], frame_buf.at[:, here], frame_sem.at[chunk]),
            pltpu.make_async_copy(weights.at[here, :], weight_buf.at[here, :], weight_sem.at[chunk]),
        )

    def add(mean, block, k):
        rows = slice(block * LANES, (block + 1) * LANES)
        lanes = slice(block % blocks * LANES, (block % blocks + 1) * LANES)
        value = jnp.dot(mean[:, lanes], weight_buf[rows, :], preferred_element_type=F32)
        acc[k] += value[:, :tile_bins]
        acc[k + 1] += value[:, tile_bins:]

    for chunk in range(min(2, chunks)):
        for load in loads(chunk):
            load.start()
    acc[...] = jnp.zeros_like(acc)
    count_row = counts[...].astype(F32)
    row = lax.broadcasted_iota(jnp.int32, (points, points), 0)
    col = lax.broadcasted_iota(jnp.int32, (points, points), 1)
    ends = jnp.sum(jnp.where(col <= row, count_row, 0.0), axis=1, keepdims=True)
    count = jnp.sum(jnp.where(col == row, count_row, 0.0), axis=1, keepdims=True)
    slot = lax.broadcasted_iota(jnp.int32, (points, slots), 1).astype(F32)
    inside = jnp.logical_and(slot >= ends - count, slot < ends)
    member[...] = jnp.where(inside, 1.0 / count, 0.0).astype(BF16)

    for chunk in range(chunks):
        for load in loads(chunk):
            load.wait()
        if chunk + 2 < chunks:
            for load in loads(chunk + 2):
                load.start()
        here = slice(chunk * width, (chunk + 1) * width)
        mean = jnp.dot(member[...], frame_buf[:, here], preferred_element_type=F32).astype(BF16)
        for block in range(chunk * blocks, (chunk + 1) * blocks):
            add(mean, block, tile_bin[block])

    for e in range(nx):
        for j in range(per_chunk):
            lanes = slice(j * tile_bins, (j + 1) * tile_bins)
            send[e, :, lanes] = acc[place[2 * e] * per_chunk + j].astype(BF16)


def integrate(frames, counts, weights, tile_bin, place, after, nx, chans):
    slots, pixels = frames.shape
    points = counts.shape[0]
    nblocks, tile_pix, pair = weights.shape
    tile_bins = pair // 2
    chunks = nblocks // 16 if nblocks % 16 == 0 else nblocks
    channel_blocks = 2 * nx * chans // tile_bins
    vmem = pl.BlockSpec(memory_space=pltpu.VMEM)
    smem = pl.BlockSpec(memory_space=pltpu.SMEM)
    anywhere = pl.BlockSpec(memory_space=pl.ANY)
    return pl.pallas_call(
        functools.partial(integrate_kernel, nx, chans // tile_bins),
        in_specs=[smem, smem, anywhere, vmem, anywhere, anywhere],
        out_specs=[vmem, vmem],
        scratch_shapes=[
            pltpu.VMEM((points, slots), BF16),
            pltpu.VMEM((slots, pixels), BF16),
            pltpu.VMEM((pixels, pair), BF16),
            pltpu.SemaphoreType.DMA((chunks,)),
            pltpu.SemaphoreType.DMA((chunks,)),
        ],
        out_shape=[
            jax.ShapeDtypeStruct((nx, points, chans), BF16),
            jax.ShapeDtypeStruct((channel_blocks, points, tile_bins), F32),
        ],
        compiler_params=pltpu.CompilerParams(vmem_limit_bytes=24 * MIB),
        cost_estimate=SMALL,
        name="integrate",
    )(
        tile_bin,
        place,
        after,
        counts.reshape(1, points),
        pltpu.with_memory_space_constraint(frames, pltpu.HBM),
        pltpu.with_memory_space_constraint(weights.reshape(pixels, pair), pltpu.HBM),
    )


def select_kernel(place, acc, own, *rest):
    _, points, tile_bins = acc.shape
    per_chunk = own.shape[1] // tile_bins
    for e, keep in enumerate((own,) + rest):
        for j in range(per_chunk):
            lanes = slice(j * tile_bins, (j + 1) * tile_bins)
            keep[:, lanes] = acc[place[2 * e + 1] * per_chunk + j]


def select(place, acc, nx, chans):
    points = acc.shape[1]
    vmem = pl.BlockSpec(memory_space=pltpu.VMEM)
    return pl.pallas_call(
        select_kernel,
        in_specs=[pl.BlockSpec(memory_space=pltpu.SMEM), vmem],
        out_specs=[vmem] * nx,
        out_shape=[jax.ShapeDtypeStruct((points, chans), F32)] * nx,
        compiler_params=pltpu.CompilerParams(vmem_limit_bytes=8 * MIB),
        cost_estimate=LARGE,
        name="select",
    )(place, acc)


def row_groups(rows):
    sizes = [min(2, rows)]
    while sum(sizes) < rows:
        sizes.append(min(6, rows - sum(sizes)))
    return sizes


def project_kernel(angles, first_row, image, out, staged, base, tile_a, tile_b, total, arrived):
    cos_tab, sin_tab = angle_tables(angles)
    tiles = (tile_a, tile_b)
    sizes = row_groups(image.shape[0] // LANES)

    def cells(group):
        return slice(sum(sizes[:group]) * LANES, sum(sizes[: group + 1]) * LANES)

    def load(group):
        here = cells(group)
        return pltpu.make_async_copy(
            image.at[here, :], staged.at[here, :], arrived.at[group]
        )

    def fill(group):
        first = first_row[0] + sum(sizes[:group])
        for i in range(sizes[group]):
            upos = (first + i).astype(F32) - HALF
            lanes = slice(i * LANES, (i + 1) * LANES)
            for a in range(angles):
                here = slice(a * NIMG, (a + 1) * NIMG)
                tiles[group % 2][here, lanes] = hat(base[here, :] + upos * cos_tab[a])

    for group in range(min(2, len(sizes))):
        load(group).start()
    vpos = lax.broadcasted_iota(jnp.int32, (NIMG, LANES), 1).astype(F32) - HALF
    offset = lax.broadcasted_iota(jnp.int32, (NIMG, LANES), 0).astype(F32) - HALF
    for a in range(angles):
        base[a * NIMG : (a + 1) * NIMG, :] = sin_tab[a] * vpos - offset
    fill(0)
    for group, size in enumerate(sizes):
        if group + 1 < len(sizes):
            fill(group + 1)
        load(group).wait()
        if group + 2 < len(sizes):
            load(group + 2).start()
        product = jnp.dot(
            tiles[group % 2][:, : size * LANES],
            staged[cells(group), :].astype(BF16),
            preferred_element_type=F32,
        )
        if group == 0:
            total[...] = product
        elif group + 1 < len(sizes):
            total[...] += product
        else:
            out[...] = (total[...] + product).astype(out.dtype)


def project(image, first_row, angles):
    cells, chans = image.shape
    rays = angles * NIMG
    sizes = row_groups(cells // LANES)
    widest = max(sizes) * LANES
    vmem = pl.BlockSpec(memory_space=pltpu.VMEM)
    anywhere = pl.BlockSpec(memory_space=pl.ANY)
    return pl.pallas_call(
        functools.partial(project_kernel, angles),
        in_specs=[pl.BlockSpec(memory_space=pltpu.SMEM), anywhere],
        out_specs=[vmem, vmem],
        scratch_shapes=[
            pltpu.VMEM((rays, LANES), F32),
            pltpu.VMEM((rays, widest), BF16),
            pltpu.VMEM((rays, widest), BF16),
            pltpu.VMEM((rays, chans), F32),
            pltpu.SemaphoreType.DMA((len(sizes),)),
        ],
        out_shape=[
            jax.ShapeDtypeStruct((rays, chans), BF16),
            jax.ShapeDtypeStruct((cells, chans), F32),
        ],
        compiler_params=pltpu.CompilerParams(vmem_limit_bytes=32 * MIB),
        cost_estimate=pl.CostEstimate(
            flops=4 * rays * cells * chans, bytes_accessed=4 * cells * chans, transcendentals=0
        ),
        name="project",
    )(first_row, pltpu.with_memory_space_constraint(image, pltpu.HBM))


def reorder_kernel(rays, rows, *refs):
    outs, hot = refs[:-1], refs[-1]
    all_rays = rows.shape[0]
    points = outs[0].shape[0]
    together = hot.shape[0]
    number = lax.broadcasted_iota(jnp.int32, (LANES, all_rays), 1)
    for start in range(0, len(outs) * points, together):
        for k in range(together // LANES):
            row = start // LANES + k
            wanted = jnp.transpose(jnp.broadcast_to(rays[row : row + 1, :], (LANES, LANES)))
            hot[k * LANES : (k + 1) * LANES, :] = jnp.where(number == jnp.tile(wanted, (1, all_rays // LANES)), 1.0, 0.0).astype(BF16)
        picked = jnp.dot(hot[...], rows[...], preferred_element_type=F32).astype(BF16)
        for k in range(0, together, points):
            outs[(start + k) // points][...] = picked[k : k + points, :]


def reorder(rays, rows, parts):
    all_rays, chans = rows.shape
    points = rays.shape[0] * LANES // parts
    together = points
    vmem = pl.BlockSpec(memory_space=pltpu.VMEM)
    return pl.pallas_call(
        reorder_kernel,
        in_specs=[vmem, vmem],
        out_specs=[vmem] * parts,
        scratch_shapes=[pltpu.VMEM((together, all_rays), BF16)],
        out_shape=[jax.ShapeDtypeStruct((points, chans), BF16)] * parts,
        compiler_params=pltpu.CompilerParams(vmem_limit_bytes=16 * MIB),
        cost_estimate=SMALL,
        name="reorder",
    )(rays, rows)


def merge_kernel(count, after, *refs):
    for own, other, out in zip(refs[:count], refs[count : 2 * count], refs[2 * count :]):
        out[...] = (own[...].astype(F32) + other[...].astype(F32)).astype(BF16)


def merge(after, shares, received):
    count = len(shares)
    vmem = pl.BlockSpec(memory_space=pltpu.VMEM)
    return pl.pallas_call(
        functools.partial(merge_kernel, count),
        in_specs=[pl.BlockSpec(memory_space=pl.ANY)] + [vmem] * (2 * count),
        out_specs=[vmem] * count,
        out_shape=[jax.ShapeDtypeStruct(x.shape, BF16) for x in shares],
        compiler_params=pltpu.CompilerParams(vmem_limit_bytes=8 * MIB),
        cost_estimate=SMALL,
        name="merge",
    )(after, *shares, *received)


def row_total_kernel(angles, after, rays, row_total):
    cos_r, sin_r, off_r = ray_geometry(rays[...], angles)
    line = lax.broadcasted_iota(jnp.int32, (LANES, LANES), 0).astype(F32) - HALF
    for k in range(rays.shape[0]):
        cosine, sine, offset = (x[k : k + 1, :] for x in (cos_r, sin_r, off_r))
        along_u = jnp.abs(cosine) >= jnp.abs(sine)
        steep = jnp.where(along_u, cosine, sine)
        flat = jnp.where(along_u, sine, cosine)
        crossing = jnp.floor((offset - flat * line) / steep + HALF)
        sums = jnp.zeros((LANES, LANES), F32)
        for near in range(-1, 3):
            cell = crossing + float(near)
            weight = hat(flat * line + steep * (cell - HALF) - offset).astype(F32)
            inside = jnp.logical_and(cell >= 0.0, cell <= NIMG - 1.0)
            sums += jnp.where(inside, weight, 0.0)
        total = jnp.sum(sums, axis=0, keepdims=True)
        row_total[k * LANES : (k + 1) * LANES, :] = jnp.transpose(
            jnp.broadcast_to(total, (LANES, LANES))
        )


def row_totals(rays, after, angles):
    points = rays.shape[0] * LANES
    vmem = pl.BlockSpec(memory_space=pltpu.VMEM)
    return pl.pallas_call(
        functools.partial(row_total_kernel, angles),
        in_specs=[pl.BlockSpec(memory_space=pl.ANY), vmem],
        out_specs=vmem,
        out_shape=jax.ShapeDtypeStruct((points, LANES), F32),
        compiler_params=pltpu.CompilerParams(vmem_limit_bytes=8 * MIB),
        cost_estimate=SMALL,
        name="row_totals",
    )(after, rays)


def join_kernel(row_total, own, *refs):
    arrived, (scaled, recip) = refs[:-2], refs[-2:]
    total = own[...].astype(F32)
    for part in arrived:
        total += part[...].astype(F32)
    recip[...] = 1.0 / row_total[...]
    for j in range(own.shape[1] // LANES):
        lanes = slice(j * LANES, (j + 1) * LANES)
        scaled[:, lanes] = total[:, lanes] * recip[...]


def join(row_total, own, arrived):
    vmem = pl.BlockSpec(memory_space=pltpu.VMEM)
    return pl.pallas_call(
        join_kernel,
        in_specs=[vmem] * (2 + len(arrived)),
        out_specs=[vmem, vmem],
        out_shape=[
            jax.ShapeDtypeStruct(own.shape, F32),
            jax.ShapeDtypeStruct(row_total.shape, F32),
        ],
        compiler_params=pltpu.CompilerParams(vmem_limit_bytes=8 * MIB),
        cost_estimate=LARGE,
        name="join",
    )(row_total, own, *arrived)


def prepare_kernel(angles, early, first_row, rays, *refs):
    residuals, (image, tile, recip, partial, base, cosine) = refs[:early], refs[early:]
    step = pl.program_id(0)
    chunks = rays.shape[0]
    chans = image.shape[1]
    rows = tile.shape[0] // LANES

    @pl.when(step == 0)
    def _():
        cos_c, sin_c, off_c = ray_geometry(rays[...], angles)
        cosine[...] = cos_c
        vpos = lax.broadcasted_iota(jnp.int32, (LANES, LANES), 0).astype(F32) - HALF
        for k in range(chunks):
            base[:, k * LANES : (k + 1) * LANES] = sin_c[k : k + 1, :] * vpos - off_c[k : k + 1, :]

    for i in range(rows):
        here = slice(i * LANES, (i + 1) * LANES)
        upos = (first_row[0] + step * rows + i).astype(F32) - HALF
        sums = jnp.zeros((LANES, LANES), F32)
        for k in range(chunks):
            lanes = slice(k * LANES, (k + 1) * LANES)
            value = hat(base[:, lanes] + cosine[k : k + 1, :] * upos)
            tile[here, lanes] = value
            sums += value.astype(F32)
        total = jnp.sum(sums, axis=1, keepdims=True)
        recip[here, :] = jnp.broadcast_to(1.0 / total, (LANES, LANES))
    joined = jnp.concatenate([r[...] for r in residuals], axis=0)
    back = jnp.dot(tile[:, : joined.shape[0]], joined, preferred_element_type=F32)
    for j in range(chans // LANES):
        lanes = slice(j * LANES, (j + 1) * LANES)
        partial[:, lanes] = image[:, lanes] + back[:, lanes] * recip[...]


def prepare(rays, residuals, image, first_row, angles):
    cells, chans = image.shape
    all_points = rays.shape[0] * LANES
    rows = min(4, cells // LANES)
    fixed = lambda shape: pl.BlockSpec(shape, lambda i, *_: (0, 0))
    sliding = lambda width: pl.BlockSpec((rows * LANES, width), lambda i, *_: (i, 0))
    return pl.pallas_call(
        functools.partial(prepare_kernel, angles, len(residuals)),
        grid_spec=pltpu.PrefetchScalarGridSpec(
            num_scalar_prefetch=1,
            grid=(cells // (rows * LANES),),
            in_specs=[fixed(rays.shape)]
            + [fixed(r.shape) for r in residuals]
            + [sliding(chans)],
            out_specs=[sliding(all_points), sliding(LANES), sliding(chans)],
            scratch_shapes=[pltpu.VMEM((LANES, all_points), F32), pltpu.VMEM(rays.shape, F32)],
        ),
        out_shape=[
            jax.ShapeDtypeStruct((cells, all_points), BF16),
            jax.ShapeDtypeStruct((cells, LANES), F32),
            jax.ShapeDtypeStruct((cells, chans), F32),
        ],
        compiler_params=pltpu.CompilerParams(vmem_limit_bytes=16 * MIB),
        cost_estimate=SMALL,
        name="prepare",
    )(first_row, rays, *residuals, image)


def gather_rows(pieces, joined):
    start = 0
    for piece in pieces:
        joined[start : start + piece.shape[0], :] = piece[...]
        start += piece.shape[0]


def add_share(here, first, tile, recip, partial, joined, out):
    columns = slice(first, first + joined.shape[0])
    back = jnp.dot(tile[here, columns], joined[...], preferred_element_type=F32)
    scale = recip[here, :]
    for j in range(out.shape[1] // LANES):
        lanes = slice(j * LANES, (j + 1) * LANES)
        out[here, lanes] = partial[here, lanes] + back[:, lanes] * scale


def add_kernel(first, count, *refs):
    pieces, (tile, recip, partial, out, joined) = refs[:count], refs[count:]
    gather_rows(pieces, joined)
    rows = min(512, out.shape[0])
    for start in range(0, out.shape[0], rows):
        add_share(slice(start, start + rows), first, tile, recip, partial, joined, out)


def add_back(pieces, first, tile, recip, partial):
    cells, chans = partial.shape
    vmem = pl.BlockSpec(memory_space=pltpu.VMEM)
    return pl.pallas_call(
        functools.partial(add_kernel, first, len(pieces)),
        in_specs=[vmem] * (len(pieces) + 3),
        out_specs=vmem,
        scratch_shapes=[pltpu.VMEM((sum(x.shape[0] for x in pieces), chans), BF16)],
        out_shape=jax.ShapeDtypeStruct((cells, chans), F32),
        compiler_params=pltpu.CompilerParams(vmem_limit_bytes=8 * MIB),
        cost_estimate=LARGE,
        name="add_back",
    )(*pieces, tile, recip, partial)


def back_kernel(first, count, *refs):
    pieces, (tile, recip, partial, out, joined, staged, sent) = refs[:count], refs[count:]
    chunks = sent.shape[0]
    rows = out.shape[0] // chunks
    gather_rows(pieces, joined)
    copies = []
    for chunk in range(chunks):
        here = slice(chunk * rows, (chunk + 1) * rows)
        add_share(here, first, tile, recip, partial, joined, staged)
        copies.append(
            pltpu.make_async_copy(staged.at[here, :], out.at[here, :], sent.at[chunk])
        )
        copies[-1].start()
    for copy in copies:
        copy.wait()


def back_project(pieces, first, tile, recip, partial):
    cells, chans = partial.shape
    chunks = max(1, cells // 512)
    vmem = pl.BlockSpec(memory_space=pltpu.VMEM)
    return pl.pallas_call(
        functools.partial(back_kernel, first, len(pieces)),
        in_specs=[vmem] * (len(pieces) + 3),
        out_specs=pl.BlockSpec(memory_space=pl.ANY),
        scratch_shapes=[
            pltpu.VMEM((sum(x.shape[0] for x in pieces), chans), BF16),
            pltpu.VMEM((cells, chans), F32),
            pltpu.SemaphoreType.DMA((chunks,)),
        ],
        out_shape=jax.ShapeDtypeStruct((cells, chans), F32),
        compiler_params=pltpu.CompilerParams(vmem_limit_bytes=16 * MIB),
        cost_estimate=SMALL,
        name="back_project",
    )(*pieces, tile, recip, partial)


def rotate(x, axis, shift, n):
    return lax.ppermute(x, axis, [(i, (i + shift) % n) for i in range(n)])


def swap(x, axis, mask, n):
    return lax.ppermute(x, axis, [(i, i ^ mask) for i in range(n)])


def onward(i):
    return i - i % 4 + (1, 3, 0, 2)[i % 4]


def backward(i):
    return i - i % 4 + (2, 0, 3, 1)[i % 4]


def pick_kernel(start, flag, first, second, out):
    @pl.when(flag[0] == 1)
    def _():
        out[...] = first[start : start + out.shape[0], :]

    @pl.when(flag[0] != 1)
    def _():
        out[...] = second[...]


def pick(flag, first, second, start):
    vmem = pl.BlockSpec(memory_space=pltpu.VMEM)
    return pl.pallas_call(
        functools.partial(pick_kernel, start),
        in_specs=[pl.BlockSpec(memory_space=pltpu.SMEM), vmem, vmem],
        out_specs=vmem,
        out_shape=jax.ShapeDtypeStruct(second.shape, second.dtype),
        compiler_params=pltpu.CompilerParams(vmem_limit_bytes=8 * MIB),
        cost_estimate=SMALL,
        name="pick",
    )(flag, first, second)


def body(frames, counts, point_ray, channel_pair_weights, tile_bin, image):
    n_scan = lax.axis_size("scan")
    n_chan = lax.axis_size("chan")
    nx = n_chan // 2
    points = counts.shape[0]
    cells, chans = image.shape
    angles = points * n_scan // NIMG
    chan_me = lax.axis_index("chan")
    x_me, core_me = chan_me // 2, chan_me % 2
    first_row = (lax.axis_index("scan") * (cells // NIMG)).astype(jnp.int32).reshape(1)

    middle = [r for r in range(1, n_scan) if r % 2 == 0] + [1]
    late = [r for r in range(3, n_scan, 2)]
    order = [0] + middle + late
    own_rays = point_ray.reshape(points // LANES, LANES)
    rays = {r: own_rays if r == 0 else swap(own_rays, "scan", r, n_scan) for r in order}
    all_rays = jnp.concatenate([rays[r] for r in order], axis=0)

    projected, near_image = project(image, first_row, angles)
    own_share, *shares = reorder(all_rays, projected, n_scan)
    share_of = dict(zip(order[1:], shares))
    relayed = {r ^ 1: swap(share_of[r], "scan", 1, n_scan) for r in late}

    place = []
    for e in range(nx):
        xi = (x_me + e) % nx
        place += [2 * xi + 1 - core_me, 2 * xi + core_me]
    place = jnp.stack(place).astype(jnp.int32)
    send, sums = integrate(
        frames, counts, channel_pair_weights, tile_bin, place, own_share, nx, chans
    )
    keep = select(place, sums, nx, chans)
    even = sorted(relayed)
    merged = merge(sums, [share_of[r] for r in even], [relayed[r] for r in even])
    arrived = [swap(x, "scan", r, n_scan) for r, x in zip(even, merged)]
    arrived.append(swap(share_of[1], "scan", 1, n_scan))
    got = swap(send, "chan", 1, n_chan)
    pattern = keep[0] + got[0].astype(F32)
    for e in range(1, nx):
        joined = (keep[e] + got[e].astype(F32)).astype(BF16)
        pattern = pattern + rotate(joined, "chan", 2 * e, n_chan).astype(F32)

    row_total = row_totals(own_rays, sums, angles)
    scaled, recip = join(row_total, own_share, arrived)
    residual = (-scaled + pattern * (float(NIMG) * recip[:, :1])).astype(BF16)
    half = points // 2
    masks = range(0, n_scan, 4)
    gathered = {0: residual}
    bit = n_scan // 2
    while bit >= 4:
        gathered |= {mask ^ bit: swap(x, "scan", bit, n_scan) for mask, x in gathered.items()}
        bit //= 2
    scan_low = lax.axis_index("scan") % 4
    outer = jnp.logical_or(scan_low == 0, scan_low == 3)
    flag = outer.astype(jnp.int32).reshape(1)
    columns = [rays[mask] for mask in masks]
    pieces = [gathered[mask] for mask in masks if mask]
    last = []
    for mask in masks:
        block = gathered[mask]
        first = lax.ppermute(block, "scan", [(i, onward(i)) for i in range(n_scan)])
        second = [
            lax.ppermute(x, "scan", [(i, backward(i)) for i in range(n_scan)])
            for x in (block[:half], block[half:])
        ]
        pieces += [first] + second
        last += [swap(pick(flag, first, x, k * half), "scan", 1, n_scan) for k, x in enumerate(second)]
        two, one = rays[mask ^ 2], rays[mask ^ 1]
        columns += [jnp.where(outer, two, one), jnp.where(outer, one, two)]
    columns = jnp.concatenate(columns + [rays[mask ^ 3] for mask in masks], axis=0)
    tile, col_recip, partial = prepare(columns, [residual], near_image, first_row, angles)
    partial = add_back(pieces, points, tile, col_recip, partial)
    return back_project(last, points * (n_scan - len(masks)), tile, col_recip, partial)


def solution(mesh):
    in_specs = (
        P(("grp", "scan"), "chan"),
        P(("grp", "scan")),
        P(("grp", "scan")),
        P("chan", None, None),
        P("chan"),
        P(("grp", "scan"), "chan"),
    )
    out_specs = P(("grp", "scan"), "chan")
    return jax.shard_map(body, mesh=mesh, in_specs=in_specs, out_specs=out_specs, check_vma=False)
```
